32 devices in a mesh: stream: 2 (over core), batch: 16 (over z, y, x).
Axes of the slice: x: 2, y: 2, z: 4, core: 2. Of those that a mesh axis runs over, the one named last changes fastest.
Arguments:
- tokens: bfloat16 [2, 16384, 1152], P('stream', 'batch'), may hold values from -6 to 6
- segments: int32 [16384], P('batch'), may hold values from 0 to 63, as said below
- timesteps: int32 [64], P('batch'), may hold values from 0 to 999
- labels: int32 [64], replicated, may hold values from 0 to 999
- head_keep: int32 [64, 16], P('batch'), may hold values 0 or 1
- token_keep: int32 [2, 16384], P('stream', 'batch'), may hold values 0 or 1
- class_table: bfloat16 [1001, 1152], replicated, may hold values from -6 to 6
- w_ada: bfloat16 [1152, 6912], replicated, may hold values from -0.1875 to 0.1875
- b_ada: float32 [6912], replicated, may hold values from -3 to 3
- w_qkv: bfloat16 [1152, 3456], replicated, may hold values from -0.1875 to 0.1875
- b_qv: float32 [2304], replicated, may hold values from -2 to 2
- w_proj: bfloat16 [1152, 1152], replicated, may hold values from -2 to 2
- b_proj: float32 [1152], replicated, may hold values from -3 to 3
- w_fc1: bfloat16 [1152, 4608], replicated, may hold values from -0.1875 to 0.1875
- b_fc1: float32 [4608], replicated, may hold values from -3 to 3
- w_fc2: bfloat16 [4608, 1152], replicated, may hold values from -0.1875 to 0.1875
- b_fc2: float32 [1152], replicated, may hold values from -3 to 3
- out_grad: bfloat16 [2, 16384, 1152], P('stream', 'batch'), may hold values from -6 to 6
Outputs:
- out: bfloat16 [2, 16384, 1152], P('stream', 'batch')
- grad_tokens: float32 [2, 16384, 1152], P('stream', 'batch')
- grad_table: float32 [1001, 1152], replicated
- grad_w_ada: float32 [1152, 6912], P(('stream', 'batch'))
- grad_b_ada: float32 [6912], P(('stream', 'batch'))
- grad_w_qkv: float32 [1152, 3456], P(('stream', 'batch'))
- grad_b_qv: float32 [2304], P(('stream', 'batch'))
- grad_w_proj: float32 [1152, 1152], P(('stream', 'batch'))
- grad_b_proj: float32 [1152], P(('stream', 'batch'))
- grad_w_fc1: float32 [1152, 4608], P(('stream', 'batch'))
- grad_b_fc1: float32 [4608], P(('stream', 'batch'))
- grad_w_fc2: float32 [4608, 1152], P(('stream', 'batch'))
- grad_b_fc2: float32 [1152], P(('stream', 'batch'))
The draws below stay inside these ranges and needn't reach their ends.
Inputs may be any that keep to these rules, and one draw needn't show every extreme that they name: `segments`: the g-th aligned group of 1024 tokens is either one image, all its tokens numbered 4 g, or four images of 256 tokens numbered 4 g, 4 g + 1, 4 g + 2, 4 g + 3 in order. The first group is four images, the second one image, and the last four images. Numbers that no token carries have timesteps, labels and head masks that nothing reads.
All inputs are finite; a program needn't handle non-finite values. No bound on the sum of `head_keep` or of `token_keep` on one device may be relied on, other than what follows from the above.
Results may differ from the reference program's by a relative error of at most 0.015.
The reference program's roundings to bfloat16 on the way count: a program that leaves them out, or rounds other values in their place, can miss the bound.
Values sent between devices are 32-bit elements; how exact they have to be, the bound alone decides.
A program may use at most 448 MiB of HBM per device.

```python
import math
import jax
import jax.numpy as jnp
from jax import lax

D = 1152
HEADS = 16
HEAD_DIM = 72
FF = 4608
CLASSES = 1000
SMALL_LEN = 256
LARGE_LEN = 1024
TOKENS = 16384
ITEMS = 64


def draw_segments(key, part):
    group_total = TOKENS // LARGE_LEN
    small_draw = jax.random.randint(key, (group_total,), 0, 5) == 0
    group_index = jnp.arange(group_total, dtype=jnp.int32)
    small_group = jnp.where(group_index == 0, True, jnp.where(group_index == 1, False, small_draw))
    small_group = jnp.where(group_index == group_total - 1, True, small_group)
    position = jnp.arange(LARGE_LEN, dtype=jnp.int32) // SMALL_LEN
    numbers = 4 * group_index[:, None] + jnp.where(small_group[:, None], position[None, :], 0)
    return numbers.reshape(TOKENS).astype(jnp.int32)


def plant(values, stream_key, smallest, top_value):
    spot = [jax.random.randint(jax.random.fold_in(stream_key, axis), (), 0, length) for axis, length in enumerate(values.shape)]
    main_axis = values.shape.index(max(values.shape))
    next_to = spot[:main_axis] + [(spot[main_axis] + 1) % values.shape[main_axis]] + spot[main_axis + 1:]
    return values.at[tuple(spot)].set(smallest).at[tuple(next_to)].set(top_value)


def block_scale(stream_key, extent, cuts, smallest, high):
    gain, own = 1.0, jax.random.fold_in(stream_key, 6)
    for dim, parts in cuts:
        draws = jnp.exp(jax.random.uniform(jax.random.fold_in(own, dim), (parts,), jnp.float32, smallest / len(cuts), high / len(cuts)))
        gain = gain * jnp.repeat(draws, extent[dim] // parts).reshape([-1 if axis == dim else 1 for axis in range(len(extent))])
    return gain


def noise(rng, extent, scale, reach, cuts=(), kind=jnp.bfloat16):
    values = jax.random.normal(rng, extent, jnp.float32) * scale
    if len(cuts) > 0:
        values = block_scale(rng, extent, cuts, -0.22, 0.18) * values
    return jnp.clip(values, min=-reach, max=reach).astype(kind)


def setup_inputs(seed: int = 0) -> dict:
    key_list = jax.random.split(jax.random.key(seed), 19)
    return {
        "tokens": noise(key_list[0], (2, TOKENS, D), 1.0, 6.0, ((0, 2), (1, 16))),
        "segments": draw_segments(jax.random.fold_in(key_list[18], 71), 0),
        "timesteps": plant(jax.random.randint(key_list[2], (ITEMS,), 0, 1000), jax.random.fold_in(key_list[2], 1), 0, 999).astype(jnp.int32),
        "labels": plant(jax.random.randint(key_list[3], (ITEMS,), 0, CLASSES), jax.random.fold_in(key_list[3], 1), 0, CLASSES - 1).astype(jnp.int32),
        "head_keep": plant((jax.random.randint(key_list[4], (ITEMS, HEADS), 0, 4) < 3).astype(jnp.int32), jax.random.fold_in(key_list[4], 1), 0, 1),
        "token_keep": plant((jax.random.randint(key_list[5], (2, TOKENS), 0, 4) < 3).astype(jnp.int32), jax.random.fold_in(key_list[5], 1), 0, 1),
        "class_table": noise(key_list[6], (CLASSES + 1, D), 1.0, 6.0),
        "w_ada": noise(key_list[7], (D, 6 * D), D ** -0.5, 0.1875),
        "b_ada": noise(key_list[8], (6 * D,), 0.5, 3.0, (), jnp.float32),
        "w_qkv": noise(key_list[9], (D, 3 * D), D ** -0.5, 0.1875),
        "b_qv": noise(key_list[10], (2 * D,), 0.3, 2.0, (), jnp.float32),
        "w_proj": noise(key_list[11], (D, D), (D * 8 // LARGE_LEN) ** -0.5, 2.0),
        "b_proj": noise(key_list[12], (D,), 0.5, 3.0, (), jnp.float32),
        "w_fc1": noise(key_list[13], (D, FF), D ** -0.5, 0.1875),
        "b_fc1": noise(key_list[14], (FF,), 0.5, 3.0, (), jnp.float32),
        "w_fc2": noise(key_list[15], (FF, D), (FF // 4) ** -0.5, 0.1875),
        "b_fc2": noise(key_list[16], (D,), 0.5, 3.0, (), jnp.float32),
        "out_grad": noise(key_list[17], (2, TOKENS, D), 1.0, 6.0, ((0, 2), (1, 16))),
    }


@jax.custom_vjp
def low(v):
    return lax.optimization_barrier(v.astype(jnp.bfloat16)).astype(jnp.float32)

@jax.custom_vjp
def low_back(v):
    return v

def low_keep(v):
    return (low(v), None)

def low_pass(kept, grad):
    return (grad,)

def back_keep(v):
    return (v, None)

def back_low(kept, grad):
    return (low(grad),)
low.defvjp(low_keep, low_pass)
low_back.defvjp(back_keep, back_low)
NORM_EPS = 1e-06
MASKED = -1e+30
HIGHEST = lax.Precision.HIGHEST

def matmul(left, right):
    return jnp.dot(left, right, precision=HIGHEST, preferred_element_type=jnp.float32)

def time_embed(steps_in, width):
    half_width = width // 2
    frequency = jnp.exp(-math.log(10000.0) * jnp.arange(half_width, dtype=jnp.float32) / half_width)
    angles = steps_in.astype(jnp.float32)[:, None] * frequency[None, :]
    return jnp.concatenate([jnp.cos(angles), jnp.sin(angles)], axis=1)

def layer_norm(values):
    centre = values - lax.optimization_barrier(jnp.mean(values, axis=-1, keepdims=True))
    spread = lax.optimization_barrier(jnp.mean(centre * centre, axis=-1, keepdims=True))
    return centre * lax.rsqrt(spread + NORM_EPS)

def attend(projected, item_rows):
    length = projected.shape[0]
    heads_split = projected.reshape(length, 3, HEADS, HEAD_DIM)
    scores = jnp.einsum('qhd,khd->hqk', heads_split[:, 0], heads_split[:, 1], precision=HIGHEST) * (1.0 / math.sqrt(HEAD_DIM))
    scores = low_back(scores)
    same_item = (item_rows[:, None] == item_rows[None, :])[None]
    scores = jnp.where(same_item, scores, MASKED)
    top_score = lax.optimization_barrier(jnp.max(scores, axis=-1, keepdims=True))
    expo = jnp.exp(scores - top_score)
    probs = expo / lax.optimization_barrier(jnp.sum(expo, axis=-1, keepdims=True))
    mixture = jnp.einsum('hqk,khd->qhd', low(probs), heads_split[:, 2], precision=HIGHEST)
    return mixture.reshape(length, D)

def reference(tokens, segments, timesteps, labels, head_keep, token_keep, class_table, w_ada, b_ada, w_qkv, b_qv, w_proj, b_proj, w_fc1, b_fc1, w_fc2, b_fc2, out_grad):
    group_total = 2 * TOKENS // LARGE_LEN
    null_rows = jnp.full((ITEMS,), CLASSES, jnp.int32)
    label_rows = jnp.concatenate([labels, null_rows])
    item_index = jnp.concatenate([segments, segments + ITEMS]).reshape(group_total, LARGE_LEN)
    keep_index = token_keep.astype(jnp.float32).reshape(group_total, LARGE_LEN)
    head_rows = jnp.repeat(jnp.concatenate([head_keep, head_keep]).astype(jnp.float32), HEAD_DIM, axis=1)
    time_rows = time_embed(jnp.concatenate([timesteps, timesteps]), D)

    def forward(tokens_f, table_f, w_ada_f, b_ada_f, w_qkv_f, b_qv_f, w_proj_f, b_proj_f, w_fc1_f, b_fc1_f, w_fc2_f, b_fc2_f):
        cond = time_rows + table_f[label_rows]
        modulation = low_back(matmul(low(jax.nn.silu(cond)), w_ada_f) + b_ada_f)
        bias_full = jnp.concatenate([b_qv_f[:D], jnp.zeros((D,), jnp.float32), b_qv_f[D:]])

        def group_pass(pieces):
            token_rows, item_rows, keep_rows = pieces
            mod_rows = modulation[item_rows]
            shift_one, scale_one, gate_one, shift_two, scale_two, gate_two = jnp.split(mod_rows, 6, axis=1)
            normed_one = low(layer_norm(token_rows) * (1.0 + scale_one) + shift_one)
            projected = low(low_back(matmul(normed_one, w_qkv_f) + bias_full))
            attended = low(low_back(attend(projected, item_rows) * head_rows[item_rows]))
            branch_one = low_back(matmul(attended, w_proj_f) + b_proj_f)
            middle = token_rows + gate_one * branch_one
            normed_two = low(layer_norm(middle) * (1.0 + scale_two) + shift_two)
            hidden_pre = low_back(matmul(normed_two, w_fc1_f) + b_fc1_f)
            hidden = low(jax.nn.gelu(hidden_pre, approximate=True))
            branch_two = low_back(matmul(hidden, w_fc2_f) + b_fc2_f)
            return middle + gate_two * keep_rows[:, None] * branch_two
        grouped = tokens_f.reshape(group_total, LARGE_LEN, D)
        result = lax.map(jax.checkpoint(group_pass), (grouped, item_index, keep_index))
        return result.reshape(2, TOKENS, D)
    floats = tuple((source.astype(jnp.float32) for source in (tokens, class_table, w_ada, b_ada, w_qkv, b_qv, w_proj, b_proj, w_fc1, b_fc1, w_fc2, b_fc2)))
    output, pullback = jax.vjp(forward, *floats)
    grads = pullback(out_grad.astype(jnp.float32))
    return (output.astype(jnp.bfloat16), grads[0], grads[1], grads[2], grads[3], grads[4], grads[5], grads[6], grads[7], grads[8], grads[9], grads[10], grads[11])
```

```python
import functools
import math

import jax
import jax.numpy as jnp
from jax import lax
from jax.experimental import pallas as pl
from jax.experimental.pallas import tpu as pltpu
from jax.sharding import PartitionSpec as P

F32 = jnp.float32
BF16 = jnp.bfloat16
HIGHEST = lax.Precision.HIGHEST
NORM_EPS = 1e-06
ROW = 256
GROUP = 1024
NN = (((1,), (0,)), ((), ()))
NT = (((1,), (1,)), ((), ()))
TN = (((0,), (0,)), ((), ()))
TT = (((0,), (1,)), ((), ()))
VMEM_LIMIT = 60 << 20


def dot(left, right, dims=NN, precision=None):
    return lax.dot_general(left, right, dims, precision=precision, preferred_element_type=F32)


def call(body, name, flops, moved, **kwargs):
    return pl.pallas_call(
        body,
        name=name,
        compiler_params=pltpu.CompilerParams(vmem_limit_bytes=VMEM_LIMIT),
        cost_estimate=pl.CostEstimate(flops=flops, bytes_accessed=moved, transcendentals=0),
        **kwargs,
    )


def shaped(shape, kind):
    return jax.ShapeDtypeStruct(shape, kind)


def normed(values):
    centre = values - jnp.mean(values, axis=-1, keepdims=True)
    spread = jnp.mean(centre * centre, axis=-1, keepdims=True)
    inverse = lax.rsqrt(spread + NORM_EPS)
    return centre * inverse, inverse


def normed_back(grad, normal, inverse):
    first = jnp.mean(grad, axis=-1, keepdims=True)
    second = jnp.mean(grad * normal, axis=-1, keepdims=True)
    return inverse * (grad - first - normal * second)


def qkv_body(x_ref, mod_ref, w_ref, b_ref, h_ref, out_ref):
    @pl.when(pl.program_id(0) == 0)
    def _():
        for tile in range(x_ref.shape[0] // ROW):
            rows = slice(tile * ROW, tile * ROW + ROW)
            normal, _ = normed(x_ref[rows].astype(F32))
            h_ref[rows] = (normal * (1.0 + mod_ref[tile, 1:2]) + mod_ref[tile, 0:1]).astype(BF16)

    out_ref[...] = (dot(h_ref[...], w_ref[...]) + b_ref[...]).astype(BF16)


def qkv_call(x, mod, w, bias):
    tokens, width = x.shape
    wide = w.shape[1]
    block = 384
    return call(
        qkv_body,
        "qkv",
        2 * tokens * width * wide,
        2 * (2 * tokens * width + width * wide + tokens * wide),
        grid=(wide // block,),
        in_specs=[
            pl.BlockSpec((tokens, width), lambda j: (0, 0)),
            pl.BlockSpec(mod.shape, lambda j: (0, 0, 0)),
            pl.BlockSpec((width, block), lambda j: (0, j)),
            pl.BlockSpec((1, block), lambda j: (0, j)),
        ],
        out_specs=[
            pl.BlockSpec((tokens, width), lambda j: (0, 0)),
            pl.BlockSpec((tokens, block), lambda j: (0, j)),
        ],
        out_shape=[shaped((tokens, width), BF16), shaped((tokens, wide), BF16)],
    )(x, mod, w, bias)


def pair_select(offset, head_width):
    row = lax.broadcasted_iota(jnp.int32, (256, 256), 0)
    col = lax.broadcasted_iota(jnp.int32, (256, 256), 1)
    lane = col & 127
    base = offset + jnp.where(col >= 128, head_width, 0)
    return jnp.where((lane < head_width) & (row == base + lane), 1.0, 0.0).astype(BF16)


def attention_body(flag_ref, qkv_ref, keep_ref, p_ref, ot_ref, om_ref, *, width, head_width):
    pair = pl.program_id(1)
    column = pair * (2 * head_width)
    start = pl.multiple_of(column // 128 * 128, 128)
    select = pair_select(column - start, head_width)
    scale = math.log2(math.e) / math.sqrt(head_width)
    tokens = qkv_ref.shape[0]

    @pl.when(pair == 0)
    def _():
        om_ref[...] = jnp.zeros_like(om_ref)

    q = dot(qkv_ref[:, pl.ds(start, 256)], select).astype(BF16)
    k = dot(qkv_ref[:, pl.ds(width + start, 256)], select).astype(BF16)
    v = dot(qkv_ref[:, pl.ds(2 * width + start, 256)], select)
    lane = lax.broadcasted_iota(jnp.int32, v.shape, 1) & 127
    v = jnp.where(lane == head_width, 1.0, v).astype(BF16)

    def part(head, first, count):
        rows = slice(first, first + count)
        lanes = slice(128 * head, 128 * head + 128)
        scores = dot(k[rows, lanes], q[rows, lanes], NT)
        top = jnp.max(scores, axis=0, keepdims=True)
        expo = jnp.exp2((scores - top) * scale)
        total = jnp.sum(expo, axis=0, keepdims=True)
        probs = (expo * (1.0 / total)).astype(BF16)
        p_ref[head, rows, rows] = probs
        mixed = dot(v[rows, lanes], probs, TN)
        ot_ref[head, :, rows] = mixed[:head_width] * (1.0 / mixed[head_width : head_width + 1])
        return (mixed * keep_ref[head, :, rows]).astype(BF16)

    def finish(parts):
        mixed = jnp.concatenate([jnp.concatenate(row, axis=1) for row in parts], axis=0)
        new = dot(mixed, select, TT)
        om_ref[:, pl.ds(start, 256)] = (om_ref[:, pl.ds(start, 256)].astype(F32) + new).astype(BF16)

    whole = flag_ref[pl.program_id(0)] == 1

    @pl.when(whole)
    def _():
        finish([[part(head, 0, tokens)] for head in range(2)])

    @pl.when(jnp.logical_not(whole))
    def _():
        finish([[part(head, at, ROW) for at in range(0, tokens, ROW)] for head in range(2)])


def attention_call(flag, qkv, keep, heads):
    tokens, wide = qkv.shape
    width = wide // 3
    head_width = width // heads
    groups = tokens // GROUP
    return call(
        functools.partial(attention_body, width=width, head_width=head_width),
        "attention",
        2 * 2 * heads * tokens * GROUP * 256,
        2 * tokens * wide + 2 * heads * tokens * GROUP + 6 * tokens * width,
        grid=(groups, heads // 2),
        in_specs=[
            pl.BlockSpec(memory_space=pltpu.SMEM),
            pl.BlockSpec((GROUP, wide), lambda g, h: (g, 0)),
            pl.BlockSpec((2, 1, GROUP), lambda g, h: (h, 0, g)),
        ],
        out_specs=[
            pl.BlockSpec((2, GROUP, GROUP), lambda g, h: (h, 0, g)),
            pl.BlockSpec((2, head_width, GROUP), lambda g, h: (h, 0, g)),
            pl.BlockSpec((GROUP, width), lambda g, h: (g, 0)),
        ],
        out_shape=[
            shaped((heads, GROUP, tokens), BF16),
            shaped((heads, head_width, tokens), F32),
            shaped((tokens, width), BF16),
        ],
    )(flag, qkv, keep)


def attention_back_body(
    flag_ref, qkv_ref, do_ref, p_ref, ot_ref, out_ref, ds_ref, *, width, head_width
):
    pair = pl.program_id(1)
    column = pair * (2 * head_width)
    start = pl.multiple_of(column // 128 * 128, 128)
    select = pair_select(column - start, head_width)
    scale = 1.0 / math.sqrt(head_width)
    tokens = qkv_ref.shape[0]

    @pl.when(pair == 0)
    def _():
        out_ref[...] = jnp.zeros_like(out_ref)

    q = dot(qkv_ref[:, pl.ds(start, 256)], select).astype(BF16)
    k = dot(qkv_ref[:, pl.ds(width + start, 256)], select).astype(BF16)
    v = dot(qkv_ref[:, pl.ds(2 * width + start, 256)], select).astype(BF16)
    window = do_ref[:, pl.ds(start, 256)]
    do = dot(window, select).astype(BF16)
    do_t = dot(select, window, TT)
    delta = [
        jnp.sum(do_t[128 * head : 128 * head + head_width] * ot_ref[head], axis=0, keepdims=True)
        for head in range(2)
    ]

    def grad_scores(head, first, count):
        rows = slice(first, first + count)
        lanes = slice(128 * head, 128 * head + 128)
        dp = dot(v[rows, lanes], do[rows, lanes], NT)
        probs = p_ref[head, rows, rows].astype(F32)
        return (probs * (dp - delta[head][:, rows])).astype(BF16)

    def add(base, value, dims):
        new = dot(value, select, dims)
        spot = pl.ds(base + start, 256)
        out_ref[:, spot] = (out_ref[:, spot].astype(F32) + new).astype(BF16)

    def run(count):
        dq, dk, dv = [], [], []
        for head in range(2):
            lanes = slice(128 * head, 128 * head + 128)
            dq_row, dk_col, dv_col = [], [], []
            for first in range(0, tokens, count):
                rows = slice(first, first + count)
                ds = grad_scores(head, first, count)
                if count == tokens:
                    ds_ref[head] = ds
                    ds = ds_ref[head]
                dq_row.append((dot(k[rows, lanes], ds, TN) * scale).astype(BF16))
                dk_col.append((dot(ds, q[rows, lanes]) * scale).astype(BF16))
                dv_col.append(dot(p_ref[head, rows, rows], do[rows, lanes]).astype(BF16))
            dq.append(jnp.concatenate(dq_row, axis=1))
            dk.append(jnp.concatenate(dk_col, axis=0))
            dv.append(jnp.concatenate(dv_col, axis=0))
        add(0, jnp.concatenate(dq, axis=0), TT)
        add(width, jnp.concatenate(dk, axis=1), NT)
        add(2 * width, jnp.concatenate(dv, axis=1), NT)

    whole = flag_ref[pl.program_id(0)] == 1

    @pl.when(whole)
    def _():
        run(tokens)

    @pl.when(jnp.logical_not(whole))
    def _():
        run(ROW)


def attention_back_call(flag, qkv, do, probs, mixed):
    tokens, wide = qkv.shape
    width = wide // 3
    heads, head_width = mixed.shape[:2]
    groups = tokens // GROUP
    return call(
        functools.partial(attention_back_body, width=width, head_width=head_width),
        "attention_back",
        4 * 2 * heads * tokens * GROUP * 256,
        4 * tokens * wide + 2 * heads * tokens * GROUP + 6 * tokens * width,
        grid=(groups, heads // 2),
        in_specs=[
            pl.BlockSpec(memory_space=pltpu.SMEM),
            pl.BlockSpec((GROUP, wide), lambda g, h: (g, 0)),
            pl.BlockSpec((GROUP, width), lambda g, h: (g, 0)),
            pl.BlockSpec((2, GROUP, GROUP), lambda g, h: (h, 0, g)),
            pl.BlockSpec((2, head_width, GROUP), lambda g, h: (h, 0, g)),
        ],
        out_specs=pl.BlockSpec((GROUP, wide), lambda g, h: (g, 0)),
        out_shape=shaped((tokens, wide), BF16),
        scratch_shapes=[pltpu.VMEM((2, GROUP, GROUP), BF16)],
    )(flag, qkv, do, probs, mixed)


def middle_body(
    om_ref, w_ref, b_ref, x_ref, mod_ref, top_ref, keep_ref, perm_ref,
    a_ref, x1_ref, h_ref, hp_ref, dm_ref, sum_ref,
):
    tile = pl.program_id(0)
    branch = dot(om_ref[...], w_ref[...]) + b_ref[...]
    a_ref[...] = branch
    middle = x_ref[...].astype(F32) + mod_ref[tile, 2:3] * branch
    x1_ref[...] = middle
    normal, _ = normed(middle)
    hidden = (normal * (1.0 + mod_ref[tile, 4:5]) + mod_ref[tile, 3:4]).astype(BF16)
    h_ref[...] = hidden
    hp_ref[...] = dot(hidden, perm_ref[...]).astype(BF16)
    grad = (top_ref[...].astype(F32) * mod_ref[tile, 5:6] * keep_ref[...]).astype(BF16)
    dm_ref[...] = grad
    sum_ref[0] = jnp.sum(grad.astype(F32), axis=0, keepdims=True)


def middle_call(om, w, bias, x, mod, top, keep, perm):
    tokens, width = x.shape
    tiles = tokens // ROW
    rows = pl.BlockSpec((ROW, width), lambda i: (i, 0))
    fixed = pl.BlockSpec((width, width), lambda i: (0, 0))
    return call(
        middle_body,
        "middle",
        4 * tokens * width * width,
        26 * tokens * width,
        grid=(tiles,),
        in_specs=[
            rows,
            fixed,
            pl.BlockSpec((1, width), lambda i: (0, 0)),
            rows,
            pl.BlockSpec(mod.shape, lambda i: (0, 0, 0)),
            rows,
            pl.BlockSpec((ROW, 1), lambda i: (i, 0)),
            fixed,
        ],
        out_specs=[rows, rows, rows, rows, rows, pl.BlockSpec((1, 1, width), lambda i: (i, 0, 0))],
        out_shape=[
            shaped((tokens, width), F32),
            shaped((tokens, width), F32),
            shaped((tokens, width), BF16),
            shaped((tokens, width), BF16),
            shaped((tokens, width), BF16),
            shaped((tiles, 1, width), F32),
        ],
    )(om, w, bias, x, mod, top, keep, perm)


def hidden_body(h_ref, hp_ref, dm_ref, w1_ref, b1_ref, w2_ref, g_ref, df_ref, sum_ref, send_ref, keep_ref):
    first, second = math.sqrt(2.0 / math.pi), 0.044715
    pre = dot(h_ref[...], w1_ref[...]) + b1_ref[...]
    square = pre * pre
    tanh = jnp.tanh(first * pre * (1.0 + second * square))
    half = 0.5 * (1.0 + tanh)
    g_ref[...] = (pre * half).astype(BF16)
    slope = half + (0.5 * first) * pre * (1.0 - tanh * tanh) * (1.0 + (3.0 * second) * square)
    grad = (dot(dm_ref[...], w2_ref[...], NT) * slope).astype(BF16)
    df_ref[...] = grad
    sum_ref[...] = jnp.sum(grad.astype(F32), axis=0, keepdims=True)
    half_rows = send_ref.shape[0]
    send_ref[...] = dot(hp_ref[:, half_rows:], grad, TN)
    keep_ref[...] = dot(hp_ref[:, :half_rows], grad, TN)


def hidden_call(h, hp, dm, w1, b1, w2, first, count):
    tokens, width = h.shape
    block = 384
    base = first // block
    full = pl.BlockSpec((tokens, width), lambda j: (0, 0))
    half = width // 2
    return call(
        hidden_body,
        "hidden",
        6 * tokens * width * count,
        6 * tokens * width + 4 * tokens * count + 8 * width * count,
        grid=(count // block,),
        in_specs=[
            full,
            full,
            full,
            pl.BlockSpec((width, block), lambda j: (0, base + j)),
            pl.BlockSpec((1, block), lambda j: (0, base + j)),
            pl.BlockSpec((block, width), lambda j: (base + j, 0)),
        ],
        out_specs=[
            pl.BlockSpec((tokens, block), lambda j: (0, j)),
            pl.BlockSpec((tokens, block), lambda j: (0, j)),
            pl.BlockSpec((1, block), lambda j: (0, j)),
            pl.BlockSpec((half, block), lambda j: (0, j)),
            pl.BlockSpec((half, block), lambda j: (0, j)),
        ],
        out_shape=[
            shaped((tokens, count), BF16),
            shaped((tokens, count), BF16),
            shaped((1, count), F32),
            shaped((half, count), F32),
            shaped((half, count), F32),
        ],
    )(h, hp, dm, w1, b1, w2)


def rows_grad_body(side_ref, spot_ref, *refs, pieces):
    g_refs, dm_ref, out_ref = refs[:pieces], refs[pieces], refs[pieces + 1]
    shard = out_ref.shape[1]
    grad = dm_ref[...]
    place = 0
    for g_ref in g_refs:
        made = dot(g_ref[...], grad, TN)
        for at in range(0, made.shape[0], shard):
            out_ref[spot_ref[place]] = made[at : at + shard]
            place += 1


def rows_grad_call(side, spots, g, dm, first, count, shards):
    tokens, hidden = g.shape
    half = hidden // 2
    block = 128
    pieces = 2
    base = first // block
    specs = [
        pl.BlockSpec((tokens, half // pieces), functools.partial(lambda j, side, spots, n: (0, side[0] * pieces + n), n=n))
        for n in range(pieces)
    ]
    return call(
        functools.partial(rows_grad_body, pieces=pieces),
        "rows_grad",
        2 * tokens * half * count,
        2 * tokens * half + 2 * tokens * count + 4 * half * count,
        grid_spec=pltpu.PrefetchScalarGridSpec(
            num_scalar_prefetch=2,
            grid=(count // block,),
            in_specs=specs + [pl.BlockSpec((tokens, block), lambda j, side, spots: (0, base + j))],
            out_specs=pl.BlockSpec((shards, half // shards, block), lambda j, side, spots: (0, 0, j)),
        ),
        out_shape=shaped((shards, half // shards, count), F32),
    )(side, spots, *([g] * pieces), dm)


def result_body(g_ref, w_ref, b_ref, x1_ref, mod_ref, top_ref, keep_ref, out_ref, sum_ref):
    tile = pl.program_id(0)
    branch = dot(g_ref[...], w_ref[...]) + b_ref[...]
    out_ref[...] = (x1_ref[...] + mod_ref[tile, 5:6] * keep_ref[...] * branch).astype(BF16)
    sum_ref[0] = jnp.sum(top_ref[...].astype(F32) * keep_ref[...] * branch, axis=0, keepdims=True)


def result_call(g, w, bias, x1, mod, top, keep):
    tokens, width = x1.shape
    hidden = g.shape[1]
    tiles = tokens // ROW
    rows = pl.BlockSpec((ROW, width), lambda i: (i, 0))
    return call(
        result_body,
        "result",
        2 * tokens * width * hidden,
        2 * tokens * hidden + 2 * hidden * width + 8 * tokens * width,
        grid=(tiles,),
        in_specs=[
            pl.BlockSpec((ROW, hidden), lambda i: (i, 0)),
            pl.BlockSpec((hidden, width), lambda i: (0, 0)),
            pl.BlockSpec((1, width), lambda i: (0, 0)),
            rows,
            pl.BlockSpec(mod.shape, lambda i: (0, 0, 0)),
            rows,
            pl.BlockSpec((ROW, 1), lambda i: (i, 0)),
        ],
        out_specs=[rows, pl.BlockSpec((1, 1, width), lambda i: (i, 0, 0))],
        out_shape=[shaped((tokens, width), BF16), shaped((tiles, 1, width), F32)],
    )(g, w, bias, x1, mod, top, keep)


def middle_back_body(
    df_ref, w1_ref, x1_ref, mod_ref, top_ref, a_ref, wp_ref, head_ref,
    dx_ref, da_ref, do_ref, sum_ref,
):
    tile = pl.program_id(0)
    grad = dot(df_ref[...], w1_ref[...], NT)
    normal, inverse = normed(x1_ref[...])
    back = normed_back(grad * (1.0 + mod_ref[tile, 4:5]), normal, inverse)
    dx = top_ref[...].astype(F32) + back
    dx_ref[...] = dx
    da = (dx * mod_ref[tile, 2:3]).astype(BF16)
    da_ref[...] = da
    do_ref[...] = (dot(da, wp_ref[...], NT) * head_ref[tile]).astype(BF16)
    sum_ref[0, 0:1] = jnp.sum(dx * a_ref[...], axis=0, keepdims=True)
    sum_ref[0, 1:2] = jnp.sum(grad, axis=0, keepdims=True)
    sum_ref[0, 2:3] = jnp.sum(grad * normal, axis=0, keepdims=True)
    sum_ref[0, 3:4] = jnp.sum(da.astype(F32), axis=0, keepdims=True)


def middle_back_call(df, w1, x1, mod, top, a, wp, head_rows):
    tokens, width = x1.shape
    hidden = df.shape[1]
    tiles = tokens // ROW
    rows = pl.BlockSpec((ROW, width), lambda i: (i, 0))
    return call(
        middle_back_body,
        "middle_back",
        2 * tokens * width * (hidden + width),
        2 * tokens * hidden + 2 * hidden * width + 18 * tokens * width,
        grid=(tiles,),
        in_specs=[
            pl.BlockSpec((ROW, hidden), lambda i: (i, 0)),
            pl.BlockSpec((width, hidden), lambda i: (0, 0)),
            rows,
            pl.BlockSpec(mod.shape, lambda i: (0, 0, 0)),
            rows,
            rows,
            pl.BlockSpec((width, width), lambda i: (0, 0)),
            pl.BlockSpec(head_rows.shape, lambda i: (0, 0, 0)),
        ],
        out_specs=[rows, rows, rows, pl.BlockSpec((1, 4, width), lambda i: (i, 0, 0))],
        out_shape=[
            shaped((tokens, width), F32),
            shaped((tokens, width), BF16),
            shaped((tokens, width), BF16),
            shaped((tiles, 4, width), F32),
        ],
    )(df, w1, x1, mod, top, a, wp, head_rows)


def columns_grad_body(left_ref, perm_ref, right_ref, send_ref, keep_ref, sum_ref, moved_ref):
    @pl.when(pl.program_id(0) == 0)
    def _():
        moved_ref[...] = dot(left_ref[...], perm_ref[...]).astype(BF16)

    half = send_ref.shape[0]
    grad = right_ref[...]
    send_ref[...] = dot(moved_ref[:, half:], grad, TN)
    keep_ref[...] = dot(moved_ref[:, :half], grad, TN)
    sum_ref[...] = jnp.sum(grad.astype(F32), axis=0, keepdims=True)


def columns_grad_call(left, perm, right, name):
    tokens, width = left.shape
    wide = right.shape[1]
    half = width // 2
    block = 384
    out = pl.BlockSpec((half, block), lambda j: (0, j))
    return call(
        columns_grad_body,
        name,
        2 * tokens * width * (wide + width),
        2 * tokens * (wide + width) + 2 * width * width + 4 * width * wide,
        grid=(wide // block,),
        in_specs=[
            pl.BlockSpec((tokens, width), lambda j: (0, 0)),
            pl.BlockSpec((width, width), lambda j: (0, 0)),
            pl.BlockSpec((tokens, block), lambda j: (0, j)),
        ],
        out_specs=[out, out, pl.BlockSpec((1, block), lambda j: (0, j))],
        out_shape=[shaped((half, wide), F32), shaped((half, wide), F32), shaped((1, wide), F32)],
        scratch_shapes=[pltpu.VMEM((tokens, width), BF16)],
    )(left, perm, right)


def first_back_body(dqkv_ref, w_ref, x_ref, mod_ref, dx_ref, out_ref, sum_ref):
    tile = pl.program_id(0)
    grad = dot(dqkv_ref[...], w_ref[...], NT)
    normal, inverse = normed(x_ref[...].astype(F32))
    out_ref[...] = dx_ref[...] + normed_back(grad * (1.0 + mod_ref[tile, 1:2]), normal, inverse)
    sum_ref[0, 0:1] = jnp.sum(grad, axis=0, keepdims=True)
    sum_ref[0, 1:2] = jnp.sum(grad * normal, axis=0, keepdims=True)


def first_back_call(dqkv, w, x, mod, dx):
    tokens, wide = dqkv.shape
    width = x.shape[1]
    tiles = tokens // ROW
    rows = pl.BlockSpec((ROW, width), lambda i: (i, 0))
    return call(
        first_back_body,
        "first_back",
        2 * tokens * width * wide,
        2 * tokens * wide + 2 * width * wide + 10 * tokens * width,
        grid=(tiles,),
        in_specs=[
            pl.BlockSpec((ROW, wide), lambda i: (i, 0)),
            pl.BlockSpec((width, wide), lambda i: (0, 0)),
            rows,
            pl.BlockSpec(mod.shape, lambda i: (0, 0, 0)),
            rows,
        ],
        out_specs=[rows, pl.BlockSpec((1, 2, width), lambda i: (i, 0, 0))],
        out_shape=[shaped((tokens, width), F32), shaped((tiles, 2, width), F32)],
    )(dqkv, w, x, mod, dx)


def bit_order(lead, bits):
    return [lead] + [bit for bit in range(bits) if bit != lead]


def part_orders(bits):
    if bits < 3:
        return [list(range(bits))]
    return [bit_order(lead, bits) for lead in range(3)]


def scatter_sum(send, keep, bits, orders=None):
    received = lax.ppermute(send, "stream", [(0, 1), (1, 0)])
    rows, wide = keep.shape
    orders = orders or part_orders(bits)
    share = wide // len(orders)
    results = []
    for number, order in enumerate(orders):
        columns = slice(number * share, number * share + share)
        terms = [keep[:, columns], received[:, columns]]
        left = list(range(bits))
        count = rows
        for bit in order:
            before = 1 << left.index(bit)
            after = count // (2 * before)

            def pick(term, which):
                return term.reshape(before, 2, after, share)[:, which].reshape(count // 2, share)

            sent = functools.reduce(lambda x, y: x + y, [pick(term, 1) for term in terms])
            pairs = [(i, i ^ (1 << bit)) for i in range(1 << bits)]
            terms = [pick(term, 0) for term in terms] + [lax.ppermute(sent, "batch", pairs)]
            left.remove(bit)
            count //= 2
        results.append(functools.reduce(lambda x, y: x + y, terms))
    return results


def device_offsets(bits):
    places = jnp.arange(1 << bits, dtype=jnp.int32)
    offset = jnp.zeros_like(places)
    for bit in range(bits):
        offset = offset | (((places >> (bits - 1 - bit)) & 1) << bit)
    return offset


def time_embed(steps_in, width):
    half_width = width // 2
    frequency = jnp.exp(-math.log(10000.0) * jnp.arange(half_width, dtype=F32) / half_width)
    angles = steps_in.astype(F32)[:, None] * frequency[None, :]
    return jnp.concatenate([jnp.cos(angles), jnp.sin(angles)], axis=1)


def per_device(
    tokens, segments, timesteps, labels, head_keep, token_keep, class_table, w_ada, b_ada,
    w_qkv, b_qv, w_proj, b_proj, w_fc1, b_fc1, w_fc2, b_fc2, out_grad, *, batch,
):
    x, top = tokens[0], out_grad[0]
    count, width = x.shape
    hidden = w_fc1.shape[1]
    heads = head_keep.shape[1]
    head_width = width // heads
    items = timesteps.shape[0]
    tiles = count // ROW
    groups = count // GROUP
    null_class = class_table.shape[0] - 1
    bits = batch.bit_length() - 1
    devices = 2 * batch
    stream = lax.axis_index("stream")
    index = lax.axis_index("batch")

    own_labels = lax.dynamic_slice_in_dim(labels, index * items, items)
    used = jnp.where(stream == 0, own_labels, null_class)
    cond = time_embed(timesteps, width) + jnp.take(class_table, used, axis=0).astype(F32)
    act = jax.nn.silu(cond).astype(BF16)
    modulation = dot(act, w_ada) + b_ada
    tile_item = segments[::ROW] - index * items
    chosen = tile_item[:, None] == jnp.arange(items, dtype=jnp.int32)[None, :]
    mod = jnp.sum(jnp.where(chosen[:, :, None], modulation[None], 0.0), axis=1)
    mod = mod.reshape(tiles, 6, width)
    tile_heads = jnp.sum(jnp.where(chosen[:, :, None], head_keep[None], 0), axis=1).astype(F32)
    head_rows = jnp.repeat(tile_heads, head_width, axis=1).reshape(tiles, 1, width)
    head_columns = jnp.repeat(tile_heads.T, ROW, axis=1).reshape(heads, 1, count)
    keep = token_keep[0].astype(F32)[:, None]
    grouped = segments.reshape(groups, GROUP)
    flag = (grouped[:, 0] == grouped[:, -1]).astype(jnp.int32)

    offset = device_offsets(bits)
    own_order = jnp.concatenate([stream * batch + (index ^ offset), (1 - stream) * batch + (index ^ offset)])
    shard = width // devices
    source = (own_order[:, None] * shard + jnp.arange(shard, dtype=jnp.int32)[None, :]).reshape(width)
    perm = (jnp.arange(width, dtype=jnp.int32)[:, None] == source[None, :]).astype(BF16)
    inverse = device_offsets(bits)
    spots = inverse[jnp.arange(batch, dtype=jnp.int32) ^ index]

    bias_full = jnp.concatenate([b_qv[:width], jnp.zeros((width,), F32), b_qv[width:]])[None]
    h1, qkv = qkv_call(x, mod, w_qkv, bias_full)
    probs, mixed, om = attention_call(flag, qkv, head_columns, heads)
    a, x1, h2, h2p, dm, sum_dm = middle_call(om, w_proj, b_proj[None], x, mod, top, keep, perm)

    cuts = [0, hidden // 4, hidden // 2, hidden]
    pieces, fc1 = [], []
    for low, high in zip(cuts[:-1], cuts[1:]):
        got = hidden_call(h2, h2p, dm, w_fc1, b_fc1[None], w_fc2, low, high - low)
        pieces.append(got[:3])
        fc1 += scatter_sum(got[3], got[4], bits)
    g = jnp.concatenate([piece[0] for piece in pieces], axis=1)
    df = jnp.concatenate([piece[1] for piece in pieces], axis=1)
    sum_df = jnp.concatenate([piece[2] for piece in pieces], axis=1)[0]
    fc2 = []
    for low, high in ((0, width // 3), (width // 3, width)):
        halves = [
            rows_grad_call(side[None], spots, g, dm, low, high - low, batch).reshape(hidden // 2, high - low)
            for side in (1 - stream, stream)
        ]
        fc2 += scatter_sum(halves[0], halves[1], bits)
    result, sum_gate = result_call(g, w_fc2, b_fc2[None], x1, mod, top, keep)
    dx1, da, do, sums_two = middle_back_call(df, w_fc1, x1, mod, top, a, w_proj, head_rows)
    send, kept, _ = columns_grad_call(om, perm, da, "proj_grad")
    proj = scatter_sum(send, kept, bits)

    dqkv = attention_back_call(flag, qkv, do, probs, mixed)
    send, kept, sum_dqkv = columns_grad_call(h1, perm, dqkv, "qkv_grad")
    wide = scatter_sum(send, kept, bits)
    grad_tokens, sums_one = first_back_call(dqkv, w_qkv, x, mod, dx1)

    biases = jnp.concatenate(
        [
            part.reshape(devices, -1)
            for part in (
                sum_df,
                jnp.sum(sum_dm, axis=(0, 1)),
                jnp.sum(sums_two[:, 3], axis=0),
                jnp.concatenate([sum_dqkv[0, :width], sum_dqkv[0, 2 * width :]]),
            )
        ],
        axis=1,
    )
    biases = biases[own_order]
    bias = scatter_sum(biases[batch:], biases[:batch], bits, [list(range(bits))])[0][0]
    ends = [hidden // devices, width // devices, width // devices, 2 * width // devices]
    at = [sum(ends[:n]) for n in range(5)]
    grad_b_fc1, grad_b_fc2, grad_b_proj, grad_b_qv = [bias[at[n] : at[n + 1]] for n in range(4)]

    by_tile = jnp.stack(
        [sums_one[:, 0], sums_one[:, 1], sums_two[:, 0], sums_two[:, 1], sums_two[:, 2], sum_gate[:, 0]],
        axis=1,
    ).reshape(tiles, 6 * width)
    grad_mod = jnp.sum(jnp.where(chosen[:, :, None], by_tile[:, None], 0.0), axis=0)
    grad_mod = grad_mod.astype(BF16).astype(F32)
    gathered = lax.all_gather(
        jnp.concatenate([grad_mod, cond], axis=1), ("stream", "batch"), axis=0, tiled=True
    )
    all_mod = gathered[:, : 6 * width]
    all_cond = gathered[:, 6 * width :]
    all_mod16 = all_mod.astype(BF16)
    me = stream * batch + index
    all_act = jax.nn.silu(all_cond).astype(BF16)
    own_act = lax.dynamic_slice_in_dim(all_act, me * shard, shard, axis=1)
    grad_w_ada = dot(own_act, all_mod16, TN)
    share = 6 * width // devices
    grad_b_ada = jnp.sum(lax.dynamic_slice_in_dim(all_mod, me * share, share, axis=1), axis=0)
    grad_act = dot(all_mod16, w_ada, NT)
    grad_cond = jax.vjp(jax.nn.silu, all_cond)[1](grad_act)[0]
    all_labels = jnp.concatenate([labels, jnp.full_like(labels, null_class)])
    class_index = jnp.arange(null_class + 1, dtype=jnp.int32)
    label_select = (all_labels[:, None] == class_index[None, :]).astype(F32)
    grad_table = dot(label_select, grad_cond, TN, HIGHEST)

    return (
        result[None],
        grad_tokens[None],
        grad_table,
        grad_w_ada,
        grad_b_ada,
        jnp.concatenate(wide, axis=1),
        grad_b_qv,
        jnp.concatenate(proj, axis=1),
        grad_b_proj,
        jnp.concatenate(fc1, axis=1),
        grad_b_fc1,
        jnp.concatenate(fc2, axis=1),
        grad_b_fc2,
    )


def solution(mesh):
    both = ("stream", "batch")
    return jax.shard_map(
        functools.partial(per_device, batch=mesh.shape["batch"]),
        mesh=mesh,
        in_specs=(
            P("stream", "batch", None),
            P("batch"),
            P("batch"),
            P(),
            P("batch", None),
            P("stream", "batch"),
            P(), P(), P(), P(), P(), P(), P(), P(), P(), P(), P(),
            P("stream", "batch", None),
        ),
        out_specs=(
            P("stream", "batch", None),
            P("stream", "batch", None),
            P(),
            P(both, None),
            P(both),
            P(both, None),
            P(both),
            P(both, None),
            P(both),
            P(both, None),
            P(both),
            P(both, None),
            P(both),
        ),
        check_vma=False,
    )
```

```python
import functools
import math

import jax
import jax.numpy as jnp
from jax import lax
from jax.experimental import pallas as pl
from jax.experimental.pallas import tpu as pltpu
from jax.sharding import PartitionSpec as P

F32 = jnp.float32
BF16 = jnp.bfloat16
HIGHEST = lax.Precision.HIGHEST
NORM_EPS = 1e-06
ROW_PARTS = ((2, 0), (1, 2))
ROW = 256
GROUP = 1024
NN = (((1,), (0,)), ((), ()))
NT = (((1,), (1,)), ((), ()))
TN = (((0,), (0,)), ((), ()))
TT = (((0,), (1,)), ((), ()))
VMEM_LIMIT = 60 << 20
COLUMNS = 384
UNITS = 512


def dot(left, right, dims=NN, precision=None):
    return lax.dot_general(left, right, dims, precision=precision, preferred_element_type=F32)


def call(body, name, flops, moved, **kwargs):
    return pl.pallas_call(
        body,
        name=name,
        compiler_params=pltpu.CompilerParams(vmem_limit_bytes=VMEM_LIMIT),
        cost_estimate=pl.CostEstimate(flops=flops // 8, bytes_accessed=moved // 8, transcendentals=0),
        **kwargs,
    )


def shaped(shape, kind):
    return jax.ShapeDtypeStruct(shape, kind)


def normed(values):
    centre = values - jnp.mean(values, axis=-1, keepdims=True)
    spread = jnp.mean(centre * centre, axis=-1, keepdims=True)
    inverse = lax.rsqrt(spread + NORM_EPS)
    return centre * inverse, inverse


def normed_back(grad, normal, inverse):
    first = jnp.mean(grad, axis=-1, keepdims=True)
    second = jnp.mean(grad * normal, axis=-1, keepdims=True)
    return inverse * (grad - first - normal * second)


def qkv_body(x_ref, mod_ref, w_ref, b_ref, h_ref, out_ref):
    @pl.when(pl.program_id(0) == 0)
    def _():
        for tile in range(x_ref.shape[0] // ROW):
            rows = slice(tile * ROW, tile * ROW + ROW)
            normal, _ = normed(x_ref[rows].astype(F32))
            h_ref[rows] = (normal * (1.0 + mod_ref[tile, 1:2]) + mod_ref[tile, 0:1]).astype(BF16)

    out_ref[...] = (dot(h_ref[...], w_ref[...]) + b_ref[...]).astype(BF16)


def qkv_call(x, mod, w, bias):
    tokens, width = x.shape
    wide = w.shape[1]
    block = width
    return call(
        qkv_body,
        "qkv",
        2 * tokens * width * wide,
        2 * (2 * tokens * width + width * wide + tokens * wide),
        grid=(wide // block,),
        in_specs=[
            pl.BlockSpec((tokens, width), lambda j: (0, 0)),
            pl.BlockSpec(mod.shape, lambda j: (0, 0, 0)),
            pl.BlockSpec((width, block), lambda j: (0, j)),
            pl.BlockSpec((1, block), lambda j: (0, j)),
        ],
        out_specs=[
            pl.BlockSpec((tokens, width), lambda j: (0, 0)),
            pl.BlockSpec((tokens, block), lambda j: (0, j)),
        ],
        out_shape=[shaped((tokens, width), BF16), shaped((tokens, wide), BF16)],
    )(x, mod, w, bias)


def pair_select(offset, head_width):
    row = lax.broadcasted_iota(jnp.int32, (256, 256), 0)
    col = lax.broadcasted_iota(jnp.int32, (256, 256), 1)
    lane = col & 127
    base = offset + jnp.where(col >= 128, head_width, 0)
    return jnp.where((lane < head_width) & (row == base + lane), 1.0, 0.0).astype(BF16)


def attention_body(flag_ref, qkv_ref, keep_ref, p_ref, ot_ref, om_ref, *, width, head_width):
    pair = pl.program_id(1)
    column = pair * (2 * head_width)
    start = pl.multiple_of(column // 128 * 128, 128)
    select = pair_select(column - start, head_width)
    scale = math.log2(math.e) / math.sqrt(head_width)
    tokens = qkv_ref.shape[0]

    @pl.when(pair == 0)
    def _():
        om_ref[...] = jnp.zeros_like(om_ref)

    q = dot(qkv_ref[:, pl.ds(start, 256)], select).astype(BF16)
    k = dot(qkv_ref[:, pl.ds(width + start, 256)], select).astype(BF16)
    v = dot(qkv_ref[:, pl.ds(2 * width + start, 256)], select)
    lane = lax.broadcasted_iota(jnp.int32, v.shape, 1) & 127
    v = jnp.where(lane == head_width, 1.0, v).astype(BF16)

    def part(head, first, count):
        rows = slice(first, first + count)
        lanes = slice(128 * head, 128 * head + 128)
        scores = dot(k[rows, lanes], q[rows, lanes], NT)
        top = jnp.max(scores, axis=0, keepdims=True)
        expo = jnp.exp2((scores - top) * scale)
        total = jnp.sum(expo, axis=0, keepdims=True)
        probs = (expo * (1.0 / total)).astype(BF16)
        p_ref[head, rows, rows] = probs
        mixed = dot(v[rows, lanes], probs, TN)
        ot_ref[head, :, rows] = mixed[:head_width] * (1.0 / mixed[head_width : head_width + 1])
        return (mixed * keep_ref[head, :, rows]).astype(BF16)

    def finish(parts):
        mixed = jnp.concatenate([jnp.concatenate(row, axis=1) for row in parts], axis=0)
        new = dot(mixed, select, TT)
        om_ref[:, pl.ds(start, 256)] = (om_ref[:, pl.ds(start, 256)].astype(F32) + new).astype(BF16)

    whole = flag_ref[pl.program_id(0)] == 1

    @pl.when(whole)
    def _():
        finish([[part(head, 0, tokens)] for head in range(2)])

    @pl.when(jnp.logical_not(whole))
    def _():
        finish([[part(head, at, ROW) for at in range(0, tokens, ROW)] for head in range(2)])


def attention_call(flag, qkv, keep, heads):
    tokens, wide = qkv.shape
    width = wide // 3
    head_width = width // heads
    groups = tokens // GROUP
    return call(
        functools.partial(attention_body, width=width, head_width=head_width),
        "attention",
        2 * 2 * heads * tokens * GROUP * 256,
        2 * tokens * wide + 2 * heads * tokens * GROUP + 6 * tokens * width,
        grid=(groups, heads // 2),
        in_specs=[
            pl.BlockSpec(memory_space=pltpu.SMEM),
            pl.BlockSpec((GROUP, wide), lambda g, h: (g, 0)),
            pl.BlockSpec((2, 1, GROUP), lambda g, h: (h, 0, g)),
        ],
        out_specs=[
            pl.BlockSpec((2, GROUP, GROUP), lambda g, h: (h, 0, g)),
            pl.BlockSpec((2, head_width, GROUP), lambda g, h: (h, 0, g)),
            pl.BlockSpec((GROUP, width), lambda g, h: (g, 0)),
        ],
        out_shape=[
            shaped((heads, GROUP, tokens), BF16),
            shaped((heads, head_width, tokens), F32),
            shaped((tokens, width), BF16),
        ],
    )(flag, qkv, keep)


def attention_back_body(
    flag_ref, qkv_ref, do_ref, p_ref, ot_ref, *refs, width, head_width, first_pair, span
):
    out_ref, ready_ref, ds_ref = refs[-3:]
    step = pl.program_id(1)
    pair = step + first_pair
    column = pair * (2 * head_width)
    start = pl.multiple_of(column // 128 * 128, 128)
    select = pair_select(column - start, head_width)
    scale = 1.0 / math.sqrt(head_width)
    tokens = qkv_ref.shape[0]

    @pl.when(step == 0)
    def _():
        out_ref[...] = refs[0][...] if len(refs) > 3 else jnp.zeros_like(out_ref)

    q = dot(qkv_ref[:, pl.ds(start, 256)], select).astype(BF16)
    k = dot(qkv_ref[:, pl.ds(width + start, 256)], select).astype(BF16)
    v = dot(qkv_ref[:, pl.ds(2 * width + start, 256)], select).astype(BF16)
    window = do_ref[:, pl.ds(start, 256)]
    do = dot(window, select).astype(BF16)
    do_t = dot(select, window, TT)
    delta = [
        jnp.sum(do_t[128 * head : 128 * head + head_width] * ot_ref[head], axis=0, keepdims=True)
        for head in range(2)
    ]

    def grad_scores(head, first, count):
        rows = slice(first, first + count)
        lanes = slice(128 * head, 128 * head + 128)
        dp = dot(v[rows, lanes], do[rows, lanes], NT)
        probs = p_ref[head, rows, rows].astype(F32)
        return (probs * (dp - delta[head][:, rows])).astype(BF16)

    def add(base, value, dims):
        new = dot(value, select, dims)
        spot = pl.ds(base + start, 256)
        out_ref[:, spot] = (out_ref[:, spot].astype(F32) + new).astype(BF16)

    def run(count):
        dq, dk, dv = [], [], []
        for head in range(2):
            lanes = slice(128 * head, 128 * head + 128)
            dq_row, dk_col, dv_col = [], [], []
            for first in range(0, tokens, count):
                rows = slice(first, first + count)
                ds = grad_scores(head, first, count)
                if count == tokens:
                    ds_ref[head] = ds
                    ds = ds_ref[head]
                dq_row.append((dot(k[rows, lanes], ds, TN) * scale).astype(BF16))
                dk_col.append((dot(ds, q[rows, lanes]) * scale).astype(BF16))
                dv_col.append(dot(p_ref[head, rows, rows], do[rows, lanes]).astype(BF16))
            dq.append(jnp.concatenate(dq_row, axis=1))
            dk.append(jnp.concatenate(dk_col, axis=0))
            dv.append(jnp.concatenate(dv_col, axis=0))
        add(0, jnp.concatenate(dq, axis=0), TT)
        add(width, jnp.concatenate(dk, axis=1), NT)
        add(2 * width, jnp.concatenate(dv, axis=1), NT)

    whole = flag_ref[pl.program_id(0)] == 1

    @pl.when(whole)
    def _():
        run(tokens)

    @pl.when(jnp.logical_not(whole))
    def _():
        run(ROW)

    @pl.when(step == pl.num_programs(1) - 1)
    def _():
        first, size = span
        for third in range(3):
            at = third * width + first
            ready_ref[:, third * size : (third + 1) * size] = out_ref[:, at : at + size]


def attention_back_call(flag, qkv, do, probs, mixed, part, *before):
    tokens, wide = qkv.shape
    width = wide // 3
    heads, head_width = mixed.shape[:2]
    groups = tokens // GROUP
    pairs = heads // 4
    base = part * pairs
    cut = width // 2 // 128 * 128
    span = (cut, width - cut) if part else (0, cut)
    whole = pl.BlockSpec((GROUP, wide), lambda g, h: (g, 0))
    return call(
        functools.partial(attention_back_body, width=width, head_width=head_width, first_pair=base, span=span),
        "attention_back",
        2 * 2 * heads * tokens * GROUP * 256,
        4 * tokens * wide + heads * tokens * GROUP + 6 * tokens * width,
        grid=(groups, pairs),
        in_specs=[
            pl.BlockSpec(memory_space=pltpu.SMEM),
            whole,
            pl.BlockSpec((GROUP, width), lambda g, h: (g, 0)),
            pl.BlockSpec((2, GROUP, GROUP), lambda g, h: (base + h, 0, g)),
            pl.BlockSpec((2, head_width, GROUP), lambda g, h: (base + h, 0, g)),
        ]
        + [whole] * len(before),
        out_specs=[whole, pl.BlockSpec((GROUP, 3 * span[1]), lambda g, h: (g, 0))],
        out_shape=[shaped((tokens, wide), BF16), shaped((tokens, 3 * span[1]), BF16)],
        scratch_shapes=[pltpu.VMEM((2, GROUP, GROUP), BF16)],
    )(flag, qkv, do, probs, mixed, *before)


def middle_body(
    om_ref, w_ref, b_ref, x_ref, mod_ref, top_ref, keep_ref, away_ref, own_ref,
    a_ref, x1_ref, h_ref, h_away_ref, h_own_ref, dm_ref, sum_ref,
):
    tile = pl.program_id(0)
    branch = dot(om_ref[...], w_ref[...]) + b_ref[...]
    a_ref[...] = branch
    middle = x_ref[...].astype(F32) + mod_ref[tile, 2:3] * branch
    x1_ref[...] = middle
    normal, _ = normed(middle)
    hidden = (normal * (1.0 + mod_ref[tile, 4:5]) + mod_ref[tile, 3:4]).astype(BF16)
    h_ref[...] = hidden
    h_away_ref[...] = dot(hidden, away_ref[...]).astype(BF16)
    h_own_ref[...] = dot(hidden, own_ref[...]).astype(BF16)
    grad = (top_ref[...].astype(F32) * mod_ref[tile, 5:6] * keep_ref[...]).astype(BF16)
    dm_ref[...] = grad
    sum_ref[0] = jnp.sum(grad.astype(F32), axis=0, keepdims=True)


def middle_call(om, w, bias, x, mod, top, keep, away, own):
    tokens, width = x.shape
    tiles = tokens // ROW
    rows = pl.BlockSpec((ROW, width), lambda i: (i, 0))
    half = pl.BlockSpec((ROW, width // 2), lambda i: (i, 0))
    fixed = pl.BlockSpec((width, width), lambda i: (0, 0))
    return call(
        middle_body,
        "middle",
        4 * tokens * width * width,
        26 * tokens * width,
        grid=(tiles,),
        in_specs=[
            rows,
            fixed,
            pl.BlockSpec((1, width), lambda i: (0, 0)),
            rows,
            pl.BlockSpec(mod.shape, lambda i: (0, 0, 0)),
            rows,
            pl.BlockSpec((ROW, 1), lambda i: (i, 0)),
            pl.BlockSpec((width, width // 2), lambda i: (0, 0)),
            pl.BlockSpec((width, width // 2), lambda i: (0, 0)),
        ],
        out_specs=[rows, rows, rows, half, half, rows, pl.BlockSpec((1, 1, width), lambda i: (i, 0, 0))],
        out_shape=[
            shaped((tokens, width), F32),
            shaped((tokens, width), F32),
            shaped((tokens, width), BF16),
            shaped((tokens, width // 2), BF16),
            shaped((tokens, width // 2), BF16),
            shaped((tokens, width), BF16),
            shaped((tiles, 1, width), F32),
        ],
    )(om, w, bias, x, mod, top, keep, away, own)


def hidden_body(h_ref, away_ref, dm_ref, w1_ref, b1_ref, w2_ref, *refs):
    g_ref, df_ref, sum_ref, send_ref = refs[-4:]
    first, second = math.sqrt(2.0 / math.pi), 0.044715
    pre = dot(h_ref[...], w1_ref[...]) + b1_ref[...]
    square = pre * pre
    tanh = jnp.tanh(first * pre * (1.0 + second * square))
    half = 0.5 * (1.0 + tanh)
    g_ref[...] = (pre * half).astype(BF16)
    slope = half + (0.5 * first) * pre * (1.0 - tanh * tanh) * (1.0 + (3.0 * second) * square)
    grad = (dot(dm_ref[...], w2_ref[...], NT) * slope).astype(BF16)
    df_ref[...] = grad
    sum_ref[...] = jnp.sum(grad.astype(F32), axis=0, keepdims=True)
    send_ref[...] = dot(away_ref[...], grad, TN)


def hidden_call(h, away, dm, w1, b1, w2, first, count, before):
    tokens, width = h.shape
    hidden = w1.shape[1]
    block = UNITS
    base = first // block
    full = pl.BlockSpec((tokens, width), lambda j: (0, 0))
    half = width // 2
    place = pl.BlockSpec(memory_space=pl.ANY)
    return call(
        hidden_body,
        "hidden",
        6 * tokens * width * count,
        6 * tokens * width + 4 * tokens * count + 8 * width * count,
        grid=(count // block,),
        in_specs=[
            full,
            pl.BlockSpec((tokens, half), lambda j: (0, 0)),
            full,
            pl.BlockSpec((width, block), lambda j: (0, base + j)),
            pl.BlockSpec((1, block), lambda j: (0, base + j)),
            pl.BlockSpec((block, width), lambda j: (base + j, 0)),
        ]
        + [place] * len(before),
        out_specs=[
            pl.BlockSpec((tokens, block), lambda j: (0, base + j)),
            pl.BlockSpec((tokens, block), lambda j: (0, base + j)),
            pl.BlockSpec((1, block), lambda j: (0, base + j)),
            pl.BlockSpec((half, block), lambda j: (0, j)),
        ],
        out_shape=[
            shaped((tokens, hidden), BF16),
            shaped((tokens, hidden), BF16),
            shaped((1, hidden), F32),
            shaped((half, count), F32),
        ],
        input_output_aliases={6 + n: n for n in range(len(before))},
    )(h, away, dm, w1, b1, w2, *before)


def shard_rows(spot_ref, g_ref, grad, put):
    shards = spot_ref.shape[1]
    rows = g_ref.shape[1] // 2
    shard = g_ref.shape[1] // shards
    part = pl.program_id(0)
    place = 0
    for piece in range(2):
        made = dot(g_ref[:, piece * rows : (piece + 1) * rows], grad, TN)
        for at in range(0, rows, shard):
            put(spot_ref[part, place], made[at : at + shard])
            place += 1


def rows_send_body(side_ref, spot_ref, g_ref, dm_ref, out_ref):
    def put(spot, value):
        out_ref[spot] = value

    shard_rows(spot_ref, g_ref, dm_ref[...], put)


def rows_send_call(side, spots, g, dm):
    tokens, hidden = g.shape
    width = dm.shape[1]
    half = hidden // 2
    shards = spots.shape[1]
    return call(
        rows_send_body,
        "rows_send",
        2 * tokens * half * width,
        2 * tokens * (half + width) + 4 * half * width,
        grid_spec=pltpu.PrefetchScalarGridSpec(
            num_scalar_prefetch=2,
            grid=(width // COLUMNS,),
            in_specs=[
                pl.BlockSpec((tokens, half), lambda j, side, spots: (0, side[0])),
                pl.BlockSpec((tokens, COLUMNS), lambda j, side, spots: (0, j)),
            ],
            out_specs=pl.BlockSpec((shards, half // shards, COLUMNS), lambda j, side, spots: (0, 0, j)),
        ),
        out_shape=shaped((shards, half // shards, width), F32),
    )(side, spots, g, dm)


def rows_keep_body(side_ref, spot_ref, g_ref, dm_ref, got_ref, *outs, bounds):
    half = spot_ref.shape[1] // 2
    step = pl.program_id(0)
    for part in range(len(bounds) - 1):

        @pl.when((step >= bounds[part]) & (step < bounds[part + 1]))
        def _():
            def put(spot, value):
                value = value + got_ref[spot]

                @pl.when(spot < half)
                def _():
                    outs[2 * part + 1][jnp.minimum(spot, half - 1)] = value

                @pl.when(spot >= half)
                def _():
                    outs[2 * part][jnp.maximum(spot - half, 0)] = value

            shard_rows(spot_ref, g_ref, dm_ref[...], put)


def rows_keep_call(side, spots, g, dm, got, counts):
    tokens, hidden = g.shape
    width = dm.shape[1]
    half = hidden // 2
    steps, shards = spots.shape
    bounds = [sum(counts[:n]) for n in range(len(counts) + 1)]
    specs, shapes = [], []
    for part, count in enumerate(counts):
        for _ in range(2):
            specs.append(
                pl.BlockSpec(
                    (shards // 2, half // shards, COLUMNS),
                    functools.partial(
                        lambda j, side, spots, first, count: (0, 0, jnp.clip(j - first, 0, count - 1)),
                        first=bounds[part],
                        count=count,
                    ),
                )
            )
            shapes.append(shaped((shards // 2, half // shards, count * COLUMNS), F32))
    made = call(
        functools.partial(rows_keep_body, bounds=bounds),
        "rows_keep",
        2 * tokens * half * width,
        2 * tokens * (half + width) + 8 * half * width,
        grid_spec=pltpu.PrefetchScalarGridSpec(
            num_scalar_prefetch=2,
            grid=(steps,),
            in_specs=[
                pl.BlockSpec((tokens, half), lambda j, side, spots: (0, side[0])),
                pl.BlockSpec((tokens, COLUMNS), lambda j, side, spots: (0, j)),
                pl.BlockSpec((shards, half // shards, COLUMNS), lambda j, side, spots: (0, 0, j)),
            ],
            out_specs=specs,
        ),
        out_shape=shapes,
    )(side, spots, g, dm, got)
    made = [array.reshape(-1, array.shape[2]) for array in made]
    return list(zip(made[::2], made[1::2]))


def result_body(g_ref, w_ref, b_ref, x1_ref, mod_ref, top_ref, keep_ref, out_ref, sum_ref):
    tile = pl.program_id(0)
    branch = dot(g_ref[...], w_ref[...]) + b_ref[...]
    out_ref[...] = (x1_ref[...] + mod_ref[tile, 5:6] * keep_ref[...] * branch).astype(BF16)
    sum_ref[0] = jnp.sum(top_ref[...].astype(F32) * keep_ref[...] * branch, axis=0, keepdims=True)


def result_call(g, w, bias, x1, mod, top, keep):
    tokens, width = x1.shape
    hidden = g.shape[1]
    tiles = tokens // ROW
    rows = pl.BlockSpec((ROW, width), lambda i: (i, 0))
    return call(
        result_body,
        "result",
        2 * tokens * width * hidden,
        2 * tokens * hidden + 2 * hidden * width + 8 * tokens * width,
        grid=(tiles,),
        in_specs=[
            pl.BlockSpec((ROW, hidden), lambda i: (i, 0)),
            pl.BlockSpec((hidden, width), lambda i: (0, 0)),
            pl.BlockSpec((1, width), lambda i: (0, 0)),
            rows,
            pl.BlockSpec(mod.shape, lambda i: (0, 0, 0)),
            rows,
            pl.BlockSpec((ROW, 1), lambda i: (i, 0)),
        ],
        out_specs=[rows, pl.BlockSpec((1, 1, width), lambda i: (i, 0, 0))],
        out_shape=[shaped((tokens, width), BF16), shaped((tiles, 1, width), F32)],
    )(g, w, bias, x1, mod, top, keep)


def middle_back_body(
    df_ref, w1_ref, x1_ref, mod_ref, top_ref, a_ref, wp_ref, head_ref,
    dx_ref, da_ref, do_ref, sum_ref,
):
    tile = pl.program_id(0)
    grad = dot(df_ref[...], w1_ref[...], NT)
    normal, inverse = normed(x1_ref[...])
    back = normed_back(grad * (1.0 + mod_ref[tile, 4:5]), normal, inverse)
    dx = top_ref[...].astype(F32) + back
    dx_ref[...] = dx
    da = (dx * mod_ref[tile, 2:3]).astype(BF16)
    da_ref[...] = da
    do_ref[...] = (dot(da, wp_ref[...], NT) * head_ref[tile]).astype(BF16)
    sum_ref[0, 0:1] = jnp.sum(dx * a_ref[...], axis=0, keepdims=True)
    sum_ref[0, 1:2] = jnp.sum(grad, axis=0, keepdims=True)
    sum_ref[0, 2:3] = jnp.sum(grad * normal, axis=0, keepdims=True)
    sum_ref[0, 3:4] = jnp.sum(da.astype(F32), axis=0, keepdims=True)


def middle_back_call(df, w1, x1, mod, top, a, wp, head_rows):
    tokens, width = x1.shape
    hidden = df.shape[1]
    tiles = tokens // ROW
    rows = pl.BlockSpec((ROW, width), lambda i: (i, 0))
    return call(
        middle_back_body,
        "middle_back",
        2 * tokens * width * (hidden + width),
        2 * tokens * hidden + 2 * hidden * width + 18 * tokens * width,
        grid=(tiles,),
        in_specs=[
            pl.BlockSpec((ROW, hidden), lambda i: (i, 0)),
            pl.BlockSpec((width, hidden), lambda i: (0, 0)),
            rows,
            pl.BlockSpec(mod.shape, lambda i: (0, 0, 0)),
            rows,
            rows,
            pl.BlockSpec((width, width), lambda i: (0, 0)),
            pl.BlockSpec(head_rows.shape, lambda i: (0, 0, 0)),
        ],
        out_specs=[rows, rows, rows, pl.BlockSpec((1, 4, width), lambda i: (i, 0, 0))],
        out_shape=[
            shaped((tokens, width), F32),
            shaped((tokens, width), BF16),
            shaped((tokens, width), BF16),
            shaped((tiles, 4, width), F32),
        ],
    )(df, w1, x1, mod, top, a, wp, head_rows)


def step_of(counts):
    return next(size for size in (512, 640, 384, 128) if all(count % size == 0 for count in counts))


def operand_specs(pairs, step):
    specs, starts, at = [], [], 0
    for left, _, first, count in pairs:
        base, steps = first // step, count // step
        specs.append(pl.BlockSpec(left.shape, lambda j: (0, 0)))
        specs.append(
            pl.BlockSpec(
                (left.shape[0], step),
                functools.partial(lambda j, at, base, steps: (0, base + jnp.clip(j - at, 0, steps - 1)), at=at, base=base, steps=steps),
            )
        )
        starts.append(at)
        at += steps
    return specs, starts + [at]


def each_pair(starts, body):
    if len(starts) == 2:
        body(0)
        return
    step = pl.program_id(0)
    for number in range(len(starts) - 1):
        pl.when((step >= starts[number]) & (step < starts[number + 1]))(functools.partial(body, number))


def columns_send_body(*refs, starts):
    send_ref, sum_ref = refs[-2:]

    def run(number):
        grad = refs[2 * number + 1][...]
        send_ref[...] = dot(refs[2 * number][...], grad, TN)
        sum_ref[...] = jnp.sum(grad.astype(F32), axis=0, keepdims=True)

    each_pair(starts, run)


def columns_send_call(pairs, name):
    tokens, half = pairs[0][0].shape
    count = sum(pair[3] for pair in pairs)
    step = step_of([pair[3] for pair in pairs])
    specs, starts = operand_specs(pairs, step)
    return call(
        functools.partial(columns_send_body, starts=starts),
        name,
        2 * tokens * half * count,
        2 * tokens * (count + half) + 4 * half * count,
        grid=(count // step,),
        in_specs=specs,
        out_specs=[
            pl.BlockSpec((half, step), lambda j: (0, j)),
            pl.BlockSpec((1, step), lambda j: (0, j)),
        ],
        out_shape=[shaped((half, count), F32), shaped((1, count), F32)],
    )(*[array for pair in pairs for array in pair[:2]])


def columns_keep_body(*refs, starts):
    got_ref, send_ref, keep_ref = refs[-3:]
    rows = keep_ref.shape[0]

    def run(number):
        made = dot(refs[2 * number][...], refs[2 * number + 1][...], TN) + got_ref[...]
        send_ref[...] = made[rows:]
        keep_ref[...] = made[:rows]

    each_pair(starts, run)


def columns_keep_call(pairs, got, name):
    tokens, half = pairs[0][0].shape
    count = got.shape[1]
    step = step_of([pair[3] for pair in pairs])
    specs, starts = operand_specs(pairs, step)
    out = pl.BlockSpec((half // 2, step), lambda j: (0, j))
    made = call(
        functools.partial(columns_keep_body, starts=starts),
        name,
        2 * tokens * half * count,
        2 * tokens * (count + half) + 8 * half * count,
        grid=(count // step,),
        in_specs=specs + [pl.BlockSpec((half, step), lambda j: (0, j))],
        out_specs=[out, out],
        out_shape=[shaped((half // 2, count), F32)] * 2,
    )(*[array for pair in pairs for array in pair[:2]], got)
    return [tuple(made)]


def moved_body(left_ref, away_ref, own_ref, left_away_ref, left_own_ref):
    left_away_ref[...] = dot(left_ref[...], away_ref[...]).astype(BF16)
    left_own_ref[...] = dot(left_ref[...], own_ref[...]).astype(BF16)


def moved_call(left, away, own):
    tokens, width = left.shape
    half = width // 2
    block = tokens // 2
    fixed = pl.BlockSpec((width, half), lambda i: (0, 0))
    out = pl.BlockSpec((block, half), lambda i: (i, 0))
    return call(
        moved_body,
        "moved",
        2 * tokens * width * width,
        4 * tokens * width + 2 * width * width,
        grid=(2,),
        in_specs=[pl.BlockSpec((block, width), lambda i: (i, 0)), fixed, fixed],
        out_specs=[out, out],
        out_shape=[shaped((tokens, half), BF16)] * 2,
    )(left, away, own)


def first_back_body(dqkv_ref, w_ref, x_ref, mod_ref, dx_ref, out_ref, sum_ref):
    tile = pl.program_id(0)
    grad = dot(dqkv_ref[...], w_ref[...], NT)
    normal, inverse = normed(x_ref[...].astype(F32))
    out_ref[...] = dx_ref[...] + normed_back(grad * (1.0 + mod_ref[tile, 1:2]), normal, inverse)
    sum_ref[0, 0:1] = jnp.sum(grad, axis=0, keepdims=True)
    sum_ref[0, 1:2] = jnp.sum(grad * normal, axis=0, keepdims=True)


def first_back_call(dqkv, w, x, mod, dx):
    tokens, wide = dqkv.shape
    width = x.shape[1]
    tiles = tokens // ROW
    rows = pl.BlockSpec((ROW, width), lambda i: (i, 0))
    return call(
        first_back_body,
        "first_back",
        2 * tokens * width * wide,
        2 * tokens * wide + 2 * width * wide + 10 * tokens * width,
        grid=(tiles,),
        in_specs=[
            pl.BlockSpec((ROW, wide), lambda i: (i, 0)),
            pl.BlockSpec((width, wide), lambda i: (0, 0)),
            rows,
            pl.BlockSpec(mod.shape, lambda i: (0, 0, 0)),
            rows,
        ],
        out_specs=[rows, pl.BlockSpec((1, 2, width), lambda i: (i, 0, 0))],
        out_shape=[shaped((tokens, width), F32), shaped((tiles, 2, width), F32)],
    )(dqkv, w, x, mod, dx)


def modulation_back_body(
    me_ref, own_ref, other_ref, own_cond_ref, other_cond_ref, label_ref, w_ref,
    grad_ref, sum_ref, table_ref, act_ref, total_ref,
):
    step = pl.program_id(0)
    half = own_ref.shape[0]
    width = act_ref.shape[1]

    @pl.when(step == 0)
    def _():
        for at, cond_ref in ((0, own_cond_ref), (half, other_cond_ref)):
            cond = cond_ref[...]
            act_ref[at : at + half] = (cond / (1.0 + jnp.exp(-cond))).astype(BF16)

    mod = jnp.concatenate([own_ref[...], other_ref[...]], axis=0)
    sum_ref[...] = jnp.sum(mod, axis=0, keepdims=True)
    mod = mod.astype(BF16)
    shard = grad_ref.shape[0]
    row = lax.broadcasted_iota(jnp.int32, (width, 128), 0)
    column = lax.broadcasted_iota(jnp.int32, (width, 128), 1)
    picked = jnp.where((column < shard) & (row == me_ref[0] * shard + column), 1.0, 0.0).astype(BF16)
    own_act = dot(act_ref[...], picked).astype(BF16)
    grad_ref[...] = dot(own_act, mod, TN)[:shard]
    part = dot(mod, w_ref[...], NT)

    @pl.when(step == 0)
    def _():
        total_ref[...] = part

    @pl.when(step > 0)
    def _():
        total_ref[...] += part

    @pl.when(step == pl.num_programs(0) - 1)
    def _():
        cond = jnp.concatenate([own_cond_ref[...], other_cond_ref[...]], axis=0)
        gate = 1.0 / (1.0 + jnp.exp(-cond))
        grad = total_ref[...] * (gate * (1.0 + cond * (1.0 - gate)))
        classes = table_ref.shape[0]
        select = (label_ref[...] == lax.broadcasted_iota(jnp.int32, (2 * half, classes), 1)).astype(F32)
        table_ref[...] = dot(select, grad, TN, HIGHEST)


def modulation_back_call(me, own, other, used, w, classes, shard):
    rows = own.shape[0]
    width, wide = w.shape
    block = 768
    at = wide // width
    part = pl.BlockSpec((rows, block), lambda j: (0, j))
    cond = pl.BlockSpec((rows, width), lambda j: (0, at))
    return call(
        modulation_back_body,
        "modulation_back",
        4 * rows * width * wide,
        2 * width * wide,
        grid=(wide // block,),
        in_specs=[
            pl.BlockSpec(memory_space=pltpu.SMEM),
            part,
            part,
            cond,
            cond,
            pl.BlockSpec(used.shape, lambda j: (0, 0)),
            pl.BlockSpec((width, block), lambda j: (0, j)),
        ],
        out_specs=[
            pl.BlockSpec((shard, block), lambda j: (0, j)),
            pl.BlockSpec((1, block), lambda j: (0, j)),
            pl.BlockSpec((classes, width), lambda j: (0, 0)),
        ],
        out_shape=[shaped((shard, wide), F32), shaped((1, wide), F32), shaped((classes, width), F32)],
        scratch_shapes=[pltpu.VMEM((2 * rows, width), BF16), pltpu.VMEM((2 * rows, width), F32)],
    )(me, own, other, own, other, used, w)


def add_body(*refs, plans):
    outs = refs[-len(plans) :]
    at = 0
    for out_ref, (count, first, rows) in zip(outs, plans):
        value = refs[at][first : first + rows]
        for term in range(1, count):
            value = value + refs[at + term][first : first + rows]
        out_ref[...] = value
        at += count


def add_call(jobs):
    steps = 3 if all(terms[0].shape[1] % 384 == 0 for terms, _, _ in jobs) else 2
    if any(terms[0].shape[1] % (128 * steps) for terms, _, _ in jobs):
        steps = 1
    operands, specs, outs, shapes, plans = [], [], [], [], []
    moved = 0
    for terms, first, rows in jobs:
        wide = terms[0].shape[1]
        block = wide // steps
        for term in terms:
            size, index, at = rows, first // rows, 0
            while size % 8 and size < term.shape[0]:
                size, index, at = size * 2, 0, first
            operands.append(term)
            specs.append(pl.BlockSpec((size, block), functools.partial(lambda j, index: (index, j), index=index)))
        plans.append((len(terms), at, rows))
        outs.append(pl.BlockSpec((rows, block), lambda j: (0, j)))
        shapes.append(shaped((rows, wide), F32))
        moved += 4 * rows * wide * (len(terms) + 1)
    return call(
        functools.partial(add_body, plans=plans),
        "add",
        moved // 4,
        moved,
        grid=(steps,),
        in_specs=specs,
        out_specs=outs,
        out_shape=shapes,
    )(*operands)


def bit_order(bits, core, lead):
    order = list(range(bits))
    if bits >= 2 and core:
        order[:2] = [1, 0]
    if lead and lead < bits:
        order.remove(lead)
        order.insert(0, lead)
    return order


class Chunk:
    def __init__(self, send, kept, wait, lead):
        self.send, self.terms, self.wait, self.lead = send, [kept], wait, lead
        self.rows = kept.shape[0]
        self.stage = 0


class Spread:
    def __init__(self, rows):
        self.own, self.other = rows, None
        self.stage = 0


class Flow:
    def __init__(self, bits):
        self.bits = bits
        self.fresh, self.crossing, self.chunks, self.last = [], [], [], []
        self.blocks = ([], [], [])
        self.spreads = []

    def emit(self, send, keep, store, waits=(0,), leads=(0,)):
        self.fresh.append((send, keep, store, waits, leads))

    def spread(self, rows):
        self.spreads.append(Spread(rows))
        return self.spreads[-1]

    def busy(self):
        moving = self.fresh or self.crossing or any(chunk.stage < self.bits for chunk in self.chunks)
        return moving or any(spread.stage <= self.bits for spread in self.spreads)

    def pairs(self, stage, lead):
        size = 1 << self.bits
        flips = [1 << bit_order(self.bits, core, lead)[stage] for core in range(2)]
        return [(core * size + i, core * size + (i ^ flips[core])) for core in range(2) for i in range(size)]

    def received(self, live):
        live, (cores, blocks, doubles) = lax.optimization_barrier((live, self.blocks))
        for spread, block in zip([spread for spread in self.spreads if spread.other is None and spread.stage], doubles):
            if spread.stage > self.bits:
                spread.other = block
            else:
                spread.own = jnp.concatenate([spread.own, block], axis=0)
        jobs, waiting = [], []
        for chunk, block in zip(self.last, blocks):
            chunk.terms.append(block)
            if chunk.stage < self.bits:
                chunk.rows //= 2
                jobs.append((chunk.terms, chunk.rows, chunk.rows))
                waiting.append(chunk)
        for (_, keep, store, waits, leads), core in zip(self.crossing, cores):
            new = [Chunk(*pair, wait, lead) for pair, wait, lead in zip(keep(core), waits, leads)]
            store += new
            self.chunks += new
        for chunk, value in zip(waiting, add_call(jobs) if jobs else []):
            chunk.send = value
        return live

    def round(self, live):
        live = self.received(live)
        moving = [chunk for chunk in self.chunks if chunk.stage < self.bits and not chunk.wait]
        for chunk in self.chunks:
            chunk.wait = max(0, chunk.wait - 1)
        crossing, self.fresh = self.fresh, []
        doubling = [spread for spread in self.spreads if spread.stage <= self.bits]
        live, cores, sends, doubles = lax.optimization_barrier(
            (
                live,
                [entry[0] for entry in crossing],
                [chunk.send for chunk in moving],
                [spread.own for spread in doubling],
            )
        )
        blocks = []
        for chunk, send in zip(moving, sends):
            blocks.append(lax.ppermute(send, ("stream", "batch"), self.pairs(chunk.stage, chunk.lead)))
            chunk.stage += 1
        cores = [lax.ppermute(send, "stream", [(0, 1), (1, 0)]) for send in cores]
        for number, (spread, rows) in enumerate(zip(doubling, doubles)):
            spread.own = rows
            if spread.stage < self.bits:
                pairs = self.pairs(self.bits - 1 - spread.stage, 0)
                doubles[number] = lax.ppermute(rows, ("stream", "batch"), pairs)
            else:
                doubles[number] = lax.ppermute(rows, "stream", [(0, 1), (1, 0)])
            spread.stage += 1
        self.crossing, self.last, self.blocks = crossing, moving, (cores, blocks, doubles)
        return live

    def totals(self, live):
        while self.busy():
            live = self.round(live)
        live = self.received(live)
        return live, add_call([(chunk.terms, 0, chunk.rows) for chunk in self.chunks])


def offsets_of(bits, side, lead):
    places = jnp.arange(1 << bits, dtype=jnp.int32)
    made = []
    for core in range(2):
        offset = jnp.zeros_like(places)
        for stage, bit in enumerate(bit_order(bits, core, lead)):
            offset = offset | (((places >> (bits - 1 - stage)) & 1) << bit)
        made.append(offset)
    return jnp.where(side == 0, made[0], made[1])


def places_of(bits, side, lead, offset):
    made = []
    for core in range(2):
        place = jnp.zeros_like(offset)
        for stage, bit in enumerate(bit_order(bits, core, lead)):
            place = place | (((offset >> bit) & 1) << (bits - 1 - stage))
        made.append(place)
    return jnp.where(side == 0, made[0], made[1])


def time_embed(steps_in, width):
    half_width = width // 2
    frequency = jnp.exp(-math.log(10000.0) * jnp.arange(half_width, dtype=F32) / half_width)
    angles = steps_in.astype(F32)[:, None] * frequency[None, :]
    return jnp.concatenate([jnp.cos(angles), jnp.sin(angles)], axis=1)


def per_device(
    tokens, segments, timesteps, labels, head_keep, token_keep, class_table, w_ada, b_ada,
    w_qkv, b_qv, w_proj, b_proj, w_fc1, b_fc1, w_fc2, b_fc2, out_grad, *, batch,
):
    x, top = tokens[0], out_grad[0]
    count, width = x.shape
    hidden = w_fc1.shape[1]
    heads = head_keep.shape[1]
    head_width = width // heads
    items = timesteps.shape[0]
    tiles = count // ROW
    groups = count // GROUP
    null_class = class_table.shape[0] - 1
    bits = batch.bit_length() - 1
    devices = 2 * batch
    stream = lax.axis_index("stream")
    index = lax.axis_index("batch")

    own_labels = lax.dynamic_slice_in_dim(labels, index * items, items)
    used = jnp.where(stream == 0, own_labels, null_class)
    cond = time_embed(timesteps, width) + jnp.take(class_table, used, axis=0).astype(F32)
    act = jax.nn.silu(cond).astype(BF16)
    modulation = dot(act, w_ada) + b_ada
    tile_item = segments[::ROW] - index * items
    chosen = tile_item[:, None] == jnp.arange(items, dtype=jnp.int32)[None, :]
    mod = jnp.sum(jnp.where(chosen[:, :, None], modulation[None], 0.0), axis=1)
    mod = mod.reshape(tiles, 6, width)
    tile_heads = jnp.sum(jnp.where(chosen[:, :, None], head_keep[None], 0), axis=1).astype(F32)
    head_rows = jnp.repeat(tile_heads, head_width, axis=1).reshape(tiles, 1, width)
    head_columns = jnp.repeat(tile_heads.T, ROW, axis=1).reshape(heads, 1, count)
    keep = token_keep[0].astype(F32)[:, None]
    grouped = segments.reshape(groups, GROUP)
    flag = (grouped[:, 0] == grouped[:, -1]).astype(jnp.int32)

    shard = width // devices

    def picked(side):
        order = side * batch + (index ^ offsets_of(bits, side, 0))
        source = (order[:, None] * shard + jnp.arange(shard, dtype=jnp.int32)[None, :]).reshape(width // 2)
        return (jnp.arange(width, dtype=jnp.int32)[:, None] == source[None, :]).astype(BF16)

    def spots(side):
        return jnp.stack([places_of(bits, side, lead, jnp.arange(batch, dtype=jnp.int32) ^ index) for steps, lead in ROW_PARTS for _ in range(steps)])

    other = 1 - stream
    away, own = picked(other), picked(stream)

    bias_full = jnp.concatenate([b_qv[:width], jnp.zeros((width,), F32), b_qv[width:]])[None]
    h1, qkv = qkv_call(x, mod, w_qkv, bias_full)
    probs, mixed, om = attention_call(flag, qkv, head_columns, heads)
    a, x1, h2, h2_away, h2_own, dm, sum_dm = middle_call(om, w_proj, b_proj[None], x, mod, top, keep, away, own)

    flow = Flow(bits)
    fc1, fc2, wide = [], [], []

    filled, latest = (), {}
    for low, high in ((0, 2 * UNITS), (2 * UNITS, 5 * UNITS), (5 * UNITS, hidden)):
        *filled, send = hidden_call(h2, h2_away, dm, w_fc1, b_fc1[None], w_fc2, low, high - low, filled)
        latest["df"] = filled[1]

        def hidden_keep(got, low=low, count=high - low):
            return columns_keep_call([(h2_own, latest["df"], low, count)], got, "hidden_keep")

        flow.emit(send, hidden_keep, fc1)
        h2, filled = flow.round((h2, filled))
        latest["df"] = filled[1]
    g, df, sum_df = filled

    rows_send = rows_send_call(other[None], spots(other), g, dm)
    flow.emit(
        rows_send.reshape(-1, width),
        lambda got: rows_keep_call(
            stream[None], spots(stream), g, dm, got.reshape(rows_send.shape), [steps for steps, _ in ROW_PARTS]
        ),
        fc2,
        [0] * len(ROW_PARTS),
        [lead for _, lead in ROW_PARTS],
    )
    om_away, om_own = moved_call(om, away, own)
    h1_away, h1_own = moved_call(h1, away, own)
    df, x1, om_away, om_own, h1_away, h1_own = flow.round((df, x1, om_away, om_own, h1_away, h1_own))
    dx1, da, do, sums_two = middle_back_call(df, w_fc1, x1, mod, top, a, w_proj, head_rows)

    def by_item(*sums):
        by_tile = jnp.concatenate(sums, axis=1)
        return jnp.sum(jnp.where(chosen[:, :, None], by_tile[:, None], 0.0), axis=0).astype(BF16).astype(F32)

    def in_rows(*sums):
        made = jnp.concatenate([part.reshape(devices, -1) for part in sums], axis=1).reshape(items, -1)
        return jnp.pad(made, ((0, 0), (0, -made.shape[1] % 128)))

    def own_part(gathered, first, count):
        each = devices // items
        rows = lax.dynamic_index_in_dim(gathered.reshape(batch, items, -1), me // each, axis=1, keepdims=False)
        return jnp.sum(lax.dynamic_slice_in_dim(rows, first + me % each * count, count, axis=1), axis=0)

    me = stream * batch + index

    def used_labels(side):
        order = bit_order(bits, 0, 0)[::-1], bit_order(bits, 1, 0)[::-1]
        places = jnp.arange(batch, dtype=jnp.int32)
        offsets = [sum(((places >> n) & 1) << bit for n, bit in enumerate(bits_of)) for bits_of in order]
        from_device = index ^ jnp.where(side == 0, offsets[0], offsets[1])
        return jnp.where(side == 0, jnp.take(labels.reshape(batch, items), from_device, axis=0).reshape(-1), null_class)

    used_rows = jnp.concatenate([used_labels(stream), used_labels(other)])[:, None]
    dx1, da, do, sums_two = flow.round((dx1, da, do, sums_two))
    dqkv, ready = attention_back_call(flag, qkv, do, probs, mixed, 0)
    first_pairs = [(om_away, da, 0, width), (h1_away, ready, 0, ready.shape[1])]
    own_pairs = [(om_own, da, 0, width), (h1_own, ready, 0, ready.shape[1])]
    send, first_sums = columns_send_call(first_pairs, "first_send")
    low_sums = first_sums[:, width:]
    flow.emit(send, lambda got: columns_keep_call(own_pairs, got, "first_keep"), wide)
    dqkv, low_sums = flow.round((dqkv, low_sums))
    dqkv, rest = attention_back_call(flag, qkv, do, probs, mixed, 1, dqkv)
    send, high_sums = columns_send_call([(h1_away, rest, 0, rest.shape[1])], "last_send")
    flow.emit(send, lambda got: columns_keep_call([(h1_own, rest, 0, rest.shape[1])], got, "last_keep"), wide)
    dqkv, dx1, high_sums, g = flow.round((dqkv, dx1, high_sums, g))
    grad_tokens, sums_one = first_back_call(dqkv, w_qkv, x, mod, dx1)
    result, sum_gate = result_call(g, w_fc2, b_fc2[None], x1, mod, top, keep)

    def in_order(low, high):
        first, second = low.shape[1] // 3, high.shape[1] // 3
        return [
            part
            for third in range(3)
            for part in (low[:, third * first : (third + 1) * first], high[:, third * second : (third + 1) * second])
        ]

    grad_tokens, sums_one, result, sum_gate = flow.round((grad_tokens, sums_one, result, sum_gate))
    column_sums = in_order(low_sums, high_sums)
    spread = flow.spread(
        jnp.concatenate(
            [
                by_item(
                    sums_one[:, 0], sums_one[:, 1], sums_two[:, 0], sums_two[:, 1], sums_two[:, 2], sum_gate[:, 0]
                ),
                cond,
                in_rows(
                    sum_df[0],
                    jnp.sum(sum_dm, axis=(0, 1)),
                    jnp.sum(sums_two[:, 3], axis=0),
                    jnp.concatenate(column_sums[:2] + column_sums[4:], axis=1)[0],
                ),
            ],
            axis=1,
        )
    )
    result, shards = flow.totals(result)
    grad_w_ada, mod_sums, grad_table = modulation_back_call(
        me[None], spread.own, spread.other, used_rows, w_ada, null_class + 1, shard
    )
    share = 6 * width // devices
    grad_b_ada = lax.dynamic_slice_in_dim(mod_sums[0], me * share, share)
    ends = [hidden // devices, width // devices, width // devices, 2 * width // devices]
    bias = sum(own_part(rows, 7 * width, sum(ends)) for rows in (spread.own, spread.other))
    at = [sum(ends[:n]) for n in range(5)]
    grad_b_fc1, grad_b_fc2, grad_b_proj, grad_b_qv = [bias[at[n] : at[n + 1]] for n in range(4)]
    shards = dict(zip(map(id, flow.chunks), shards))
    grad_w_fc1, grad_w_fc2 = [
        jnp.concatenate([shards[id(chunk)] for chunk in store], axis=1) for store in (fc1, fc2)
    ]
    first_shard, last_shard = [shards[id(chunk)] for chunk in wide]
    grad_w_proj = first_shard[:, :width]
    grad_w_qkv = jnp.concatenate(in_order(first_shard[:, width:], last_shard), axis=1)

    return (
        result[None],
        grad_tokens[None],
        grad_table,
        grad_w_ada,
        grad_b_ada,
        grad_w_qkv,
        grad_b_qv,
        grad_w_proj,
        grad_b_proj,
        grad_w_fc1,
        grad_b_fc1,
        grad_w_fc2,
        grad_b_fc2,
    )


def solution(mesh):
    both = ("stream", "batch")
    return jax.shard_map(
        functools.partial(per_device, batch=mesh.shape["batch"]),
        mesh=mesh,
        in_specs=(
            P("stream", "batch", None),
            P("batch"),
            P("batch"),
            P(),
            P("batch", None),
            P("stream", "batch"),
            P(), P(), P(), P(), P(), P(), P(), P(), P(), P(), P(),
            P("stream", "batch", None),
        ),
        out_specs=(
            P("stream", "batch", None),
            P("stream", "batch", None),
            P(),
            P(both, None),
            P(both),
            P(both, None),
            P(both),
            P(both, None),
            P(both),
            P(both, None),
            P(both),
            P(both, None),
            P(both),
        ),
        check_vma=False,
    )
```

```python
import functools
import math

import jax
import jax.numpy as jnp
from jax import lax
from jax.experimental import pallas as pl
from jax.experimental.pallas import tpu as pltpu
from jax.sharding import PartitionSpec as P

F32 = jnp.float32
BF16 = jnp.bfloat16
HIGHEST = lax.Precision.HIGHEST
NORM_EPS = 1e-06
ROW_PARTS = ((2, 0), (1, 2))
ROW = 256
GROUP = 1024
NN = (((1,), (0,)), ((), ()))
NT = (((1,), (1,)), ((), ()))
TN = (((0,), (0,)), ((), ()))
TT = (((0,), (1,)), ((), ()))
VMEM_LIMIT = 60 << 20
COLUMNS = 384
UNITS = 512


def dot(left, right, dims=NN, precision=None):
    return lax.dot_general(left, right, dims, precision=precision, preferred_element_type=F32)


def call(body, name, flops, moved, **kwargs):
    return pl.pallas_call(
        body,
        name=name,
        compiler_params=pltpu.CompilerParams(vmem_limit_bytes=VMEM_LIMIT),
        cost_estimate=pl.CostEstimate(flops=flops // 8, bytes_accessed=moved // 8, transcendentals=0),
        **kwargs,
    )


def shaped(shape, kind):
    return jax.ShapeDtypeStruct(shape, kind)


def normed(values):
    centre = values - jnp.mean(values, axis=-1, keepdims=True)
    spread = jnp.mean(centre * centre, axis=-1, keepdims=True)
    inverse = lax.rsqrt(spread + NORM_EPS)
    return centre * inverse, inverse


def normed_back(grad, normal, inverse):
    first = jnp.mean(grad, axis=-1, keepdims=True)
    second = jnp.mean(grad * normal, axis=-1, keepdims=True)
    return inverse * (grad - first - normal * second)


def qkv_body(x_ref, mod_ref, w_ref, b_ref, h_ref, out_ref):
    @pl.when(pl.program_id(0) == 0)
    def _():
        for tile in range(x_ref.shape[0] // ROW):
            rows = slice(tile * ROW, tile * ROW + ROW)
            normal, _ = normed(x_ref[rows].astype(F32))
            h_ref[rows] = (normal * (1.0 + mod_ref[tile, 1:2]) + mod_ref[tile, 0:1]).astype(BF16)

    out_ref[...] = (dot(w_ref[...], h_ref[...], TT) + b_ref[...]).astype(BF16)


def qkv_call(x, mod, w, bias):
    tokens, width = x.shape
    wide = w.shape[1]
    block = width
    return call(
        qkv_body,
        "qkv",
        2 * tokens * width * wide,
        2 * (2 * tokens * width + width * wide + tokens * wide),
        grid=(wide // block,),
        in_specs=[
            pl.BlockSpec((tokens, width), lambda j: (0, 0)),
            pl.BlockSpec(mod.shape, lambda j: (0, 0, 0)),
            pl.BlockSpec((width, block), lambda j: (0, j)),
            pl.BlockSpec((block, 1), lambda j: (j, 0)),
        ],
        out_specs=[
            pl.BlockSpec((tokens, width), lambda j: (0, 0)),
            pl.BlockSpec((block, tokens), lambda j: (j, 0)),
        ],
        out_shape=[shaped((tokens, width), BF16), shaped((wide, tokens), BF16)],
    )(x, mod, w, bias)


def heads_of(ref, head_width):
    values = ref[...].astype(F32)
    return [values[head * head_width : (head + 1) * head_width] for head in range(2)]


def attention_body(flag_ref, q_ref, k_ref, v_ref, keep_ref, p_ref, ot_ref, om_ref):
    head_width = ot_ref.shape[1]
    scale = math.log2(math.e) / math.sqrt(head_width)
    tokens = q_ref.shape[1]
    q, k = [[part.astype(BF16) for part in heads_of(ref, head_width)] for ref in (q_ref, k_ref)]
    v = [jnp.concatenate([part, jnp.ones((8, tokens), F32)], axis=0).astype(BF16) for part in heads_of(v_ref, head_width)]

    def part(head, first, count):
        rows = slice(first, first + count)
        scores = dot(k[head][:, rows], q[head][:, rows], TN)
        top = jnp.max(scores, axis=0, keepdims=True)
        expo = jnp.exp2((scores - top) * scale)
        total = jnp.sum(expo, axis=0, keepdims=True)
        probs = (expo * (1.0 / total)).astype(BF16)
        p_ref[head, rows, rows] = probs
        mixed = dot(v[head][:, rows], probs)
        ot_ref[head, :, rows] = mixed[:head_width] * (1.0 / mixed[head_width : head_width + 1])
        return mixed[:head_width] * keep_ref[head, :, rows]

    def run(count):
        made = [
            jnp.concatenate([part(head, at, count) for at in range(0, tokens, count)], axis=1) for head in range(2)
        ]
        om_ref[...] = jnp.concatenate(made, axis=0).astype(BF16)

    whole = flag_ref[pl.program_id(0)] == 1
    pl.when(whole)(lambda: run(tokens))
    pl.when(jnp.logical_not(whole))(lambda: run(ROW))


def attention_call(flag, qkv, keep, heads):
    wide, tokens = qkv.shape
    width = wide // 3
    head_width = width // heads
    groups = tokens // GROUP
    pairs = heads // 2
    rows = 2 * head_width

    def third(number):
        return pl.BlockSpec((rows, GROUP), functools.partial(lambda g, h, base: (base + h, g), base=number * pairs))

    return call(
        attention_body,
        "attention",
        2 * 2 * heads * tokens * GROUP * 256,
        2 * tokens * wide + 2 * heads * tokens * GROUP + 6 * tokens * width,
        grid=(groups, pairs),
        in_specs=[
            pl.BlockSpec(memory_space=pltpu.SMEM),
            third(0),
            third(1),
            third(2),
            pl.BlockSpec((2, 1, GROUP), lambda g, h: (h, 0, g)),
        ],
        out_specs=[
            pl.BlockSpec((2, GROUP, GROUP), lambda g, h: (h, 0, g)),
            pl.BlockSpec((2, head_width, GROUP), lambda g, h: (h, 0, g)),
            third(0),
        ],
        out_shape=[
            shaped((heads, GROUP, tokens), BF16),
            shaped((heads, head_width, tokens), F32),
            shaped((width, tokens), BF16),
        ],
    )(flag, qkv, qkv, qkv, keep)


def attention_back_body(flag_ref, q_ref, k_ref, v_ref, do_ref, keep_ref, p_ref, ot_ref, out_ref, ds_ref):
    head_width = ot_ref.shape[1]
    scale = 1.0 / math.sqrt(head_width)
    tokens = q_ref.shape[1]
    q, k, v = [[part.astype(BF16) for part in heads_of(ref, head_width)] for ref in (q_ref, k_ref, v_ref)]
    kept = [part * keep_ref[head] for head, part in enumerate(heads_of(do_ref, head_width))]
    do = [part.astype(BF16) for part in kept]
    delta = [jnp.sum(kept[head] * ot_ref[head], axis=0, keepdims=True) for head in range(2)]

    def run(count):
        made = [[], [], []]
        for head in range(2):
            row = [[], [], []]
            for first in range(0, tokens, count):
                rows = slice(first, first + count)
                dp = dot(v[head][:, rows], do[head][:, rows], TN)
                probs = p_ref[head, rows, rows].astype(F32)
                ds = (probs * (dp - delta[head][:, rows])).astype(BF16)
                if count == tokens:
                    ds_ref[head] = ds
                    ds = ds_ref[head]
                row[0].append(dot(k[head][:, rows], ds) * scale)
                row[1].append(dot(q[head][:, rows], ds, NT) * scale)
                row[2].append(dot(do[head][:, rows], p_ref[head, rows, rows], NT))
            for third in range(3):
                made[third].append(jnp.concatenate(row[third], axis=1))
        for third in range(3):
            out_ref[third] = jnp.concatenate(made[third], axis=0).astype(BF16)

    whole = flag_ref[pl.program_id(0)] == 1
    pl.when(whole)(lambda: run(tokens))
    pl.when(jnp.logical_not(whole))(lambda: run(ROW))


def attention_back_call(flag, qkv, do, keep, probs, mixed, part):
    wide, tokens = qkv.shape
    width = wide // 3
    heads, head_width = mixed.shape[:2]
    groups = tokens // GROUP
    pairs = heads // 4
    base = part * pairs
    rows = 2 * head_width

    def third(number):
        first = number * heads // 2 + base
        return pl.BlockSpec((rows, GROUP), functools.partial(lambda g, h, first: (first + h, g), first=first))

    return call(
        attention_back_body,
        "attention_back",
        2 * 2 * heads * tokens * GROUP * 256,
        2 * tokens * wide + heads * tokens * GROUP + 6 * tokens * width,
        grid=(groups, pairs),
        in_specs=[
            pl.BlockSpec(memory_space=pltpu.SMEM),
            third(0),
            third(1),
            third(2),
            third(0),
            pl.BlockSpec((2, 1, GROUP), lambda g, h: (base + h, 0, g)),
            pl.BlockSpec((2, GROUP, GROUP), lambda g, h: (base + h, 0, g)),
            pl.BlockSpec((2, head_width, GROUP), lambda g, h: (base + h, 0, g)),
        ],
        out_specs=pl.BlockSpec((3, rows, GROUP), lambda g, h: (0, h, g)),
        out_shape=shaped((3, width // 2, tokens), BF16),
        scratch_shapes=[pltpu.VMEM((2, GROUP, GROUP), BF16)],
    )(flag, qkv, qkv, qkv, do, keep, probs, mixed)


def middle_body(
    om_ref, w_ref, b_ref, x_ref, mod_ref, top_ref, keep_ref, away_ref, own_ref,
    a_ref, x1_ref, h_ref, h_away_ref, h_own_ref, dm_ref, sum_ref,
):
    tile = pl.program_id(0)
    branch = dot(om_ref[...], w_ref[...], TN) + b_ref[...]
    a_ref[...] = branch
    middle = x_ref[...].astype(F32) + mod_ref[tile, 2:3] * branch
    x1_ref[...] = middle
    normal, _ = normed(middle)
    hidden = (normal * (1.0 + mod_ref[tile, 4:5]) + mod_ref[tile, 3:4]).astype(BF16)
    h_ref[...] = hidden
    h_away_ref[...] = dot(hidden, away_ref[...]).astype(BF16)
    h_own_ref[...] = dot(hidden, own_ref[...]).astype(BF16)
    grad = (top_ref[...].astype(F32) * mod_ref[tile, 5:6] * keep_ref[...]).astype(BF16)
    dm_ref[...] = grad
    sum_ref[0] = jnp.sum(grad.astype(F32), axis=0, keepdims=True)


def middle_call(om, w, bias, x, mod, top, keep, away, own):
    tokens, width = x.shape
    tiles = tokens // ROW
    rows = pl.BlockSpec((ROW, width), lambda i: (i, 0))
    half = pl.BlockSpec((ROW, width // 2), lambda i: (i, 0))
    fixed = pl.BlockSpec((width, width), lambda i: (0, 0))
    return call(
        middle_body,
        "middle",
        4 * tokens * width * width,
        26 * tokens * width,
        grid=(tiles,),
        in_specs=[
            pl.BlockSpec((width, ROW), lambda i: (0, i)),
            fixed,
            pl.BlockSpec((1, width), lambda i: (0, 0)),
            rows,
            pl.BlockSpec(mod.shape, lambda i: (0, 0, 0)),
            rows,
            pl.BlockSpec((ROW, 1), lambda i: (i, 0)),
            pl.BlockSpec((width, width // 2), lambda i: (0, 0)),
            pl.BlockSpec((width, width // 2), lambda i: (0, 0)),
        ],
        out_specs=[rows, rows, rows, half, half, rows, pl.BlockSpec((1, 1, width), lambda i: (i, 0, 0))],
        out_shape=[
            shaped((tokens, width), F32),
            shaped((tokens, width), F32),
            shaped((tokens, width), BF16),
            shaped((tokens, width // 2), BF16),
            shaped((tokens, width // 2), BF16),
            shaped((tokens, width), BF16),
            shaped((tiles, 1, width), F32),
        ],
    )(om, w, bias, x, mod, top, keep, away, own)


def hidden_body(h_ref, away_ref, dm_ref, w1_ref, b1_ref, w2_ref, *refs):
    g_ref, df_ref, sum_ref, send_ref = refs[-4:]
    first, second = math.sqrt(2.0 / math.pi), 0.044715
    pre = dot(h_ref[...], w1_ref[...]) + b1_ref[...]
    square = pre * pre
    tanh = jnp.tanh(first * pre * (1.0 + second * square))
    half = 0.5 * (1.0 + tanh)
    g_ref[...] = (pre * half).astype(BF16)
    slope = half + (0.5 * first) * pre * (1.0 - tanh * tanh) * (1.0 + (3.0 * second) * square)
    grad = (dot(dm_ref[...], w2_ref[...], NT) * slope).astype(BF16)
    df_ref[...] = grad
    sum_ref[...] = jnp.sum(grad.astype(F32), axis=0, keepdims=True)
    send_ref[...] = dot(away_ref[...], grad, TN)


def hidden_call(h, away, dm, w1, b1, w2, first, count, before):
    tokens, width = h.shape
    hidden = w1.shape[1]
    block = UNITS
    base = first // block
    full = pl.BlockSpec((tokens, width), lambda j: (0, 0))
    half = width // 2
    place = pl.BlockSpec(memory_space=pl.ANY)
    return call(
        hidden_body,
        "hidden",
        6 * tokens * width * count,
        6 * tokens * width + 4 * tokens * count + 8 * width * count,
        grid=(count // block,),
        in_specs=[
            full,
            pl.BlockSpec((tokens, half), lambda j: (0, 0)),
            full,
            pl.BlockSpec((width, block), lambda j: (0, base + j)),
            pl.BlockSpec((1, block), lambda j: (0, base + j)),
            pl.BlockSpec((block, width), lambda j: (base + j, 0)),
        ]
        + [place] * len(before),
        out_specs=[
            pl.BlockSpec((tokens, block), lambda j: (0, base + j)),
            pl.BlockSpec((tokens, block), lambda j: (0, base + j)),
            pl.BlockSpec((1, block), lambda j: (0, base + j)),
            pl.BlockSpec((half, block), lambda j: (0, j)),
        ],
        out_shape=[
            shaped((tokens, hidden), BF16),
            shaped((tokens, hidden), BF16),
            shaped((1, hidden), F32),
            shaped((half, count), F32),
        ],
        input_output_aliases={6 + n: n for n in range(len(before))},
    )(h, away, dm, w1, b1, w2, *before)


def shard_rows(spot_ref, g_ref, grad, put):
    shards = spot_ref.shape[1]
    rows = g_ref.shape[1] // 2
    shard = g_ref.shape[1] // shards
    part = pl.program_id(0)
    place = 0
    for piece in range(2):
        made = dot(g_ref[:, piece * rows : (piece + 1) * rows], grad, TN)
        for at in range(0, rows, shard):
            put(spot_ref[part, place], made[at : at + shard])
            place += 1


def rows_send_body(side_ref, spot_ref, g_ref, dm_ref, out_ref):
    def put(spot, value):
        out_ref[spot] = value

    shard_rows(spot_ref, g_ref, dm_ref[...], put)


def rows_send_call(side, spots, g, dm):
    tokens, hidden = g.shape
    width = dm.shape[1]
    half = hidden // 2
    shards = spots.shape[1]
    return call(
        rows_send_body,
        "rows_send",
        2 * tokens * half * width,
        2 * tokens * (half + width) + 4 * half * width,
        grid_spec=pltpu.PrefetchScalarGridSpec(
            num_scalar_prefetch=2,
            grid=(width // COLUMNS,),
            in_specs=[
                pl.BlockSpec((tokens, half), lambda j, side, spots: (0, side[0])),
                pl.BlockSpec((tokens, COLUMNS), lambda j, side, spots: (0, j)),
            ],
            out_specs=pl.BlockSpec((shards, half // shards, COLUMNS), lambda j, side, spots: (0, 0, j)),
        ),
        out_shape=shaped((shards, half // shards, width), F32),
    )(side, spots, g, dm)


def rows_keep_body(side_ref, spot_ref, g_ref, dm_ref, got_ref, *outs, bounds):
    half = spot_ref.shape[1] // 2
    step = pl.program_id(0)
    for part in range(len(bounds) - 1):

        @pl.when((step >= bounds[part]) & (step < bounds[part + 1]))
        def _():
            def put(spot, value):
                value = value + got_ref[spot]

                @pl.when(spot < half)
                def _():
                    outs[2 * part + 1][jnp.minimum(spot, half - 1)] = value

                @pl.when(spot >= half)
                def _():
                    outs[2 * part][jnp.maximum(spot - half, 0)] = value

            shard_rows(spot_ref, g_ref, dm_ref[...], put)


def rows_keep_call(side, spots, g, dm, got, counts):
    tokens, hidden = g.shape
    width = dm.shape[1]
    half = hidden // 2
    steps, shards = spots.shape
    bounds = [sum(counts[:n]) for n in range(len(counts) + 1)]
    specs, shapes = [], []
    for part, count in enumerate(counts):
        for _ in range(2):
            specs.append(
                pl.BlockSpec(
                    (shards // 2, half // shards, COLUMNS),
                    functools.partial(
                        lambda j, side, spots, first, count: (0, 0, jnp.clip(j - first, 0, count - 1)),
                        first=bounds[part],
                        count=count,
                    ),
                )
            )
            shapes.append(shaped((shards // 2, half // shards, count * COLUMNS), F32))
    made = call(
        functools.partial(rows_keep_body, bounds=bounds),
        "rows_keep",
        2 * tokens * half * width,
        2 * tokens * (half + width) + 8 * half * width,
        grid_spec=pltpu.PrefetchScalarGridSpec(
            num_scalar_prefetch=2,
            grid=(steps,),
            in_specs=[
                pl.BlockSpec((tokens, half), lambda j, side, spots: (0, side[0])),
                pl.BlockSpec((tokens, COLUMNS), lambda j, side, spots: (0, j)),
                pl.BlockSpec((shards, half // shards, COLUMNS), lambda j, side, spots: (0, 0, j)),
            ],
            out_specs=specs,
        ),
        out_shape=shapes,
    )(side, spots, g, dm, got)
    made = [array.reshape(-1, array.shape[2]) for array in made]
    return list(zip(made[::2], made[1::2]))


def result_body(g_ref, w_ref, b_ref, x1_ref, mod_ref, top_ref, keep_ref, out_ref, sum_ref):
    tile = pl.program_id(0)
    branch = dot(g_ref[...], w_ref[...]) + b_ref[...]
    out_ref[...] = (x1_ref[...] + mod_ref[tile, 5:6] * keep_ref[...] * branch).astype(BF16)
    sum_ref[0] = jnp.sum(top_ref[...].astype(F32) * keep_ref[...] * branch, axis=0, keepdims=True)


def result_call(g, w, bias, x1, mod, top, keep):
    tokens, width = x1.shape
    hidden = g.shape[1]
    tiles = tokens // ROW
    rows = pl.BlockSpec((ROW, width), lambda i: (i, 0))
    return call(
        result_body,
        "result",
        2 * tokens * width * hidden,
        2 * tokens * hidden + 2 * hidden * width + 8 * tokens * width,
        grid=(tiles,),
        in_specs=[
            pl.BlockSpec((ROW, hidden), lambda i: (i, 0)),
            pl.BlockSpec((hidden, width), lambda i: (0, 0)),
            pl.BlockSpec((1, width), lambda i: (0, 0)),
            rows,
            pl.BlockSpec(mod.shape, lambda i: (0, 0, 0)),
            rows,
            pl.BlockSpec((ROW, 1), lambda i: (i, 0)),
        ],
        out_specs=[rows, pl.BlockSpec((1, 1, width), lambda i: (i, 0, 0))],
        out_shape=[shaped((tokens, width), BF16), shaped((tiles, 1, width), F32)],
    )(g, w, bias, x1, mod, top, keep)


def middle_back_body(
    df_ref, w1_ref, x1_ref, mod_ref, top_ref, a_ref, wp_ref,
    dx_ref, da_ref, do_ref, sum_ref,
):
    tile = pl.program_id(0)
    grad = dot(df_ref[...], w1_ref[...], NT)
    normal, inverse = normed(x1_ref[...])
    back = normed_back(grad * (1.0 + mod_ref[tile, 4:5]), normal, inverse)
    dx = top_ref[...].astype(F32) + back
    dx_ref[...] = dx
    da = (dx * mod_ref[tile, 2:3]).astype(BF16)
    da_ref[...] = da
    do_ref[...] = dot(wp_ref[...], da, NT).astype(BF16)
    sum_ref[0, 0:1] = jnp.sum(dx * a_ref[...], axis=0, keepdims=True)
    sum_ref[0, 1:2] = jnp.sum(grad, axis=0, keepdims=True)
    sum_ref[0, 2:3] = jnp.sum(grad * normal, axis=0, keepdims=True)
    sum_ref[0, 3:4] = jnp.sum(da.astype(F32), axis=0, keepdims=True)


def middle_back_call(df, w1, x1, mod, top, a, wp):
    tokens, width = x1.shape
    hidden = df.shape[1]
    tiles = tokens // ROW
    rows = pl.BlockSpec((ROW, width), lambda i: (i, 0))
    return call(
        middle_back_body,
        "middle_back",
        2 * tokens * width * (hidden + width),
        2 * tokens * hidden + 2 * hidden * width + 18 * tokens * width,
        grid=(tiles,),
        in_specs=[
            pl.BlockSpec((ROW, hidden), lambda i: (i, 0)),
            pl.BlockSpec((width, hidden), lambda i: (0, 0)),
            rows,
            pl.BlockSpec(mod.shape, lambda i: (0, 0, 0)),
            rows,
            rows,
            pl.BlockSpec((width, width), lambda i: (0, 0)),
        ],
        out_specs=[
            rows,
            rows,
            pl.BlockSpec((width, ROW), lambda i: (0, i)),
            pl.BlockSpec((1, 4, width), lambda i: (i, 0, 0)),
        ],
        out_shape=[
            shaped((tokens, width), F32),
            shaped((tokens, width), BF16),
            shaped((width, tokens), BF16),
            shaped((tiles, 4, width), F32),
        ],
    )(df, w1, x1, mod, top, a, wp)


class Wide:
    def __init__(self, *parts):
        self.parts = parts
        self.count = sum(rows for _, _, rows in parts)
        self.steps = 3

    def arrays(self):
        return [array for array, _, _ in self.parts]

    def specs(self, at):
        return [
            pl.BlockSpec(
                (1, rows, array.shape[2]),
                functools.partial(lambda j, at, index: (jnp.clip(j - at, 0, 2), index, 0), at=at, index=first // rows),
            )
            for array, first, rows in self.parts
        ]

    def value(self, refs):
        got = [ref[0] for ref in refs]
        return jnp.concatenate(got, axis=0) if len(got) > 1 else got[0]

    def product(self, left, right):
        return dot(left, right, TT)

    def sums(self, right):
        return dot(jnp.ones((8, right.shape[1]), BF16), right, NT)[:1]


class Plain:
    def __init__(self, array, first, count, steps):
        self.array, self.first, self.count, self.steps = array, first, count, steps

    def arrays(self):
        return [self.array]

    def specs(self, at):
        base, steps = self.first // self.count, self.steps
        index = functools.partial(
            lambda j, at, base, steps: (0, base + jnp.clip(j - at, 0, steps - 1)), at=at, base=base, steps=steps
        )
        return [pl.BlockSpec((self.array.shape[0], self.count), index)]

    def value(self, refs):
        return refs[0][...]

    def product(self, left, right):
        return dot(left, right, TN)

    def sums(self, right):
        return jnp.sum(right.astype(F32), axis=0, keepdims=True)


def columns_body(*refs, right, both):
    count = len(right.arrays())
    left_ref, right_refs, rest = refs[0], refs[1 : 1 + count], refs[1 + count :]
    value = right.value(right_refs)
    made = right.product(left_ref[...], value)
    if both:
        got_ref, send_ref, keep_ref = rest
        made = made + got_ref[...]
        rows = keep_ref.shape[0]
        send_ref[...] = made[rows:]
        keep_ref[...] = made[:rows]
    else:
        send_ref, sum_ref = rest
        send_ref[...] = made
        sum_ref[...] = right.sums(value)


def columns_call(left, right, name, got=None):
    tokens, half = left.shape
    count = right.count * right.steps
    both = got is not None
    wide = pl.BlockSpec((half, right.count), lambda j: (0, j))
    narrow = pl.BlockSpec((half // 2, right.count), lambda j: (0, j))
    made = call(
        functools.partial(columns_body, right=right, both=both),
        name,
        2 * tokens * half * count,
        2 * tokens * (count + half) + 8 * half * count,
        grid=(right.steps,),
        in_specs=[pl.BlockSpec(left.shape, lambda j: (0, 0)), *right.specs(0)] + [wide] * both,
        out_specs=[narrow, narrow] if both else [wide, pl.BlockSpec((1, right.count), lambda j: (0, j))],
        out_shape=[shaped((half // 2, count), F32)] * 2
        if both
        else [shaped((half, count), F32), shaped((1, count), F32)],
    )(left, *right.arrays(), *([got] if both else []))
    return [tuple(made)] if both else made


def pair_body(*refs, rights, both):
    counts = [len(right.arrays()) for right in rights]
    step = pl.program_id(0)
    at = 0
    rest = refs[2 + sum(counts) :]
    for number, (right, count) in enumerate(zip(rights, counts)):
        mine = (refs[at], *refs[at + 1 : at + 1 + count], *rest)
        when = step < rights[0].steps if number == 0 else step >= rights[0].steps
        pl.when(when)(functools.partial(columns_body, *mine, right=right, both=both))
        at += 1 + count


def pair_call(lefts, rights, name, got=None):
    tokens, half = lefts[0].shape
    step = rights[0].count
    steps = sum(right.steps for right in rights)
    count = step * steps
    both = got is not None
    wide = pl.BlockSpec((half, step), lambda j: (0, j))
    narrow = pl.BlockSpec((half // 2, step), lambda j: (0, j))
    operands, specs, at = [], [], 0
    for left, right in zip(lefts, rights):
        operands += [left, *right.arrays()]
        specs += [pl.BlockSpec(left.shape, lambda j: (0, 0)), *right.specs(at)]
        at += right.steps
    made = call(
        functools.partial(pair_body, rights=rights, both=both),
        name,
        2 * tokens * half * count,
        2 * tokens * (count + half) + 8 * half * count,
        grid=(steps,),
        in_specs=specs + [wide] * both,
        out_specs=[narrow, narrow] if both else [wide, pl.BlockSpec((1, step), lambda j: (0, j))],
        out_shape=[shaped((half // 2, count), F32)] * 2
        if both
        else [shaped((half, count), F32), shaped((1, count), F32)],
    )(*operands, *([got] if both else []))
    return [tuple(made)] if both else made


def moved_body(om_ref, h_ref, away_ref, own_ref, *out_refs):
    om, hidden = om_ref[...], h_ref[...]
    out_refs[0][...] = dot(om, away_ref[...], TN).astype(BF16)
    out_refs[1][...] = dot(om, own_ref[...], TN).astype(BF16)
    out_refs[2][...] = dot(hidden, away_ref[...]).astype(BF16)
    out_refs[3][...] = dot(hidden, own_ref[...]).astype(BF16)


def moved_call(om, hidden, away, own):
    tokens, width = hidden.shape
    half = width // 2
    block = tokens // 2
    fixed = pl.BlockSpec((width, half), lambda i: (0, 0))
    out = pl.BlockSpec((block, half), lambda i: (i, 0))
    return call(
        moved_body,
        "moved",
        4 * tokens * width * width,
        8 * tokens * width + 2 * width * width,
        grid=(2,),
        in_specs=[
            pl.BlockSpec((width, block), lambda i: (0, i)),
            pl.BlockSpec((block, width), lambda i: (i, 0)),
            fixed,
            fixed,
        ],
        out_specs=[out] * 4,
        out_shape=[shaped((tokens, half), BF16)] * 4,
    )(om, hidden, away, own)


def first_back_body(low_ref, high_ref, w_ref, x_ref, mod_ref, dx_ref, out_ref, sum_ref):
    tile = pl.program_id(0)
    width = x_ref.shape[1]
    grad = None
    for third in range(3):
        rows = jnp.concatenate([low_ref[third], high_ref[third]], axis=0)
        part = dot(rows, w_ref[:, third * width : (third + 1) * width], TT)
        grad = part if grad is None else grad + part
    normal, inverse = normed(x_ref[...].astype(F32))
    out_ref[...] = dx_ref[...] + normed_back(grad * (1.0 + mod_ref[tile, 1:2]), normal, inverse)
    sum_ref[0, 0:1] = jnp.sum(grad, axis=0, keepdims=True)
    sum_ref[0, 1:2] = jnp.sum(grad * normal, axis=0, keepdims=True)


def first_back_call(low, high, w, x, mod, dx):
    tokens, width = x.shape
    wide = w.shape[1]
    half = pl.BlockSpec((3, width // 2, ROW), lambda i: (0, 0, i))
    tiles = tokens // ROW
    rows = pl.BlockSpec((ROW, width), lambda i: (i, 0))
    return call(
        first_back_body,
        "first_back",
        2 * tokens * width * wide,
        2 * tokens * wide + 2 * width * wide + 10 * tokens * width,
        grid=(tiles,),
        in_specs=[
            half,
            half,
            pl.BlockSpec((width, wide), lambda i: (0, 0)),
            rows,
            pl.BlockSpec(mod.shape, lambda i: (0, 0, 0)),
            rows,
        ],
        out_specs=[rows, pl.BlockSpec((1, 2, width), lambda i: (i, 0, 0))],
        out_shape=[shaped((tokens, width), F32), shaped((tiles, 2, width), F32)],
    )(low, high, w, x, mod, dx)


def modulation_back_body(me_ref, *refs, count):
    part_refs, cond_refs, sum_refs = refs[:count], refs[count : 2 * count], refs[2 * count : 3 * count]
    label_ref, w_ref, grad_ref, bias_ref, table_ref, own_sums_ref, act_ref, own_ref, total_ref = refs[3 * count :]
    step = pl.program_id(0)
    width = act_ref.shape[1]
    shard = grad_ref.shape[0]
    items = own_sums_ref.shape[0]

    @pl.when(step == 0)
    def _():
        at = 0
        for cond_ref in cond_refs:
            cond = cond_ref[...]
            act_ref[at : at + cond.shape[0]] = (cond / (1.0 + jnp.exp(-cond))).astype(BF16)
            at += cond.shape[0]
        row = lax.broadcasted_iota(jnp.int32, (width, 128), 0)
        column = lax.broadcasted_iota(jnp.int32, (width, 128), 1)
        picked = jnp.where((column < shard) & (row == me_ref[0] * shard + column), 1.0, 0.0).astype(BF16)
        own_ref[...] = dot(act_ref[...], picked).astype(BF16)
        total_ref[...] = jnp.zeros_like(total_ref)
        sums = None
        for sum_ref in sum_refs:
            rows = sum_ref.shape[0]
            item = lax.broadcasted_iota(jnp.int32, (items, rows), 0)
            source = lax.broadcasted_iota(jnp.int32, (items, rows), 1)
            select = (lax.rem(source, jnp.full_like(source, items)) == item).astype(F32)
            part = dot(select, sum_ref[...], NN, HIGHEST)
            sums = part if sums is None else sums + part
        own_sums_ref[...] = sums

    mod = jnp.concatenate([part_ref[...] for part_ref in part_refs], axis=0)
    bias_ref[...] = jnp.sum(mod, axis=0, keepdims=True)
    mod = mod.astype(BF16)
    grad_ref[...] = dot(own_ref[...], mod, TN)[:shard]
    total_ref[...] += dot(w_ref[...], mod, NT)

    @pl.when(step == pl.num_programs(0) - 1)
    def _():
        cond = jnp.concatenate([cond_ref[...] for cond_ref in cond_refs], axis=0)
        gate = 1.0 / (1.0 + jnp.exp(-cond))
        grad = total_ref[...].T * (gate * (1.0 + cond * (1.0 - gate)))
        classes = table_ref.shape[0]
        select = (label_ref[...] == lax.broadcasted_iota(jnp.int32, (grad.shape[0], classes), 1)).astype(F32)
        table_ref[...] = dot(select, grad, TN, HIGHEST)


def modulation_back_call(me, parts, used, w, classes, shard, items):
    width, wide = w.shape
    block = 1152
    rows = sum(part.shape[0] for part in parts)
    extra = parts[0].shape[1] - wide - width
    at = (wide + extra) // width
    return call(
        functools.partial(modulation_back_body, count=len(parts)),
        "modulation_back",
        4 * rows * width * wide,
        2 * width * wide,
        grid=(wide // block,),
        in_specs=[
            pl.BlockSpec(memory_space=pltpu.SMEM),
            *[pl.BlockSpec((part.shape[0], block), lambda j: (0, j)) for part in parts],
            *[pl.BlockSpec((part.shape[0], width), lambda j: (0, at)) for part in parts],
            *[pl.BlockSpec((part.shape[0], extra), lambda j: (0, wide // extra)) for part in parts],
            pl.BlockSpec(used.shape, lambda j: (0, 0)),
            pl.BlockSpec((width, block), lambda j: (0, j)),
        ],
        out_specs=[
            pl.BlockSpec((shard, block), lambda j: (0, j)),
            pl.BlockSpec((1, block), lambda j: (0, j)),
            pl.BlockSpec((classes, width), lambda j: (0, 0)),
            pl.BlockSpec((items, extra), lambda j: (0, 0)),
        ],
        out_shape=[
            shaped((shard, wide), F32),
            shaped((1, wide), F32),
            shaped((classes, width), F32),
            shaped((items, extra), F32),
        ],
        scratch_shapes=[
            pltpu.VMEM((rows, width), BF16),
            pltpu.VMEM((rows, 128), BF16),
            pltpu.VMEM((width, rows), F32),
        ],
    )(me, *parts, *parts, *parts, used, w)


def add_body(*refs, plans):
    outs = refs[-len(plans) :]
    at = 0
    for out_ref, (count, first, rows) in zip(outs, plans):
        value = refs[at][first : first + rows]
        for term in range(1, count):
            value = value + refs[at + term][first : first + rows]
        out_ref[...] = value
        at += count


def add_call(jobs):
    steps = 3 if all(terms[0].shape[1] % 384 == 0 for terms, _, _ in jobs) else 2
    if any(terms[0].shape[1] % (128 * steps) for terms, _, _ in jobs):
        steps = 1
    operands, specs, outs, shapes, plans = [], [], [], [], []
    moved = 0
    for terms, first, rows in jobs:
        wide = terms[0].shape[1]
        block = wide // steps
        for term in terms:
            size, index, at = rows, first // rows, 0
            while size % 8 and size < term.shape[0]:
                size, index, at = size * 2, 0, first
            operands.append(term)
            specs.append(pl.BlockSpec((size, block), functools.partial(lambda j, index: (index, j), index=index)))
        plans.append((len(terms), at, rows))
        outs.append(pl.BlockSpec((rows, block), lambda j: (0, j)))
        shapes.append(shaped((rows, wide), F32))
        moved += 4 * rows * wide * (len(terms) + 1)
    return call(
        functools.partial(add_body, plans=plans),
        "add",
        moved // 4,
        moved,
        grid=(steps,),
        in_specs=specs,
        out_specs=outs,
        out_shape=shapes,
    )(*operands)


def assemble_body(*refs, plans):
    outs = refs[-len(plans) :]
    for out_ref, (rows, blocks) in zip(outs, plans):
        for terms, source, target, count in blocks:
            value = refs[terms[0]][:rows, source : source + count]
            for term in terms[1:]:
                value = value + refs[term][:rows, source : source + count]
            out_ref[:, target : target + count] = value


def assemble_call(outputs):
    operands, specs, known, plans, shapes = [], [], {}, [], []
    for blocks in outputs:
        rows, target, made = blocks[0][0].rows, 0, []
        for chunk, source, count in blocks:
            if id(chunk) not in known:
                known[id(chunk)] = []
                for term in chunk.terms:
                    size = rows
                    while size % 8 and size < term.shape[0]:
                        size *= 2
                    known[id(chunk)].append(len(operands))
                    operands.append(term)
                    specs.append(pl.BlockSpec((size, term.shape[1]), lambda j: (0, 0)))
            made.append((known[id(chunk)], source, target, count))
            target += count
        plans.append((rows, made))
        shapes.append(shaped((rows, target), F32))
    return call(
        functools.partial(assemble_body, plans=plans),
        "assemble",
        0,
        sum(8 * 4 * shape.shape[0] * shape.shape[1] for shape in shapes),
        grid=(1,),
        in_specs=specs,
        out_specs=[pl.BlockSpec(shape.shape, lambda j: (0, 0)) for shape in shapes],
        out_shape=shapes,
    )(*operands)


def bit_order(bits, core, lead):
    order = list(range(bits))
    if bits >= 2 and core:
        order[:2] = [1, 0]
    if lead and lead < bits:
        order.remove(lead)
        order.insert(0, lead)
    return order


class Chunk:
    def __init__(self, send, kept, wait, lead):
        self.send, self.terms, self.wait, self.lead = send, [kept], wait, lead
        self.rows = kept.shape[0]
        self.stage = 0


class Spread:
    def __init__(self, rows):
        self.own, self.other = [rows], None
        self.stage = 0


class Flow:
    def __init__(self, bits):
        self.bits = bits
        self.fresh, self.crossing, self.chunks, self.last = [], [], [], []
        self.blocks = ([], [], [])
        self.spreads = []

    def emit(self, send, keep, store, waits=(0,), leads=(0,)):
        self.fresh.append((send, keep, store, waits, leads))

    def spread(self, rows):
        self.spreads.append(Spread(rows))
        return self.spreads[-1]

    def busy(self):
        moving = self.fresh or self.crossing or any(chunk.stage < self.bits for chunk in self.chunks)
        return moving or any(spread.stage <= self.bits for spread in self.spreads)

    def pairs(self, stage, lead):
        size = 1 << self.bits
        flips = [1 << bit_order(self.bits, core, lead)[stage] for core in range(2)]
        return [(core * size + i, core * size + (i ^ flips[core])) for core in range(2) for i in range(size)]

    def received(self, live):
        live, (cores, blocks, doubles) = lax.optimization_barrier((live, self.blocks))
        for spread, block in zip([spread for spread in self.spreads if spread.other is None and spread.stage], doubles):
            if spread.stage > self.bits:
                spread.other = block
            elif spread.stage == self.bits:
                spread.own += block
            else:
                spread.own = [jnp.concatenate(spread.own + block, axis=0)]
        jobs, waiting = [], []
        for chunk, block in zip(self.last, blocks):
            chunk.terms.append(block)
            if chunk.stage < self.bits:
                chunk.rows //= 2
                jobs.append((chunk.terms, chunk.rows, chunk.rows))
                waiting.append(chunk)
        for (_, keep, store, waits, leads), core in zip(self.crossing, cores):
            new = [Chunk(*pair, wait, lead) for pair, wait, lead in zip(keep(core), waits, leads)]
            store += new
            self.chunks += new
        for chunk, value in zip(waiting, add_call(jobs) if jobs else []):
            chunk.send = value
        return live

    def round(self, live):
        live = self.received(live)
        moving = [chunk for chunk in self.chunks if chunk.stage < self.bits and not chunk.wait]
        for chunk in self.chunks:
            chunk.wait = max(0, chunk.wait - 1)
        crossing, self.fresh = self.fresh, []
        doubling = [spread for spread in self.spreads if spread.stage <= self.bits]
        live, cores, sends, doubles = lax.optimization_barrier(
            (
                live,
                [entry[0] for entry in crossing],
                [chunk.send for chunk in moving],
                [spread.own for spread in doubling],
            )
        )
        blocks = []
        for chunk, send in zip(moving, sends):
            blocks.append(lax.ppermute(send, ("stream", "batch"), self.pairs(chunk.stage, chunk.lead)))
            chunk.stage += 1
        cores = [lax.ppermute(send, "stream", [(0, 1), (1, 0)]) for send in cores]
        for number, (spread, rows) in enumerate(zip(doubling, doubles)):
            spread.own = rows
            if spread.stage < self.bits:
                pairs = self.pairs(self.bits - 1 - spread.stage, 0)
                doubles[number] = [lax.ppermute(piece, ("stream", "batch"), pairs) for piece in rows]
            else:
                doubles[number] = [lax.ppermute(piece, "stream", [(0, 1), (1, 0)]) for piece in rows]
            spread.stage += 1
        self.crossing, self.last, self.blocks = crossing, moving, (cores, blocks, doubles)
        return live


def offsets_of(bits, side, lead):
    places = jnp.arange(1 << bits, dtype=jnp.int32)
    made = []
    for core in range(2):
        offset = jnp.zeros_like(places)
        for stage, bit in enumerate(bit_order(bits, core, lead)):
            offset = offset | (((places >> (bits - 1 - stage)) & 1) << bit)
        made.append(offset)
    return jnp.where(side == 0, made[0], made[1])


def places_of(bits, side, lead, offset):
    made = []
    for core in range(2):
        place = jnp.zeros_like(offset)
        for stage, bit in enumerate(bit_order(bits, core, lead)):
            place = place | (((offset >> bit) & 1) << (bits - 1 - stage))
        made.append(place)
    return jnp.where(side == 0, made[0], made[1])


def time_embed(steps_in, width):
    half_width = width // 2
    frequency = jnp.exp(-math.log(10000.0) * jnp.arange(half_width, dtype=F32) / half_width)
    angles = steps_in.astype(F32)[:, None] * frequency[None, :]
    return jnp.concatenate([jnp.cos(angles), jnp.sin(angles)], axis=1)


def per_device(
    tokens, segments, timesteps, labels, head_keep, token_keep, class_table, w_ada, b_ada,
    w_qkv, b_qv, w_proj, b_proj, w_fc1, b_fc1, w_fc2, b_fc2, out_grad, *, batch,
):
    x, top = tokens[0], out_grad[0]
    count, width = x.shape
    hidden = w_fc1.shape[1]
    heads = head_keep.shape[1]
    items = timesteps.shape[0]
    tiles = count // ROW
    groups = count // GROUP
    null_class = class_table.shape[0] - 1
    bits = batch.bit_length() - 1
    devices = 2 * batch
    stream = lax.axis_index("stream")
    index = lax.axis_index("batch")

    own_labels = lax.dynamic_slice_in_dim(labels, index * items, items)
    used = jnp.where(stream == 0, own_labels, null_class)
    cond = time_embed(timesteps, width) + jnp.take(class_table, used, axis=0).astype(F32)
    act = jax.nn.silu(cond).astype(BF16)
    modulation = dot(act, w_ada) + b_ada
    tile_item = segments[::ROW] - index * items
    chosen = tile_item[:, None] == jnp.arange(items, dtype=jnp.int32)[None, :]
    mod = jnp.sum(jnp.where(chosen[:, :, None], modulation[None], 0.0), axis=1)
    mod = mod.reshape(tiles, 6, width)
    tile_heads = jnp.sum(jnp.where(chosen[:, :, None], head_keep[None], 0), axis=1).astype(F32)
    head_columns = jnp.repeat(tile_heads.T, ROW, axis=1).reshape(heads, 1, count)
    keep = token_keep[0].astype(F32)[:, None]
    grouped = segments.reshape(groups, GROUP)
    flag = (grouped[:, 0] == grouped[:, -1]).astype(jnp.int32)

    shard = width // devices

    def picked(side):
        order = side * batch + (index ^ offsets_of(bits, side, 0))
        source = (order[:, None] * shard + jnp.arange(shard, dtype=jnp.int32)[None, :]).reshape(width // 2)
        return (jnp.arange(width, dtype=jnp.int32)[:, None] == source[None, :]).astype(BF16)

    def spots(side):
        return jnp.stack([places_of(bits, side, lead, jnp.arange(batch, dtype=jnp.int32) ^ index) for steps, lead in ROW_PARTS for _ in range(steps)])

    other = 1 - stream
    away, own = picked(other), picked(stream)

    bias_full = jnp.concatenate([b_qv[:width], jnp.zeros((width,), F32), b_qv[width:]])[:, None]
    h1, qkv = qkv_call(x, mod, w_qkv, bias_full)
    probs, mixed, om = attention_call(flag, qkv, head_columns, heads)
    a, x1, h2, h2_away, h2_own, dm, sum_dm = middle_call(om, w_proj, b_proj[None], x, mod, top, keep, away, own)

    flow = Flow(bits)
    fc1, fc2, wide = [], [], []

    filled, latest = (), {}
    for low, high in ((0, 2 * UNITS), (2 * UNITS, 5 * UNITS), (5 * UNITS, hidden)):
        *filled, send = hidden_call(h2, h2_away, dm, w_fc1, b_fc1[None], w_fc2, low, high - low, filled)
        latest["df"] = filled[1]

        def hidden_keep(got, low=low, count=high - low):
            return columns_call(h2_own, Plain(latest["df"], low, UNITS, count // UNITS), "hidden_keep", got)

        flow.emit(send, hidden_keep, fc1)
        h2, filled = flow.round((h2, filled))
        latest["df"] = filled[1]
    g, df, sum_df = filled

    rows_send = rows_send_call(other[None], spots(other), g, dm)
    flow.emit(
        rows_send.reshape(-1, width),
        lambda got: rows_keep_call(
            stream[None], spots(stream), g, dm, got.reshape(rows_send.shape), [steps for steps, _ in ROW_PARTS]
        ),
        fc2,
        [0] * len(ROW_PARTS),
        [lead for _, lead in ROW_PARTS],
    )
    om_away, om_own, h1_away, h1_own = moved_call(om, h1, away, own)
    df, x1, om_away, om_own, h1_away, h1_own = flow.round((df, x1, om_away, om_own, h1_away, h1_own))
    dx1, da, do, sums_two = middle_back_call(df, w_fc1, x1, mod, top, a, w_proj)

    def by_item(*sums):
        by_tile = jnp.concatenate(sums, axis=1)
        return jnp.sum(jnp.where(chosen[:, :, None], by_tile[:, None], 0.0), axis=0).astype(BF16).astype(F32)

    def in_rows(*sums):
        made = jnp.concatenate([part.reshape(devices, -1) for part in sums], axis=1).reshape(items, -1)
        return jnp.pad(made, ((0, 0), (0, -made.shape[1] % 128)))

    me = stream * batch + index

    def used_labels(side):
        order = bit_order(bits, 0, 0)[::-1], bit_order(bits, 1, 0)[::-1]
        places = jnp.arange(batch, dtype=jnp.int32)
        offsets = [sum(((places >> n) & 1) << bit for n, bit in enumerate(bits_of)) for bits_of in order]
        from_device = index ^ jnp.where(side == 0, offsets[0], offsets[1])
        return jnp.where(side == 0, jnp.take(labels.reshape(batch, items), from_device, axis=0).reshape(-1), null_class)

    used_rows = jnp.concatenate([used_labels(stream), used_labels(other)])[:, None]
    dx1, da, do, sums_two = flow.round((dx1, da, do, sums_two))
    half = width // 2
    low = attention_back_call(flag, qkv, do, head_columns, probs, mixed, 0)
    rights = [Plain(da, 0, COLUMNS, width // COLUMNS), Wide((low, 0, COLUMNS))]
    send, first_sums = pair_call([om_away, h1_away], rights, "first_send")
    flow.emit(send, lambda got: pair_call([om_own, h1_own], rights, "first_keep", got), wide)
    low, first_sums = flow.round((low, first_sums))
    high = attention_back_call(flag, qkv, do, head_columns, probs, mixed, 1)
    rest = Wide((low, COLUMNS, half - COLUMNS), (high, 0, half))
    send, high_sums = columns_call(h1_away, rest, "last_send")
    flow.emit(send, lambda got: columns_call(h1_own, rest, "last_keep", got), wide)
    low, high, dx1, high_sums, g = flow.round((low, high, dx1, high_sums, g))
    grad_tokens, sums_one = first_back_call(low, high, w_qkv, x, mod, dx1)
    result, sum_gate = result_call(g, w_fc2, b_fc2[None], x1, mod, top, keep)

    def in_order(low, high):
        first, second = low.shape[1] // 3, high.shape[1] // 3
        return [
            part
            for third in range(3)
            for part in (low[:, third * first : (third + 1) * first], high[:, third * second : (third + 1) * second])
        ]

    grad_tokens, sums_one, result, sum_gate = flow.round((grad_tokens, sums_one, result, sum_gate))
    column_sums = in_order(first_sums[:, width:], high_sums)
    spread = flow.spread(
        jnp.concatenate(
            [
                by_item(
                    sums_one[:, 0], sums_one[:, 1], sums_two[:, 0], sums_two[:, 1], sums_two[:, 2], sum_gate[:, 0]
                ),
                in_rows(
                    sum_df[0],
                    jnp.sum(sum_dm, axis=(0, 1)),
                    jnp.sum(sums_two[:, 3], axis=0),
                    jnp.concatenate(column_sums[:2] + column_sums[4:], axis=1)[0],
                ),
                cond,
            ],
            axis=1,
        )
    )
    while any(chunk.stage < bits for chunk in fc1 + fc2):
        result = flow.round(result)
    result = flow.round(result)
    grad_w_fc1, grad_w_fc2 = assemble_call(
        [[(chunk, 0, chunk.terms[0].shape[1]) for chunk in store] for store in (fc1, fc2)]
    )
    result, grad_w_fc1, grad_w_fc2 = flow.round((result, grad_w_fc1, grad_w_fc2))
    while any(chunk.stage < bits for chunk in wide):
        result = flow.round(result)
    result = flow.round(result) if flow.busy() else flow.received(result)
    first, last = wide
    each = COLUMNS, width - COLUMNS
    blocks = [
        block
        for third in range(3)
        for block in ((first, width + third * each[0], each[0]), (last, third * each[1], each[1]))
    ]
    grad_w_proj, grad_w_qkv = assemble_call([[(first, 0, width)], blocks])
    while flow.busy():
        result = flow.round(result)
    result, grad_w_proj = flow.received((result, grad_w_proj))
    grad_w_ada, mod_sums, grad_table, own_sums = modulation_back_call(
        me[None], spread.own + spread.other, used_rows, w_ada, null_class + 1, shard, items
    )
    share = 6 * width // devices
    grad_b_ada = lax.dynamic_slice_in_dim(mod_sums[0], me * share, share)
    ends = [hidden // devices, width // devices, width // devices, 2 * width // devices]
    each = devices // items
    bias = lax.dynamic_slice(own_sums, (me // each, me % each * sum(ends)), (1, sum(ends)))[0]
    at = [sum(ends[:n]) for n in range(5)]
    grad_b_fc1, grad_b_fc2, grad_b_proj, grad_b_qv = [bias[at[n] : at[n + 1]] for n in range(4)]

    return (
        result[None],
        grad_tokens[None],
        grad_table,
        grad_w_ada,
        grad_b_ada,
        grad_w_qkv,
        grad_b_qv,
        grad_w_proj,
        grad_b_proj,
        grad_w_fc1,
        grad_b_fc1,
        grad_w_fc2,
        grad_b_fc2,
    )


def solution(mesh):
    both = ("stream", "batch")
    return jax.shard_map(
        functools.partial(per_device, batch=mesh.shape["batch"]),
        mesh=mesh,
        in_specs=(
            P("stream", "batch", None),
            P("batch"),
            P("batch"),
            P(),
            P("batch", None),
            P("stream", "batch"),
            P(), P(), P(), P(), P(), P(), P(), P(), P(), P(), P(),
            P("stream", "batch", None),
        ),
        out_specs=(
            P("stream", "batch", None),
            P("stream", "batch", None),
            P(),
            P(both, None),
            P(both),
            P(both, None),
            P(both),
            P(both, None),
            P(both),
            P(both, None),
            P(both),
            P(both, None),
            P(both),
        ),
        check_vma=False,
    )
```

```python
import functools
import math

import jax
import jax.numpy as jnp
from jax import lax
from jax.experimental import pallas as pl
from jax.experimental.pallas import tpu as pltpu
from jax.sharding import PartitionSpec as P

F32 = jnp.float32
BF16 = jnp.bfloat16
HIGHEST = lax.Precision.HIGHEST
NORM_EPS = 1e-06
ROW_PARTS = ((2, 0), (1, 2))
ROW = 256
GROUP = 1024
NN = (((1,), (0,)), ((), ()))
NT = (((1,), (1,)), ((), ()))
TN = (((0,), (0,)), ((), ()))
TT = (((0,), (1,)), ((), ()))
VMEM_LIMIT = 60 << 20
COLUMNS = 384
UNITS = 512


def dot(left, right, dims=NN, precision=None):
    return lax.dot_general(left, right, dims, precision=precision, preferred_element_type=F32)


def call(body, name, flops, moved, **kwargs):
    return pl.pallas_call(
        body,
        name=name,
        compiler_params=pltpu.CompilerParams(vmem_limit_bytes=VMEM_LIMIT),
        cost_estimate=pl.CostEstimate(flops=flops // 8, bytes_accessed=moved // 8, transcendentals=0),
        **kwargs,
    )


def shaped(shape, kind):
    return jax.ShapeDtypeStruct(shape, kind)


def normed(values):
    centre = values - jnp.mean(values, axis=-1, keepdims=True)
    spread = jnp.mean(centre * centre, axis=-1, keepdims=True)
    inverse = lax.rsqrt(spread + NORM_EPS)
    return centre * inverse, inverse


def normed_back(grad, normal, inverse):
    first = jnp.mean(grad, axis=-1, keepdims=True)
    second = jnp.mean(grad * normal, axis=-1, keepdims=True)
    return inverse * (grad - first - normal * second)


def qkv_body(x_ref, mod_ref, w_ref, b_ref, h_ref, out_ref):
    @pl.when(pl.program_id(0) == 0)
    def _():
        for tile in range(x_ref.shape[0] // ROW):
            rows = slice(tile * ROW, tile * ROW + ROW)
            normal, _ = normed(x_ref[rows].astype(F32))
            h_ref[rows] = (normal * (1.0 + mod_ref[tile, 1:2]) + mod_ref[tile, 0:1]).astype(BF16)

    out_ref[...] = (dot(w_ref[...], h_ref[...], TT) + b_ref[...]).astype(BF16)


def qkv_call(x, mod, w, bias):
    tokens, width = x.shape
    wide = w.shape[1]
    block = width
    return call(
        qkv_body,
        "qkv",
        2 * tokens * width * wide,
        2 * (2 * tokens * width + width * wide + tokens * wide),
        grid=(wide // block,),
        in_specs=[
            pl.BlockSpec((tokens, width), lambda j: (0, 0)),
            pl.BlockSpec(mod.shape, lambda j: (0, 0, 0)),
            pl.BlockSpec((width, block), lambda j: (0, j)),
            pl.BlockSpec((block, 1), lambda j: (j, 0)),
        ],
        out_specs=[
            pl.BlockSpec((tokens, width), lambda j: (0, 0)),
            pl.BlockSpec((block, tokens), lambda j: (j, 0)),
        ],
        out_shape=[shaped((tokens, width), BF16), shaped((wide, tokens), BF16)],
    )(x, mod, w, bias)


def heads_of(ref, head_width):
    values = ref[...].astype(F32)
    return [values[head * head_width : (head + 1) * head_width] for head in range(2)]


def attention_body(flag_ref, q_ref, k_ref, v_ref, keep_ref, p_ref, ot_ref, om_ref):
    head_width = ot_ref.shape[1]
    scale = math.log2(math.e) / math.sqrt(head_width)
    tokens = q_ref.shape[1]
    q, k = [[part.astype(BF16) for part in heads_of(ref, head_width)] for ref in (q_ref, k_ref)]
    v = [jnp.concatenate([part, jnp.ones((8, tokens), F32)], axis=0).astype(BF16) for part in heads_of(v_ref, head_width)]

    def part(head, first, count):
        rows = slice(first, first + count)
        scores = dot(k[head][:, rows], q[head][:, rows], TN)
        top = jnp.max(scores, axis=0, keepdims=True)
        expo = jnp.exp2((scores - top) * scale)
        total = jnp.sum(expo, axis=0, keepdims=True)
        probs = (expo * (1.0 / total)).astype(BF16)
        p_ref[head, rows, rows] = probs
        mixed = dot(v[head][:, rows], probs)
        ot_ref[head, :, rows] = mixed[:head_width] * (1.0 / mixed[head_width : head_width + 1])
        return mixed[:head_width] * keep_ref[head, :, rows]

    def run(count):
        made = [
            jnp.concatenate([part(head, at, count) for at in range(0, tokens, count)], axis=1) for head in range(2)
        ]
        om_ref[...] = jnp.concatenate(made, axis=0).astype(BF16)

    whole = flag_ref[pl.program_id(0)] == 1
    pl.when(whole)(lambda: run(tokens))
    pl.when(jnp.logical_not(whole))(lambda: run(ROW))


def attention_call(flag, qkv, keep, heads):
    wide, tokens = qkv.shape
    width = wide // 3
    head_width = width // heads
    groups = tokens // GROUP
    pairs = heads // 2
    rows = 2 * head_width

    def third(number):
        return pl.BlockSpec((rows, GROUP), functools.partial(lambda g, h, base: (base + h, g), base=number * pairs))

    return call(
        attention_body,
        "attention",
        2 * 2 * heads * tokens * GROUP * 256,
        2 * tokens * wide + 2 * heads * tokens * GROUP + 6 * tokens * width,
        grid=(groups, pairs),
        in_specs=[
            pl.BlockSpec(memory_space=pltpu.SMEM),
            third(0),
            third(1),
            third(2),
            pl.BlockSpec((2, 1, GROUP), lambda g, h: (h, 0, g)),
        ],
        out_specs=[
            pl.BlockSpec((2, GROUP, GROUP), lambda g, h: (h, 0, g)),
            pl.BlockSpec((2, head_width, GROUP), lambda g, h: (h, 0, g)),
            third(0),
        ],
        out_shape=[
            shaped((heads, GROUP, tokens), BF16),
            shaped((heads, head_width, tokens), F32),
            shaped((width, tokens), BF16),
        ],
    )(flag, qkv, qkv, qkv, keep)


def attention_back_body(flag_ref, q_ref, k_ref, v_ref, do_ref, keep_ref, p_ref, ot_ref, out_ref, ds_ref):
    head_width = ot_ref.shape[1]
    scale = 1.0 / math.sqrt(head_width)
    tokens = q_ref.shape[1]
    q, k, v = [[part.astype(BF16) for part in heads_of(ref, head_width)] for ref in (q_ref, k_ref, v_ref)]
    kept = [part * keep_ref[head] for head, part in enumerate(heads_of(do_ref, head_width))]
    do = [part.astype(BF16) for part in kept]
    delta = [jnp.sum(kept[head] * ot_ref[head], axis=0, keepdims=True) for head in range(2)]

    def run(count):
        made = [[], [], []]
        for head in range(2):
            row = [[], [], []]
            for first in range(0, tokens, count):
                rows = slice(first, first + count)
                dp = dot(v[head][:, rows], do[head][:, rows], TN)
                probs = p_ref[head, rows, rows].astype(F32)
                ds = (probs * (dp - delta[head][:, rows])).astype(BF16)
                if count == tokens:
                    ds_ref[head] = ds
                    ds = ds_ref[head]
                row[0].append(dot(k[head][:, rows], ds) * scale)
                row[1].append(dot(q[head][:, rows], ds, NT) * scale)
                row[2].append(dot(do[head][:, rows], p_ref[head, rows, rows], NT))
            for third in range(3):
                made[third].append(jnp.concatenate(row[third], axis=1))
        for third in range(3):
            out_ref[third] = jnp.concatenate(made[third], axis=0).astype(BF16)

    whole = flag_ref[pl.program_id(0)] == 1
    pl.when(whole)(lambda: run(tokens))
    pl.when(jnp.logical_not(whole))(lambda: run(ROW))


def attention_back_call(flag, qkv, do, keep, probs, mixed, part):
    wide, tokens = qkv.shape
    width = wide // 3
    heads, head_width = mixed.shape[:2]
    groups = tokens // GROUP
    pairs = heads // 4
    base = part * pairs
    rows = 2 * head_width

    def third(number):
        first = number * heads // 2 + base
        return pl.BlockSpec((rows, GROUP), functools.partial(lambda g, h, first: (first + h, g), first=first))

    return call(
        attention_back_body,
        "attention_back",
        2 * 2 * heads * tokens * GROUP * 256,
        2 * tokens * wide + heads * tokens * GROUP + 6 * tokens * width,
        grid=(groups, pairs),
        in_specs=[
            pl.BlockSpec(memory_space=pltpu.SMEM),
            third(0),
            third(1),
            third(2),
            third(0),
            pl.BlockSpec((2, 1, GROUP), lambda g, h: (base + h, 0, g)),
            pl.BlockSpec((2, GROUP, GROUP), lambda g, h: (base + h, 0, g)),
            pl.BlockSpec((2, head_width, GROUP), lambda g, h: (base + h, 0, g)),
        ],
        out_specs=pl.BlockSpec((3, rows, GROUP), lambda g, h: (0, h, g)),
        out_shape=shaped((3, width // 2, tokens), BF16),
        scratch_shapes=[pltpu.VMEM((2, GROUP, GROUP), BF16)],
    )(flag, qkv, qkv, qkv, do, keep, probs, mixed)


def middle_body(
    om_ref, w_ref, b_ref, x_ref, mod_ref, top_ref, keep_ref, away_ref, own_ref,
    a_ref, x1_ref, h_ref, h_away_ref, h_own_ref, dm_ref, sum_ref,
):
    tile = pl.program_id(0)
    branch = dot(om_ref[...], w_ref[...], TN) + b_ref[...]
    a_ref[...] = branch
    middle = x_ref[...].astype(F32) + mod_ref[tile, 2:3] * branch
    x1_ref[...] = middle
    normal, _ = normed(middle)
    hidden = (normal * (1.0 + mod_ref[tile, 4:5]) + mod_ref[tile, 3:4]).astype(BF16)
    h_ref[...] = hidden
    h_away_ref[...] = dot(hidden, away_ref[...]).astype(BF16)
    h_own_ref[...] = dot(hidden, own_ref[...]).astype(BF16)
    grad = (top_ref[...].astype(F32) * mod_ref[tile, 5:6] * keep_ref[...]).astype(BF16)
    dm_ref[...] = grad
    sum_ref[0] = jnp.sum(grad.astype(F32), axis=0, keepdims=True)


def middle_call(om, w, bias, x, mod, top, keep, away, own):
    tokens, width = x.shape
    tiles = tokens // ROW
    rows = pl.BlockSpec((ROW, width), lambda i: (i, 0))
    half = pl.BlockSpec((ROW, width // 2), lambda i: (i, 0))
    fixed = pl.BlockSpec((width, width), lambda i: (0, 0))
    return call(
        middle_body,
        "middle",
        4 * tokens * width * width,
        26 * tokens * width,
        grid=(tiles,),
        in_specs=[
            pl.BlockSpec((width, ROW), lambda i: (0, i)),
            fixed,
            pl.BlockSpec((1, width), lambda i: (0, 0)),
            rows,
            pl.BlockSpec(mod.shape, lambda i: (0, 0, 0)),
            rows,
            pl.BlockSpec((ROW, 1), lambda i: (i, 0)),
            pl.BlockSpec((width, width // 2), lambda i: (0, 0)),
            pl.BlockSpec((width, width // 2), lambda i: (0, 0)),
        ],
        out_specs=[rows, rows, rows, half, half, rows, pl.BlockSpec((1, 1, width), lambda i: (i, 0, 0))],
        out_shape=[
            shaped((tokens, width), F32),
            shaped((tokens, width), F32),
            shaped((tokens, width), BF16),
            shaped((tokens, width // 2), BF16),
            shaped((tokens, width // 2), BF16),
            shaped((tokens, width), BF16),
            shaped((tiles, 1, width), F32),
        ],
    )(om, w, bias, x, mod, top, keep, away, own)


def hidden_body(h_ref, away_ref, dm_ref, w1_ref, b1_ref, w2_ref, *refs):
    g_ref, df_ref, sum_ref, send_ref = refs[-4:]
    first, second = math.sqrt(2.0 / math.pi), 0.044715
    pre = dot(h_ref[...], w1_ref[...]) + b1_ref[...]
    square = pre * pre
    tanh = jnp.tanh(first * pre * (1.0 + second * square))
    half = 0.5 * (1.0 + tanh)
    g_ref[...] = (pre * half).astype(BF16)
    slope = half + (0.5 * first) * pre * (1.0 - tanh * tanh) * (1.0 + (3.0 * second) * square)
    grad = (dot(dm_ref[...], w2_ref[...], NT) * slope).astype(BF16)
    df_ref[...] = grad
    sum_ref[...] = jnp.sum(grad.astype(F32), axis=0, keepdims=True)
    send_ref[...] = dot(away_ref[...], grad, TN)


def hidden_call(h, away, dm, w1, b1, w2, first, count, before):
    tokens, width = h.shape
    hidden = w1.shape[1]
    block = UNITS
    base = first // block
    full = pl.BlockSpec((tokens, width), lambda j: (0, 0))
    half = width // 2
    place = pl.BlockSpec(memory_space=pl.ANY)
    return call(
        hidden_body,
        "hidden",
        6 * tokens * width * count,
        6 * tokens * width + 4 * tokens * count + 8 * width * count,
        grid=(count // block,),
        in_specs=[
            full,
            pl.BlockSpec((tokens, half), lambda j: (0, 0)),
            full,
            pl.BlockSpec((width, block), lambda j: (0, base + j)),
            pl.BlockSpec((1, block), lambda j: (0, base + j)),
            pl.BlockSpec((block, width), lambda j: (base + j, 0)),
        ]
        + [place] * len(before),
        out_specs=[
            pl.BlockSpec((tokens, block), lambda j: (0, base + j)),
            pl.BlockSpec((tokens, block), lambda j: (0, base + j)),
            pl.BlockSpec((1, block), lambda j: (0, base + j)),
            pl.BlockSpec((half, block), lambda j: (0, j)),
        ],
        out_shape=[
            shaped((tokens, hidden), BF16),
            shaped((tokens, hidden), BF16),
            shaped((1, hidden), F32),
            shaped((half, count), F32),
        ],
        input_output_aliases={6 + n: n for n in range(len(before))},
    )(h, away, dm, w1, b1, w2, *before)


def shard_rows(spot_ref, g_ref, grad, put):
    shards = spot_ref.shape[1]
    rows = g_ref.shape[1] // 2
    shard = g_ref.shape[1] // shards
    part = pl.program_id(0)
    place = 0
    for piece in range(2):
        made = dot(g_ref[:, piece * rows : (piece + 1) * rows], grad, TN)
        for at in range(0, rows, shard):
            put(spot_ref[part, place], made[at : at + shard])
            place += 1


def rows_send_body(side_ref, spot_ref, g_ref, dm_ref, out_ref):
    def put(spot, value):
        out_ref[spot] = value

    shard_rows(spot_ref, g_ref, dm_ref[...], put)


def rows_send_call(side, spots, g, dm):
    tokens, hidden = g.shape
    width = dm.shape[1]
    half = hidden // 2
    shards = spots.shape[1]
    return call(
        rows_send_body,
        "rows_send",
        2 * tokens * half * width,
        2 * tokens * (half + width) + 4 * half * width,
        grid_spec=pltpu.PrefetchScalarGridSpec(
            num_scalar_prefetch=2,
            grid=(width // COLUMNS,),
            in_specs=[
                pl.BlockSpec((tokens, half), lambda j, side, spots: (0, side[0])),
                pl.BlockSpec((tokens, COLUMNS), lambda j, side, spots: (0, j)),
            ],
            out_specs=pl.BlockSpec((shards, half // shards, COLUMNS), lambda j, side, spots: (0, 0, j)),
        ),
        out_shape=shaped((shards, half // shards, width), F32),
    )(side, spots, g, dm)


def rows_keep_body(side_ref, spot_ref, g_ref, dm_ref, got_ref, *outs, bounds):
    half = spot_ref.shape[1] // 2
    step = pl.program_id(0)
    for part in range(len(bounds) - 1):

        @pl.when((step >= bounds[part]) & (step < bounds[part + 1]))
        def _():
            def put(spot, value):
                value = value + got_ref[spot]

                @pl.when(spot < half)
                def _():
                    outs[2 * part + 1][jnp.minimum(spot, half - 1)] = value

                @pl.when(spot >= half)
                def _():
                    outs[2 * part][jnp.maximum(spot - half, 0)] = value

            shard_rows(spot_ref, g_ref, dm_ref[...], put)


def rows_keep_call(side, spots, g, dm, got, counts):
    tokens, hidden = g.shape
    width = dm.shape[1]
    half = hidden // 2
    steps, shards = spots.shape
    bounds = [sum(counts[:n]) for n in range(len(counts) + 1)]
    specs, shapes = [], []
    for part, count in enumerate(counts):
        for _ in range(2):
            specs.append(
                pl.BlockSpec(
                    (shards // 2, half // shards, COLUMNS),
                    functools.partial(
                        lambda j, side, spots, first, count: (0, 0, jnp.clip(j - first, 0, count - 1)),
                        first=bounds[part],
                        count=count,
                    ),
                )
            )
            shapes.append(shaped((shards // 2, half // shards, count * COLUMNS), F32))
    made = call(
        functools.partial(rows_keep_body, bounds=bounds),
        "rows_keep",
        2 * tokens * half * width,
        2 * tokens * (half + width) + 8 * half * width,
        grid_spec=pltpu.PrefetchScalarGridSpec(
            num_scalar_prefetch=2,
            grid=(steps,),
            in_specs=[
                pl.BlockSpec((tokens, half), lambda j, side, spots: (0, side[0])),
                pl.BlockSpec((tokens, COLUMNS), lambda j, side, spots: (0, j)),
                pl.BlockSpec((shards, half // shards, COLUMNS), lambda j, side, spots: (0, 0, j)),
            ],
            out_specs=specs,
        ),
        out_shape=shapes,
    )(side, spots, g, dm, got)
    made = [array.reshape(-1, array.shape[2]) for array in made]
    return list(zip(made[::2], made[1::2]))


def result_body(g_ref, w_ref, b_ref, x1_ref, mod_ref, top_ref, keep_ref, out_ref, sum_ref):
    tile = pl.program_id(0)
    branch = dot(g_ref[...], w_ref[...]) + b_ref[...]
    out_ref[...] = (x1_ref[...] + mod_ref[tile, 5:6] * keep_ref[...] * branch).astype(BF16)
    sum_ref[0] = jnp.sum(top_ref[...].astype(F32) * keep_ref[...] * branch, axis=0, keepdims=True)


def result_call(g, w, bias, x1, mod, top, keep):
    tokens, width = x1.shape
    hidden = g.shape[1]
    tiles = tokens // ROW
    rows = pl.BlockSpec((ROW, width), lambda i: (i, 0))
    return call(
        result_body,
        "result",
        2 * tokens * width * hidden,
        2 * tokens * hidden + 2 * hidden * width + 8 * tokens * width,
        grid=(tiles,),
        in_specs=[
            pl.BlockSpec((ROW, hidden), lambda i: (i, 0)),
            pl.BlockSpec((hidden, width), lambda i: (0, 0)),
            pl.BlockSpec((1, width), lambda i: (0, 0)),
            rows,
            pl.BlockSpec(mod.shape, lambda i: (0, 0, 0)),
            rows,
            pl.BlockSpec((ROW, 1), lambda i: (i, 0)),
        ],
        out_specs=[rows, pl.BlockSpec((1, 1, width), lambda i: (i, 0, 0))],
        out_shape=[shaped((tokens, width), BF16), shaped((tiles, 1, width), F32)],
    )(g, w, bias, x1, mod, top, keep)


def middle_back_body(
    df_ref, w1_ref, x1_ref, mod_ref, top_ref, a_ref, wp_ref,
    dx_ref, da_ref, do_ref, sum_ref,
):
    tile = pl.program_id(0)
    grad = dot(df_ref[...], w1_ref[...], NT)
    normal, inverse = normed(x1_ref[...])
    back = normed_back(grad * (1.0 + mod_ref[tile, 4:5]), normal, inverse)
    dx = top_ref[...].astype(F32) + back
    dx_ref[...] = dx
    da = (dx * mod_ref[tile, 2:3]).astype(BF16)
    da_ref[...] = da
    do_ref[...] = dot(wp_ref[...], da, NT).astype(BF16)
    sum_ref[0, 0:1] = jnp.sum(dx * a_ref[...], axis=0, keepdims=True)
    sum_ref[0, 1:2] = jnp.sum(grad, axis=0, keepdims=True)
    sum_ref[0, 2:3] = jnp.sum(grad * normal, axis=0, keepdims=True)
    sum_ref[0, 3:4] = jnp.sum(da.astype(F32), axis=0, keepdims=True)


def middle_back_call(df, w1, x1, mod, top, a, wp):
    tokens, width = x1.shape
    hidden = df.shape[1]
    tiles = tokens // ROW
    rows = pl.BlockSpec((ROW, width), lambda i: (i, 0))
    return call(
        middle_back_body,
        "middle_back",
        2 * tokens * width * (hidden + width),
        2 * tokens * hidden + 2 * hidden * width + 18 * tokens * width,
        grid=(tiles,),
        in_specs=[
            pl.BlockSpec((ROW, hidden), lambda i: (i, 0)),
            pl.BlockSpec((width, hidden), lambda i: (0, 0)),
            rows,
            pl.BlockSpec(mod.shape, lambda i: (0, 0, 0)),
            rows,
            rows,
            pl.BlockSpec((width, width), lambda i: (0, 0)),
        ],
        out_specs=[
            rows,
            rows,
            pl.BlockSpec((width, ROW), lambda i: (0, i)),
            pl.BlockSpec((1, 4, width), lambda i: (i, 0, 0)),
        ],
        out_shape=[
            shaped((tokens, width), F32),
            shaped((tokens, width), BF16),
            shaped((width, tokens), BF16),
            shaped((tiles, 4, width), F32),
        ],
    )(df, w1, x1, mod, top, a, wp)


class Wide:
    def __init__(self, *parts):
        self.parts = parts
        self.count = sum(rows for _, _, rows in parts)
        self.steps = 3

    def arrays(self):
        return [array for array, _, _ in self.parts]

    def specs(self, at):
        return [
            pl.BlockSpec(
                (1, rows, array.shape[2]),
                functools.partial(lambda j, at, index: (jnp.clip(j - at, 0, 2), index, 0), at=at, index=first // rows),
            )
            for array, first, rows in self.parts
        ]

    def value(self, refs):
        got = [ref[0] for ref in refs]
        return jnp.concatenate(got, axis=0) if len(got) > 1 else got[0]

    def product(self, left, right):
        return dot(left, right, TT)

    def sums(self, right):
        return dot(jnp.ones((8, right.shape[1]), BF16), right, NT)[:1]


class Plain:
    def __init__(self, array, first, count, steps):
        self.array, self.first, self.count, self.steps = array, first, count, steps

    def arrays(self):
        return [self.array]

    def specs(self, at):
        base, steps = self.first // self.count, self.steps
        index = functools.partial(
            lambda j, at, base, steps: (0, base + jnp.clip(j - at, 0, steps - 1)), at=at, base=base, steps=steps
        )
        return [pl.BlockSpec((self.array.shape[0], self.count), index)]

    def value(self, refs):
        return refs[0][...]

    def product(self, left, right):
        return dot(left, right, TN)

    def sums(self, right):
        return jnp.sum(right.astype(F32), axis=0, keepdims=True)


def columns_body(*refs, right, both):
    count = len(right.arrays())
    left_ref, right_refs, rest = refs[0], refs[1 : 1 + count], refs[1 + count :]
    value = right.value(right_refs)
    made = right.product(left_ref[...], value)
    if both:
        got_ref, send_ref, keep_ref = rest
        made = made + got_ref[...]
        rows = keep_ref.shape[0]
        send_ref[...] = made[rows:]
        keep_ref[...] = made[:rows]
    else:
        send_ref, sum_ref = rest
        send_ref[...] = made
        sum_ref[...] = right.sums(value)


def columns_call(left, right, name, got=None):
    tokens, half = left.shape
    count = right.count * right.steps
    both = got is not None
    wide = pl.BlockSpec((half, right.count), lambda j: (0, j))
    narrow = pl.BlockSpec((half // 2, right.count), lambda j: (0, j))
    made = call(
        functools.partial(columns_body, right=right, both=both),
        name,
        2 * tokens * half * count,
        2 * tokens * (count + half) + 8 * half * count,
        grid=(right.steps,),
        in_specs=[pl.BlockSpec(left.shape, lambda j: (0, 0)), *right.specs(0)] + [wide] * both,
        out_specs=[narrow, narrow] if both else [wide, pl.BlockSpec((1, right.count), lambda j: (0, j))],
        out_shape=[shaped((half // 2, count), F32)] * 2
        if both
        else [shaped((half, count), F32), shaped((1, count), F32)],
    )(left, *right.arrays(), *([got] if both else []))
    return [tuple(made)] if both else made


def pair_body(*refs, rights, both):
    counts = [len(right.arrays()) for right in rights]
    step = pl.program_id(0)
    at = 0
    rest = refs[2 + sum(counts) :]
    for number, (right, count) in enumerate(zip(rights, counts)):
        mine = (refs[at], *refs[at + 1 : at + 1 + count], *rest)
        when = step < rights[0].steps if number == 0 else step >= rights[0].steps
        pl.when(when)(functools.partial(columns_body, *mine, right=right, both=both))
        at += 1 + count


def pair_call(lefts, rights, name, got=None):
    tokens, half = lefts[0].shape
    step = rights[0].count
    steps = sum(right.steps for right in rights)
    count = step * steps
    both = got is not None
    wide = pl.BlockSpec((half, step), lambda j: (0, j))
    narrow = pl.BlockSpec((half // 2, step), lambda j: (0, j))
    operands, specs, at = [], [], 0
    for left, right in zip(lefts, rights):
        operands += [left, *right.arrays()]
        specs += [pl.BlockSpec(left.shape, lambda j: (0, 0)), *right.specs(at)]
        at += right.steps
    made = call(
        functools.partial(pair_body, rights=rights, both=both),
        name,
        2 * tokens * half * count,
        2 * tokens * (count + half) + 8 * half * count,
        grid=(steps,),
        in_specs=specs + [wide] * both,
        out_specs=[narrow, narrow] if both else [wide, pl.BlockSpec((1, step), lambda j: (0, j))],
        out_shape=[shaped((half // 2, count), F32)] * 2
        if both
        else [shaped((half, count), F32), shaped((1, count), F32)],
    )(*operands, *([got] if both else []))
    return [tuple(made)] if both else made


def moved_body(om_ref, h_ref, away_ref, own_ref, *out_refs):
    om, hidden = om_ref[...], h_ref[...]
    out_refs[0][...] = dot(om, away_ref[...], TN).astype(BF16)
    out_refs[1][...] = dot(om, own_ref[...], TN).astype(BF16)
    out_refs[2][...] = dot(hidden, away_ref[...]).astype(BF16)
    out_refs[3][...] = dot(hidden, own_ref[...]).astype(BF16)


def moved_call(om, hidden, away, own):
    tokens, width = hidden.shape
    half = width // 2
    block = tokens // 2
    fixed = pl.BlockSpec((width, half), lambda i: (0, 0))
    out = pl.BlockSpec((block, half), lambda i: (i, 0))
    return call(
        moved_body,
        "moved",
        4 * tokens * width * width,
        8 * tokens * width + 2 * width * width,
        grid=(2,),
        in_specs=[
            pl.BlockSpec((width, block), lambda i: (0, i)),
            pl.BlockSpec((block, width), lambda i: (i, 0)),
            fixed,
            fixed,
        ],
        out_specs=[out] * 4,
        out_shape=[shaped((tokens, half), BF16)] * 4,
    )(om, hidden, away, own)


def first_back_body(low_ref, high_ref, w_ref, x_ref, mod_ref, dx_ref, out_ref, sum_ref):
    tile = pl.program_id(0)
    width = x_ref.shape[1]
    grad = None
    for third in range(3):
        rows = jnp.concatenate([low_ref[third], high_ref[third]], axis=0)
        part = dot(rows, w_ref[:, third * width : (third + 1) * width], TT)
        grad = part if grad is None else grad + part
    normal, inverse = normed(x_ref[...].astype(F32))
    out_ref[...] = dx_ref[...] + normed_back(grad * (1.0 + mod_ref[tile, 1:2]), normal, inverse)
    sum_ref[0, 0:1] = jnp.sum(grad, axis=0, keepdims=True)
    sum_ref[0, 1:2] = jnp.sum(grad * normal, axis=0, keepdims=True)


def first_back_call(low, high, w, x, mod, dx):
    tokens, width = x.shape
    wide = w.shape[1]
    half = pl.BlockSpec((3, width // 2, ROW), lambda i: (0, 0, i))
    tiles = tokens // ROW
    rows = pl.BlockSpec((ROW, width), lambda i: (i, 0))
    return call(
        first_back_body,
        "first_back",
        2 * tokens * width * wide,
        2 * tokens * wide + 2 * width * wide + 10 * tokens * width,
        grid=(tiles,),
        in_specs=[
            half,
            half,
            pl.BlockSpec((width, wide), lambda i: (0, 0)),
            rows,
            pl.BlockSpec(mod.shape, lambda i: (0, 0, 0)),
            rows,
        ],
        out_specs=[rows, pl.BlockSpec((1, 2, width), lambda i: (i, 0, 0))],
        out_shape=[shaped((tokens, width), F32), shaped((tiles, 2, width), F32)],
    )(low, high, w, x, mod, dx)


def payload_body(item_ref, one_ref, two_ref, gate_ref, dm_ref, df_ref, first_ref, last_ref, cond_ref, out_ref):
    tiles, _, width = one_ref.shape
    items = out_ref.shape[0]
    parts = [(one_ref, 0), (one_ref, 1), (two_ref, 0), (two_ref, 1), (two_ref, 2), (gate_ref, 0)]
    for number, (ref, row) in enumerate(parts):
        for item in range(items):
            total = jnp.zeros((1, width), F32)
            for tile in range(tiles):
                total = total + jnp.where(item_ref[tile] == item, ref[tile, row : row + 1], 0.0)
            out_ref[item : item + 1, number * width : (number + 1) * width] = total.astype(BF16).astype(F32)
    at = 6 * width
    hidden = df_ref.shape[1]
    out_ref[0:1, at : at + hidden // 2] = df_ref[:, : hidden // 2]
    out_ref[1:2, at : at + hidden // 2] = df_ref[:, hidden // 2 :]
    out_ref[2:3, at : at + width] = jnp.sum(dm_ref[:, 0], axis=0, keepdims=True)
    out_ref[2:3, at + width : at + 2 * width] = jnp.sum(two_ref[:, 3], axis=0, keepdims=True)
    rest = width - COLUMNS
    for number, third in enumerate((0, 2)):
        spot = at + number * width
        out_ref[3:4, spot : spot + COLUMNS] = first_ref[:, width + third * COLUMNS : width + (third + 1) * COLUMNS]
        out_ref[3:4, spot + COLUMNS : spot + width] = last_ref[:, third * rest : (third + 1) * rest]
    out_ref[:, at + 2 * width :] = cond_ref[...]


def payload_call(tile_item, *sums):
    items, width = sums[-1].shape
    out = shaped((items, 9 * width), F32)
    return call(
        payload_body,
        "payload",
        0,
        0,
        grid=(1,),
        in_specs=[pl.BlockSpec(memory_space=pltpu.SMEM)]
        + [pl.BlockSpec(part.shape, functools.partial(lambda j, rank: (0,) * rank, rank=part.ndim)) for part in sums],
        out_specs=pl.BlockSpec(out.shape, lambda j: (0, 0)),
        out_shape=out,
    )(tile_item, *sums)


def modulation_back_body(me_ref, *refs, count):
    part_refs, cond_refs, sum_refs = refs[:count], refs[count : 2 * count], refs[2 * count : 3 * count]
    label_ref, w_ref, grad_ref, bias_ref, table_ref, own_sums_ref, act_ref, own_ref, total_ref = refs[3 * count :]
    step = pl.program_id(0)
    width = act_ref.shape[1]
    shard = grad_ref.shape[0]
    items = own_sums_ref.shape[0]

    @pl.when(step == 0)
    def _():
        at = 0
        for cond_ref in cond_refs:
            cond = cond_ref[...]
            act_ref[at : at + cond.shape[0]] = (cond / (1.0 + jnp.exp(-cond))).astype(BF16)
            at += cond.shape[0]
        row = lax.broadcasted_iota(jnp.int32, (width, 128), 0)
        column = lax.broadcasted_iota(jnp.int32, (width, 128), 1)
        picked = jnp.where((column < shard) & (row == me_ref[0] * shard + column), 1.0, 0.0).astype(BF16)
        own_ref[...] = dot(act_ref[...], picked).astype(BF16)
        total_ref[...] = jnp.zeros_like(total_ref)
        sums = None
        for sum_ref in sum_refs:
            rows = sum_ref.shape[0]
            item = lax.broadcasted_iota(jnp.int32, (items, rows), 0)
            source = lax.broadcasted_iota(jnp.int32, (items, rows), 1)
            select = (lax.rem(source, jnp.full_like(source, items)) == item).astype(F32)
            part = dot(select, sum_ref[...], NN, HIGHEST)
            sums = part if sums is None else sums + part
        own_sums_ref[...] = sums

    mod = jnp.concatenate([part_ref[...] for part_ref in part_refs], axis=0)
    bias_ref[...] = jnp.sum(mod, axis=0, keepdims=True)
    mod = mod.astype(BF16)
    grad_ref[...] = dot(own_ref[...], mod, TN)[:shard]
    total_ref[...] += dot(w_ref[...], mod, NT)

    @pl.when(step == pl.num_programs(0) - 1)
    def _():
        cond = jnp.concatenate([cond_ref[...] for cond_ref in cond_refs], axis=0)
        gate = 1.0 / (1.0 + jnp.exp(-cond))
        grad = total_ref[...].T * (gate * (1.0 + cond * (1.0 - gate)))
        classes = table_ref.shape[0]
        select = (label_ref[...] == lax.broadcasted_iota(jnp.int32, (grad.shape[0], classes), 1)).astype(F32)
        table_ref[...] = dot(select, grad, TN, HIGHEST)


def modulation_back_call(me, parts, used, w, classes, shard, items):
    width, wide = w.shape
    block = 1152
    rows = sum(part.shape[0] for part in parts)
    extra = parts[0].shape[1] - wide - width
    at = (wide + extra) // width
    return call(
        functools.partial(modulation_back_body, count=len(parts)),
        "modulation_back",
        4 * rows * width * wide,
        2 * width * wide,
        grid=(wide // block,),
        in_specs=[
            pl.BlockSpec(memory_space=pltpu.SMEM),
            *[pl.BlockSpec((part.shape[0], block), lambda j: (0, j)) for part in parts],
            *[pl.BlockSpec((part.shape[0], width), lambda j: (0, at)) for part in parts],
            *[pl.BlockSpec((part.shape[0], extra), lambda j: (0, wide // extra)) for part in parts],
            pl.BlockSpec(used.shape, lambda j: (0, 0)),
            pl.BlockSpec((width, block), lambda j: (0, j)),
        ],
        out_specs=[
            pl.BlockSpec((shard, block), lambda j: (0, j)),
            pl.BlockSpec((1, block), lambda j: (0, j)),
            pl.BlockSpec((classes, width), lambda j: (0, 0)),
            pl.BlockSpec((items, extra), lambda j: (0, 0)),
        ],
        out_shape=[
            shaped((shard, wide), F32),
            shaped((1, wide), F32),
            shaped((classes, width), F32),
            shaped((items, extra), F32),
        ],
        scratch_shapes=[
            pltpu.VMEM((rows, width), BF16),
            pltpu.VMEM((rows, 128), BF16),
            pltpu.VMEM((width, rows), F32),
        ],
    )(me, *parts, *parts, *parts, used, w)


def add_body(*refs, plans):
    outs = refs[-len(plans) :]
    at = 0
    for out_ref, (count, first, rows) in zip(outs, plans):
        value = refs[at][first : first + rows]
        for term in range(1, count):
            value = value + refs[at + term][first : first + rows]
        out_ref[...] = value
        at += count


def add_call(jobs):
    steps = 3 if all(terms[0].shape[1] % 384 == 0 for terms, _, _ in jobs) else 2
    if any(terms[0].shape[1] % (128 * steps) for terms, _, _ in jobs):
        steps = 1
    operands, specs, outs, shapes, plans = [], [], [], [], []
    moved = 0
    for terms, first, rows in jobs:
        wide = terms[0].shape[1]
        block = wide // steps
        for term in terms:
            size, index, at = rows, first // rows, 0
            while size % 8 and size < term.shape[0]:
                size, index, at = size * 2, 0, first
            operands.append(term)
            specs.append(pl.BlockSpec((size, block), functools.partial(lambda j, index: (index, j), index=index)))
        plans.append((len(terms), at, rows))
        outs.append(pl.BlockSpec((rows, block), lambda j: (0, j)))
        shapes.append(shaped((rows, wide), F32))
        moved += 4 * rows * wide * (len(terms) + 1)
    return call(
        functools.partial(add_body, plans=plans),
        "add",
        moved // 4,
        moved,
        grid=(steps,),
        in_specs=specs,
        out_specs=outs,
        out_shape=shapes,
    )(*operands)


def assemble_body(*refs, plans):
    outs = refs[-len(plans) :]
    for out_ref, (rows, blocks) in zip(outs, plans):
        for terms, source, target, count in blocks:
            value = refs[terms[0]][:rows, source : source + count]
            for term in terms[1:]:
                value = value + refs[term][:rows, source : source + count]
            out_ref[:, target : target + count] = value


def assemble_call(outputs):
    operands, specs, known, plans, shapes = [], [], {}, [], []
    for blocks in outputs:
        rows, target, made = blocks[0][0].rows, 0, []
        for chunk, source, count in blocks:
            if id(chunk) not in known:
                known[id(chunk)] = []
                for term in chunk.terms:
                    size = rows
                    while size % 8 and size < term.shape[0]:
                        size *= 2
                    known[id(chunk)].append(len(operands))
                    operands.append(term)
                    specs.append(pl.BlockSpec((size, term.shape[1]), lambda j: (0, 0)))
            made.append((known[id(chunk)], source, target, count))
            target += count
        plans.append((rows, made))
        shapes.append(shaped((rows, target), F32))
    return call(
        functools.partial(assemble_body, plans=plans),
        "assemble",
        0,
        sum(8 * 4 * shape.shape[0] * shape.shape[1] for shape in shapes),
        grid=(1,),
        in_specs=specs,
        out_specs=[pl.BlockSpec(shape.shape, lambda j: (0, 0)) for shape in shapes],
        out_shape=shapes,
    )(*operands)


def bit_order(bits, core, lead):
    order = list(range(bits))
    if bits >= 2 and core:
        order[:2] = [1, 0]
    if lead and lead < bits:
        order.remove(lead)
        order.insert(0, lead)
    return order


class Chunk:
    def __init__(self, send, kept, wait, lead):
        self.send, self.terms, self.wait, self.lead = send, [kept], wait, lead
        self.rows = kept.shape[0]
        self.stage = 0


class Spread:
    def __init__(self, rows):
        self.own, self.other = [rows], None
        self.stage = 0


class Flow:
    def __init__(self, bits):
        self.bits = bits
        self.fresh, self.crossing, self.chunks, self.last = [], [], [], []
        self.blocks = ([], [], [])
        self.spreads = []

    def emit(self, send, keep, store, waits=(0,), leads=(0,)):
        self.fresh.append((send, keep, store, waits, leads))

    def spread(self, rows):
        self.spreads.append(Spread(rows))
        return self.spreads[-1]

    def busy(self):
        moving = self.fresh or self.crossing or any(chunk.stage < self.bits for chunk in self.chunks)
        return moving or any(spread.stage <= self.bits for spread in self.spreads)

    def pairs(self, stage, lead):
        size = 1 << self.bits
        flips = [1 << bit_order(self.bits, core, lead)[stage] for core in range(2)]
        return [(core * size + i, core * size + (i ^ flips[core])) for core in range(2) for i in range(size)]

    def received(self, live):
        live, (cores, blocks, doubles) = lax.optimization_barrier((live, self.blocks))
        for spread, block in zip([spread for spread in self.spreads if spread.other is None and spread.stage], doubles):
            if spread.stage > self.bits:
                spread.other = block
            elif spread.stage == self.bits:
                spread.own += block
            else:
                spread.own = [jnp.concatenate(spread.own + block, axis=0)]
        jobs, waiting = [], []
        for chunk, block in zip(self.last, blocks):
            chunk.terms.append(block)
            if chunk.stage < self.bits:
                chunk.rows //= 2
                jobs.append((chunk.terms, chunk.rows, chunk.rows))
                waiting.append(chunk)
        for (_, keep, store, waits, leads), core in zip(self.crossing, cores):
            new = [Chunk(*pair, wait, lead) for pair, wait, lead in zip(keep(core), waits, leads)]
            store += new
            self.chunks += new
        for chunk, value in zip(waiting, add_call(jobs) if jobs else []):
            chunk.send = value
        return live

    def round(self, live):
        live = self.received(live)
        moving = [chunk for chunk in self.chunks if chunk.stage < self.bits and not chunk.wait]
        for chunk in self.chunks:
            chunk.wait = max(0, chunk.wait - 1)
        crossing, self.fresh = self.fresh, []
        doubling = [spread for spread in self.spreads if spread.stage <= self.bits]
        live, cores, sends, doubles = lax.optimization_barrier(
            (
                live,
                [entry[0] for entry in crossing],
                [chunk.send for chunk in moving],
                [spread.own for spread in doubling],
            )
        )
        blocks = []
        for chunk, send in zip(moving, sends):
            blocks.append(lax.ppermute(send, ("stream", "batch"), self.pairs(chunk.stage, chunk.lead)))
            chunk.stage += 1
        cores = [lax.ppermute(send, "stream", [(0, 1), (1, 0)]) for send in cores]
        for number, (spread, rows) in enumerate(zip(doubling, doubles)):
            spread.own = rows
            if spread.stage < self.bits:
                pairs = self.pairs(self.bits - 1 - spread.stage, 0)
                doubles[number] = [lax.ppermute(piece, ("stream", "batch"), pairs) for piece in rows]
            else:
                doubles[number] = [lax.ppermute(piece, "stream", [(0, 1), (1, 0)]) for piece in rows]
            spread.stage += 1
        self.crossing, self.last, self.blocks = crossing, moving, (cores, blocks, doubles)
        return live


def offsets_of(bits, side, lead):
    places = jnp.arange(1 << bits, dtype=jnp.int32)
    made = []
    for core in range(2):
        offset = jnp.zeros_like(places)
        for stage, bit in enumerate(bit_order(bits, core, lead)):
            offset = offset | (((places >> (bits - 1 - stage)) & 1) << bit)
        made.append(offset)
    return jnp.where(side == 0, made[0], made[1])


def places_of(bits, side, lead, offset):
    made = []
    for core in range(2):
        place = jnp.zeros_like(offset)
        for stage, bit in enumerate(bit_order(bits, core, lead)):
            place = place | (((offset >> bit) & 1) << (bits - 1 - stage))
        made.append(place)
    return jnp.where(side == 0, made[0], made[1])


def time_embed(steps_in, width):
    half_width = width // 2
    frequency = jnp.exp(-math.log(10000.0) * jnp.arange(half_width, dtype=F32) / half_width)
    angles = steps_in.astype(F32)[:, None] * frequency[None, :]
    return jnp.concatenate([jnp.cos(angles), jnp.sin(angles)], axis=1)


def per_device(
    tokens, segments, timesteps, labels, head_keep, token_keep, class_table, w_ada, b_ada,
    w_qkv, b_qv, w_proj, b_proj, w_fc1, b_fc1, w_fc2, b_fc2, out_grad, *, batch,
):
    x, top = tokens[0], out_grad[0]
    count, width = x.shape
    hidden = w_fc1.shape[1]
    heads = head_keep.shape[1]
    items = timesteps.shape[0]
    tiles = count // ROW
    groups = count // GROUP
    null_class = class_table.shape[0] - 1
    bits = batch.bit_length() - 1
    devices = 2 * batch
    stream = lax.axis_index("stream")
    index = lax.axis_index("batch")

    own_labels = lax.dynamic_slice_in_dim(labels, index * items, items)
    used = jnp.where(stream == 0, own_labels, null_class)
    cond = time_embed(timesteps, width) + jnp.take(class_table, used, axis=0).astype(F32)
    act = jax.nn.silu(cond).astype(BF16)
    modulation = dot(act, w_ada) + b_ada
    tile_item = segments[::ROW] - index * items
    chosen = tile_item[:, None] == jnp.arange(items, dtype=jnp.int32)[None, :]
    mod = jnp.sum(jnp.where(chosen[:, :, None], modulation[None], 0.0), axis=1)
    mod = mod.reshape(tiles, 6, width)
    tile_heads = jnp.sum(jnp.where(chosen[:, :, None], head_keep[None], 0), axis=1).astype(F32)
    head_columns = jnp.repeat(tile_heads.T, ROW, axis=1).reshape(heads, 1, count)
    keep = token_keep[0].astype(F32)[:, None]
    grouped = segments.reshape(groups, GROUP)
    flag = (grouped[:, 0] == grouped[:, -1]).astype(jnp.int32)

    shard = width // devices

    def picked(side):
        order = side * batch + (index ^ offsets_of(bits, side, 0))
        source = (order[:, None] * shard + jnp.arange(shard, dtype=jnp.int32)[None, :]).reshape(width // 2)
        return (jnp.arange(width, dtype=jnp.int32)[:, None] == source[None, :]).astype(BF16)

    def spots(side):
        return jnp.stack([places_of(bits, side, lead, jnp.arange(batch, dtype=jnp.int32) ^ index) for steps, lead in ROW_PARTS for _ in range(steps)])

    other = 1 - stream
    away, own = picked(other), picked(stream)

    bias_full = jnp.concatenate([b_qv[:width], jnp.zeros((width,), F32), b_qv[width:]])[:, None]
    h1, qkv = qkv_call(x, mod, w_qkv, bias_full)
    probs, mixed, om = attention_call(flag, qkv, head_columns, heads)
    a, x1, h2, h2_away, h2_own, dm, sum_dm = middle_call(om, w_proj, b_proj[None], x, mod, top, keep, away, own)

    flow = Flow(bits)
    fc1, fc2, wide = [], [], []

    filled, latest = (), {}
    for low, high in ((0, 2 * UNITS), (2 * UNITS, 5 * UNITS), (5 * UNITS, hidden)):
        *filled, send = hidden_call(h2, h2_away, dm, w_fc1, b_fc1[None], w_fc2, low, high - low, filled)
        latest["df"] = filled[1]

        def hidden_keep(got, low=low, count=high - low):
            return columns_call(h2_own, Plain(latest["df"], low, UNITS, count // UNITS), "hidden_keep", got)

        flow.emit(send, hidden_keep, fc1)
        h2, filled = flow.round((h2, filled))
        latest["df"] = filled[1]
    g, df, sum_df = filled

    rows_send = rows_send_call(other[None], spots(other), g, dm)
    flow.emit(
        rows_send.reshape(-1, width),
        lambda got: rows_keep_call(
            stream[None], spots(stream), g, dm, got.reshape(rows_send.shape), [steps for steps, _ in ROW_PARTS]
        ),
        fc2,
        [0] * len(ROW_PARTS),
        [lead for _, lead in ROW_PARTS],
    )
    om_away, om_own, h1_away, h1_own = moved_call(om, h1, away, own)
    df, x1, om_away, om_own, h1_away, h1_own = flow.round((df, x1, om_away, om_own, h1_away, h1_own))
    dx1, da, do, sums_two = middle_back_call(df, w_fc1, x1, mod, top, a, w_proj)

    me = stream * batch + index

    def used_labels(side):
        order = bit_order(bits, 0, 0)[::-1], bit_order(bits, 1, 0)[::-1]
        places = jnp.arange(batch, dtype=jnp.int32)
        offsets = [sum(((places >> n) & 1) << bit for n, bit in enumerate(bits_of)) for bits_of in order]
        from_device = index ^ jnp.where(side == 0, offsets[0], offsets[1])
        return jnp.where(side == 0, jnp.take(labels.reshape(batch, items), from_device, axis=0).reshape(-1), null_class)

    used_rows = jnp.concatenate([used_labels(stream), used_labels(other)])[:, None]
    dx1, da, do, sums_two, g = flow.round((dx1, da, do, sums_two, g))
    half = width // 2
    low = attention_back_call(flag, qkv, do, head_columns, probs, mixed, 0)
    rights = [Plain(da, 0, COLUMNS, width // COLUMNS), Wide((low, 0, COLUMNS))]
    send, first_sums = pair_call([om_away, h1_away], rights, "first_send")
    flow.emit(send, lambda got: pair_call([om_own, h1_own], rights, "first_keep", got), wide)
    result, sum_gate = result_call(g, w_fc2, b_fc2[None], x1, mod, top, keep)
    low, first_sums, result, sum_gate = flow.round((low, first_sums, result, sum_gate))
    high = attention_back_call(flag, qkv, do, head_columns, probs, mixed, 1)
    rest = Wide((low, COLUMNS, half - COLUMNS), (high, 0, half))
    send, high_sums = columns_call(h1_away, rest, "last_send")
    flow.emit(send, lambda got: columns_call(h1_own, rest, "last_keep", got), wide)
    low, high, dx1, high_sums = flow.round((low, high, dx1, high_sums))
    grad_tokens, sums_one = first_back_call(low, high, w_qkv, x, mod, dx1)

    spread = flow.spread(
        payload_call(tile_item, sums_one, sums_two, sum_gate, sum_dm, sum_df, first_sums, high_sums, cond)
    )
    while any(chunk.stage < bits for chunk in fc1 + fc2):
        result = flow.round(result)
    result = flow.round(result)
    grad_w_fc1, grad_w_fc2 = assemble_call(
        [[(chunk, 0, chunk.terms[0].shape[1]) for chunk in store] for store in (fc1, fc2)]
    )
    result, grad_w_fc1, grad_w_fc2 = flow.round((result, grad_w_fc1, grad_w_fc2))
    while any(chunk.stage < bits for chunk in wide):
        result = flow.round(result)
    result = flow.round(result)
    first, last = wide
    each = COLUMNS, width - COLUMNS
    blocks = [
        block
        for third in range(3)
        for block in ((first, width + third * each[0], each[0]), (last, third * each[1], each[1]))
    ]
    grad_w_proj, grad_w_qkv = assemble_call([[(first, 0, width)], blocks])
    while flow.busy():
        result = flow.round(result)
    result, grad_w_proj = flow.received((result, grad_w_proj))
    grad_w_ada, mod_sums, grad_table, own_sums = modulation_back_call(
        me[None], spread.own + spread.other, used_rows, w_ada, null_class + 1, shard, items
    )
    share = 6 * width // devices
    grad_b_ada = lax.dynamic_slice_in_dim(mod_sums[0], me * share, share)
    def own_sums_of(row, first, count):
        return lax.dynamic_slice(own_sums, (row, first), (1, count))[0]

    each = hidden // devices
    grad_b_fc1 = own_sums_of(me // (devices // 2), me % (devices // 2) * each, each)
    grad_b_fc2 = own_sums_of(2, me * shard, shard)
    grad_b_proj = own_sums_of(2, width + me * shard, shard)
    grad_b_qv = own_sums_of(3, me * 2 * shard, 2 * shard)

    return (
        result[None],
        grad_tokens[None],
        grad_table,
        grad_w_ada,
        grad_b_ada,
        grad_w_qkv,
        grad_b_qv,
        grad_w_proj,
        grad_b_proj,
        grad_w_fc1,
        grad_b_fc1,
        grad_w_fc2,
        grad_b_fc2,
    )


def solution(mesh):
    both = ("stream", "batch")
    return jax.shard_map(
        functools.partial(per_device, batch=mesh.shape["batch"]),
        mesh=mesh,
        in_specs=(
            P("stream", "batch", None),
            P("batch"),
            P("batch"),
            P(),
            P("batch", None),
            P("stream", "batch"),
            P(), P(), P(), P(), P(), P(), P(), P(), P(), P(), P(),
            P("stream", "batch", None),
        ),
        out_specs=(
            P("stream", "batch", None),
            P("stream", "batch", None),
            P(),
            P(both, None),
            P(both),
            P(both, None),
            P(both),
            P(both, None),
            P(both),
            P(both, None),
            P(both),
            P(both, None),
            P(both),
        ),
        check_vma=False,
    )
```

```python
import functools
import math

import jax
import jax.numpy as jnp
from jax import lax
from jax.experimental import pallas as pl
from jax.experimental.pallas import tpu as pltpu
from jax.sharding import PartitionSpec as P

F32 = jnp.float32
BF16 = jnp.bfloat16
HIGHEST = lax.Precision.HIGHEST
NORM_EPS = 1e-06
ROW_PARTS = ((2, 0), (1, 2))
ROW = 256
GROUP = 1024
NN = (((1,), (0,)), ((), ()))
NT = (((1,), (1,)), ((), ()))
TN = (((0,), (0,)), ((), ()))
TT = (((0,), (1,)), ((), ()))
VMEM_LIMIT = 60 << 20
COLUMNS = 384
UNITS = 512


def dot(left, right, dims=NN, precision=None):
    return lax.dot_general(left, right, dims, precision=precision, preferred_element_type=F32)


def call(body, name, flops, moved, **kwargs):
    return pl.pallas_call(
        body,
        name=name,
        compiler_params=pltpu.CompilerParams(vmem_limit_bytes=VMEM_LIMIT),
        cost_estimate=pl.CostEstimate(flops=flops // 8, bytes_accessed=moved // 8, transcendentals=0),
        **kwargs,
    )


def shaped(shape, kind):
    return jax.ShapeDtypeStruct(shape, kind)


def normed(values):
    centre = values - jnp.mean(values, axis=-1, keepdims=True)
    spread = jnp.mean(centre * centre, axis=-1, keepdims=True)
    inverse = lax.rsqrt(spread + NORM_EPS)
    return centre * inverse, inverse


def normed_back(grad, normal, inverse):
    first = jnp.mean(grad, axis=-1, keepdims=True)
    second = jnp.mean(grad * normal, axis=-1, keepdims=True)
    return inverse * (grad - first - normal * second)


def qkv_body(x_ref, mod_ref, w_ref, b_ref, h_ref, out_ref):
    @pl.when(pl.program_id(0) == 0)
    def _():
        for tile in range(x_ref.shape[0] // ROW):
            rows = slice(tile * ROW, tile * ROW + ROW)
            normal, _ = normed(x_ref[rows].astype(F32))
            h_ref[rows] = (normal * (1.0 + mod_ref[tile, 1:2]) + mod_ref[tile, 0:1]).astype(BF16)

    out_ref[...] = (dot(w_ref[...], h_ref[...], TT) + b_ref[...].T).astype(BF16)


def qkv_call(x, mod, w, bias):
    tokens, width = x.shape
    wide = w.shape[1]
    block = width
    return call(
        qkv_body,
        "qkv",
        2 * tokens * width * wide,
        2 * (2 * tokens * width + width * wide + tokens * wide),
        grid=(wide // block,),
        in_specs=[
            pl.BlockSpec((tokens, width), lambda j: (0, 0)),
            pl.BlockSpec(mod.shape, lambda j: (0, 0, 0)),
            pl.BlockSpec((width, block), lambda j: (0, j)),
            pl.BlockSpec((1, block), lambda j: (0, j)),
        ],
        out_specs=[
            pl.BlockSpec((tokens, width), lambda j: (0, 0)),
            pl.BlockSpec((block, tokens), lambda j: (j, 0)),
        ],
        out_shape=[shaped((tokens, width), BF16), shaped((wide, tokens), BF16)],
    )(x, mod, w, bias)


def heads_of(ref, head_width):
    values = ref[...].astype(F32)
    return [values[head * head_width : (head + 1) * head_width] for head in range(2)]


def attention_body(flag_ref, q_ref, k_ref, v_ref, keep_ref, p_ref, ot_ref, om_ref):
    head_width = ot_ref.shape[1]
    scale = math.log2(math.e) / math.sqrt(head_width)
    tokens = q_ref.shape[1]
    q, k = [[part.astype(BF16) for part in heads_of(ref, head_width)] for ref in (q_ref, k_ref)]
    v = [jnp.concatenate([part, jnp.ones((8, tokens), F32)], axis=0).astype(BF16) for part in heads_of(v_ref, head_width)]

    def part(head, first, count):
        rows = slice(first, first + count)
        scores = dot(k[head][:, rows], q[head][:, rows], TN)
        top = jnp.max(scores, axis=0, keepdims=True)
        expo = jnp.exp2((scores - top) * scale)
        total = jnp.sum(expo, axis=0, keepdims=True)
        probs = (expo * (1.0 / total)).astype(BF16)
        p_ref[head, rows, rows] = probs
        mixed = dot(v[head][:, rows], probs)
        ot_ref[head, :, rows] = mixed[:head_width] * (1.0 / mixed[head_width : head_width + 1])
        return mixed[:head_width] * keep_ref[head, :, rows]

    def run(count):
        made = [
            jnp.concatenate([part(head, at, count) for at in range(0, tokens, count)], axis=1) for head in range(2)
        ]
        om_ref[...] = jnp.concatenate(made, axis=0).astype(BF16)

    whole = flag_ref[pl.program_id(0)] == 1
    pl.when(whole)(lambda: run(tokens))
    pl.when(jnp.logical_not(whole))(lambda: run(ROW))


def attention_call(flag, qkv, keep, heads):
    wide, tokens = qkv.shape
    width = wide // 3
    head_width = width // heads
    groups = tokens // GROUP
    pairs = heads // 2
    rows = 2 * head_width

    def third(number):
        return pl.BlockSpec((rows, GROUP), functools.partial(lambda g, h, base: (base + h, g), base=number * pairs))

    return call(
        attention_body,
        "attention",
        2 * 2 * heads * tokens * GROUP * 256,
        2 * tokens * wide + 2 * heads * tokens * GROUP + 6 * tokens * width,
        grid=(groups, pairs),
        in_specs=[
            pl.BlockSpec(memory_space=pltpu.SMEM),
            third(0),
            third(1),
            third(2),
            pl.BlockSpec((2, 1, GROUP), lambda g, h: (h, 0, g)),
        ],
        out_specs=[
            pl.BlockSpec((2, GROUP, GROUP), lambda g, h: (h, 0, g)),
            pl.BlockSpec((2, head_width, GROUP), lambda g, h: (h, 0, g)),
            third(0),
        ],
        out_shape=[
            shaped((heads, GROUP, tokens), BF16),
            shaped((heads, head_width, tokens), F32),
            shaped((width, tokens), BF16),
        ],
    )(flag, qkv, qkv, qkv, keep)


def attention_back_body(flag_ref, q_ref, k_ref, v_ref, do_ref, keep_ref, p_ref, ot_ref, out_ref, ds_ref):
    head_width = ot_ref.shape[1]
    scale = 1.0 / math.sqrt(head_width)
    tokens = q_ref.shape[1]
    q, k, v = [[part.astype(BF16) for part in heads_of(ref, head_width)] for ref in (q_ref, k_ref, v_ref)]
    kept = [part * keep_ref[head] for head, part in enumerate(heads_of(do_ref, head_width))]
    do = [part.astype(BF16) for part in kept]
    delta = [jnp.sum(kept[head] * ot_ref[head], axis=0, keepdims=True) for head in range(2)]

    def run(count):
        made = [[], [], []]
        for head in range(2):
            row = [[], [], []]
            for first in range(0, tokens, count):
                rows = slice(first, first + count)
                dp = dot(v[head][:, rows], do[head][:, rows], TN)
                probs = p_ref[head, rows, rows].astype(F32)
                ds = (probs * (dp - delta[head][:, rows])).astype(BF16)
                if count == tokens:
                    ds_ref[head] = ds
                    ds = ds_ref[head]
                row[0].append(dot(k[head][:, rows], ds) * scale)
                row[1].append(dot(q[head][:, rows], ds, NT) * scale)
                row[2].append(dot(do[head][:, rows], p_ref[head, rows, rows], NT))
            for third in range(3):
                made[third].append(jnp.concatenate(row[third], axis=1))
        for third in range(3):
            out_ref[third] = jnp.concatenate(made[third], axis=0).astype(BF16)

    whole = flag_ref[pl.program_id(0)] == 1
    pl.when(whole)(lambda: run(tokens))
    pl.when(jnp.logical_not(whole))(lambda: run(ROW))


def attention_back_call(flag, qkv, do, keep, probs, mixed, part):
    wide, tokens = qkv.shape
    width = wide // 3
    heads, head_width = mixed.shape[:2]
    groups = tokens // GROUP
    pairs = heads // 4
    base = part * pairs
    rows = 2 * head_width

    def third(number):
        first = number * heads // 2 + base
        return pl.BlockSpec((rows, GROUP), functools.partial(lambda g, h, first: (first + h, g), first=first))

    return call(
        attention_back_body,
        "attention_back",
        2 * 2 * heads * tokens * GROUP * 256,
        2 * tokens * wide + heads * tokens * GROUP + 6 * tokens * width,
        grid=(groups, pairs),
        in_specs=[
            pl.BlockSpec(memory_space=pltpu.SMEM),
            third(0),
            third(1),
            third(2),
            third(0),
            pl.BlockSpec((2, 1, GROUP), lambda g, h: (base + h, 0, g)),
            pl.BlockSpec((2, GROUP, GROUP), lambda g, h: (base + h, 0, g)),
            pl.BlockSpec((2, head_width, GROUP), lambda g, h: (base + h, 0, g)),
        ],
        out_specs=pl.BlockSpec((3, rows, GROUP), lambda g, h: (0, h, g)),
        out_shape=shaped((3, width // 2, tokens), BF16),
        scratch_shapes=[pltpu.VMEM((2, GROUP, GROUP), BF16)],
    )(flag, qkv, qkv, qkv, do, keep, probs, mixed)


def middle_body(
    om_ref, w_ref, b_ref, x_ref, mod_ref, top_ref, keep_ref, away_ref, own_ref,
    a_ref, x1_ref, h_ref, h_away_ref, h_own_ref, dm_ref, sum_ref,
):
    tile = pl.program_id(0)
    branch = dot(om_ref[...], w_ref[...], TN) + b_ref[...]
    a_ref[...] = branch
    middle = x_ref[...].astype(F32) + mod_ref[tile, 2:3] * branch
    x1_ref[...] = middle
    normal, _ = normed(middle)
    hidden = (normal * (1.0 + mod_ref[tile, 4:5]) + mod_ref[tile, 3:4]).astype(BF16)
    h_ref[...] = hidden
    h_away_ref[...] = dot(hidden, away_ref[...]).astype(BF16)
    h_own_ref[...] = dot(hidden, own_ref[...]).astype(BF16)
    grad = (top_ref[...].astype(F32) * mod_ref[tile, 5:6] * keep_ref[...]).astype(BF16)
    dm_ref[...] = grad
    sum_ref[0] = jnp.sum(grad.astype(F32), axis=0, keepdims=True)


def middle_call(om, w, bias, x, mod, top, keep, away, own):
    tokens, width = x.shape
    tiles = tokens // ROW
    rows = pl.BlockSpec((ROW, width), lambda i: (i, 0))
    half = pl.BlockSpec((ROW, width // 2), lambda i: (i, 0))
    fixed = pl.BlockSpec((width, width), lambda i: (0, 0))
    return call(
        middle_body,
        "middle",
        4 * tokens * width * width,
        26 * tokens * width,
        grid=(tiles,),
        in_specs=[
            pl.BlockSpec((width, ROW), lambda i: (0, i)),
            fixed,
            pl.BlockSpec((1, width), lambda i: (0, 0)),
            rows,
            pl.BlockSpec(mod.shape, lambda i: (0, 0, 0)),
            rows,
            pl.BlockSpec((ROW, 1), lambda i: (i, 0)),
            pl.BlockSpec((width, width // 2), lambda i: (0, 0)),
            pl.BlockSpec((width, width // 2), lambda i: (0, 0)),
        ],
        out_specs=[rows, rows, rows, half, half, rows, pl.BlockSpec((1, 1, width), lambda i: (i, 0, 0))],
        out_shape=[
            shaped((tokens, width), F32),
            shaped((tokens, width), F32),
            shaped((tokens, width), BF16),
            shaped((tokens, width // 2), BF16),
            shaped((tokens, width // 2), BF16),
            shaped((tokens, width), BF16),
            shaped((tiles, 1, width), F32),
        ],
    )(om, w, bias, x, mod, top, keep, away, own)


def hidden_body(h_ref, away_ref, dm_ref, w1_ref, b1_ref, w2_ref, *refs):
    g_ref, df_ref, sum_ref, send_ref = refs[-4:]
    first, second = math.sqrt(2.0 / math.pi), 0.044715
    pre = dot(h_ref[...], w1_ref[...]) + b1_ref[...]
    square = pre * pre
    tanh = jnp.tanh(first * pre * (1.0 + second * square))
    half = 0.5 * (1.0 + tanh)
    g_ref[...] = (pre * half).astype(BF16)
    slope = half + (0.5 * first) * pre * (1.0 - tanh * tanh) * (1.0 + (3.0 * second) * square)
    grad = (dot(dm_ref[...], w2_ref[...], NT) * slope).astype(BF16)
    df_ref[...] = grad
    sum_ref[...] = jnp.sum(grad.astype(F32), axis=0, keepdims=True)
    send_ref[...] = dot(away_ref[...], grad, TN)


def hidden_call(h, away, dm, w1, b1, w2, first, count, before):
    tokens, width = h.shape
    hidden = w1.shape[1]
    block = UNITS
    base = first // block
    full = pl.BlockSpec((tokens, width), lambda j: (0, 0))
    half = width // 2
    place = pl.BlockSpec(memory_space=pl.ANY)
    return call(
        hidden_body,
        "hidden",
        6 * tokens * width * count,
        6 * tokens * width + 4 * tokens * count + 8 * width * count,
        grid=(count // block,),
        in_specs=[
            full,
            pl.BlockSpec((tokens, half), lambda j: (0, 0)),
            full,
            pl.BlockSpec((width, block), lambda j: (0, base + j)),
            pl.BlockSpec((1, block), lambda j: (0, base + j)),
            pl.BlockSpec((block, width), lambda j: (base + j, 0)),
        ]
        + [place] * len(before),
        out_specs=[
            pl.BlockSpec((tokens, block), lambda j: (0, base + j)),
            pl.BlockSpec((tokens, block), lambda j: (0, base + j)),
            pl.BlockSpec((1, block), lambda j: (0, base + j)),
            pl.BlockSpec((half, block), lambda j: (0, j)),
        ],
        out_shape=[
            shaped((tokens, hidden), BF16),
            shaped((tokens, hidden), BF16),
            shaped((1, hidden), F32),
            shaped((half, count), F32),
        ],
        input_output_aliases={6 + n: n for n in range(len(before))},
    )(h, away, dm, w1, b1, w2, *before)


def shard_rows(spot_ref, g_ref, grad, made_ref):
    shards = spot_ref.shape[1]
    rows = g_ref.shape[1] // 2
    shard = g_ref.shape[1] // shards
    part = pl.program_id(0)
    for piece in range(2):
        made = dot(g_ref[:, piece * rows : (piece + 1) * rows], grad, TN)
        for number in range(shards // 2):
            made_ref[piece * (shards // 2) + number] = made[number * shard : (number + 1) * shard]

    def rows_of(place):
        return made_ref[spot_ref[part, place]]

    return rows_of


def rows_send_body(side_ref, spot_ref, g_ref, dm_ref, out_ref, made_ref):
    rows_of = shard_rows(spot_ref, g_ref, dm_ref[...], made_ref)
    for place in range(out_ref.shape[0]):
        out_ref[place] = rows_of(place)


def rows_send_call(side, spots, g, dm):
    tokens, hidden = g.shape
    width = dm.shape[1]
    half = hidden // 2
    shards = spots.shape[1]
    return call(
        rows_send_body,
        "rows_send",
        2 * tokens * half * width,
        2 * tokens * (half + width) + 4 * half * width,
        grid_spec=pltpu.PrefetchScalarGridSpec(
            num_scalar_prefetch=2,
            grid=(width // COLUMNS,),
            in_specs=[
                pl.BlockSpec((tokens, half), lambda j, side, spots: (0, side[0])),
                pl.BlockSpec((tokens, COLUMNS), lambda j, side, spots: (0, j)),
            ],
            out_specs=pl.BlockSpec((shards, half // shards, COLUMNS), lambda j, side, spots: (0, 0, j)),
            scratch_shapes=[pltpu.VMEM((shards, half // shards, COLUMNS), F32)],
        ),
        out_shape=shaped((shards, half // shards, width), F32),
    )(side, spots, g, dm)


def rows_keep_body(side_ref, spot_ref, g_ref, dm_ref, got_ref, *outs, bounds):
    *outs, made_ref = outs
    half = spot_ref.shape[1] // 2
    step = pl.program_id(0)
    rows_of = shard_rows(spot_ref, g_ref, dm_ref[...], made_ref)
    for part in range(len(bounds) - 1):

        @pl.when((step >= bounds[part]) & (step < bounds[part + 1]))
        def _():
            for place in range(half):
                outs[2 * part + 1][place] = rows_of(place) + got_ref[place]
                outs[2 * part][place] = rows_of(half + place) + got_ref[half + place]


def rows_keep_call(side, spots, g, dm, got, counts):
    tokens, hidden = g.shape
    width = dm.shape[1]
    half = hidden // 2
    steps, shards = spots.shape
    bounds = [sum(counts[:n]) for n in range(len(counts) + 1)]
    specs, shapes = [], []
    for part, count in enumerate(counts):
        for _ in range(2):
            specs.append(
                pl.BlockSpec(
                    (shards // 2, half // shards, COLUMNS),
                    functools.partial(
                        lambda j, side, spots, first, count: (0, 0, jnp.clip(j - first, 0, count - 1)),
                        first=bounds[part],
                        count=count,
                    ),
                )
            )
            shapes.append(shaped((shards // 2, half // shards, count * COLUMNS), F32))
    made = call(
        functools.partial(rows_keep_body, bounds=bounds),
        "rows_keep",
        2 * tokens * half * width,
        2 * tokens * (half + width) + 8 * half * width,
        grid_spec=pltpu.PrefetchScalarGridSpec(
            num_scalar_prefetch=2,
            grid=(steps,),
            in_specs=[
                pl.BlockSpec((tokens, half), lambda j, side, spots: (0, side[0])),
                pl.BlockSpec((tokens, COLUMNS), lambda j, side, spots: (0, j)),
                pl.BlockSpec((shards, half // shards, COLUMNS), lambda j, side, spots: (0, 0, j)),
            ],
            out_specs=specs,
            scratch_shapes=[pltpu.VMEM((shards, half // shards, COLUMNS), F32)],
        ),
        out_shape=shapes,
    )(side, spots, g, dm, got)
    made = [array.reshape(-1, array.shape[2]) for array in made]
    return list(zip(made[::2], made[1::2]))


def result_body(g_ref, w_ref, b_ref, x1_ref, mod_ref, top_ref, keep_ref, out_ref, sum_ref):
    tile = pl.program_id(0)
    branch = dot(g_ref[...], w_ref[...]) + b_ref[...]
    out_ref[...] = (x1_ref[...] + mod_ref[tile, 5:6] * keep_ref[...] * branch).astype(BF16)
    sum_ref[0] = jnp.sum(top_ref[...].astype(F32) * keep_ref[...] * branch, axis=0, keepdims=True)


def result_call(g, w, bias, x1, mod, top, keep):
    tokens, width = x1.shape
    hidden = g.shape[1]
    tiles = tokens // ROW
    rows = pl.BlockSpec((ROW, width), lambda i: (i, 0))
    return call(
        result_body,
        "result",
        2 * tokens * width * hidden,
        2 * tokens * hidden + 2 * hidden * width + 8 * tokens * width,
        grid=(tiles,),
        in_specs=[
            pl.BlockSpec((ROW, hidden), lambda i: (i, 0)),
            pl.BlockSpec((hidden, width), lambda i: (0, 0)),
            pl.BlockSpec((1, width), lambda i: (0, 0)),
            rows,
            pl.BlockSpec(mod.shape, lambda i: (0, 0, 0)),
            rows,
            pl.BlockSpec((ROW, 1), lambda i: (i, 0)),
        ],
        out_specs=[rows, pl.BlockSpec((1, 1, width), lambda i: (i, 0, 0))],
        out_shape=[shaped((tokens, width), BF16), shaped((tiles, 1, width), F32)],
    )(g, w, bias, x1, mod, top, keep)


def middle_back_body(
    df_ref, w1_ref, x1_ref, mod_ref, top_ref, a_ref, wp_ref,
    dx_ref, da_ref, do_ref, sum_ref,
):
    tile = pl.program_id(0)
    grad = dot(df_ref[...], w1_ref[...], NT)
    normal, inverse = normed(x1_ref[...])
    back = normed_back(grad * (1.0 + mod_ref[tile, 4:5]), normal, inverse)
    dx = top_ref[...].astype(F32) + back
    dx_ref[...] = dx
    da = (dx * mod_ref[tile, 2:3]).astype(BF16)
    da_ref[...] = da
    do_ref[...] = dot(wp_ref[...], da, NT).astype(BF16)
    sum_ref[0, 0:1] = jnp.sum(dx * a_ref[...], axis=0, keepdims=True)
    sum_ref[0, 1:2] = jnp.sum(grad, axis=0, keepdims=True)
    sum_ref[0, 2:3] = jnp.sum(grad * normal, axis=0, keepdims=True)
    sum_ref[0, 3:4] = jnp.sum(da.astype(F32), axis=0, keepdims=True)


def middle_back_call(df, w1, x1, mod, top, a, wp):
    tokens, width = x1.shape
    hidden = df.shape[1]
    tiles = tokens // ROW
    rows = pl.BlockSpec((ROW, width), lambda i: (i, 0))
    return call(
        middle_back_body,
        "middle_back",
        2 * tokens * width * (hidden + width),
        2 * tokens * hidden + 2 * hidden * width + 18 * tokens * width,
        grid=(tiles,),
        in_specs=[
            pl.BlockSpec((ROW, hidden), lambda i: (i, 0)),
            pl.BlockSpec((width, hidden), lambda i: (0, 0)),
            rows,
            pl.BlockSpec(mod.shape, lambda i: (0, 0, 0)),
            rows,
            rows,
            pl.BlockSpec((width, width), lambda i: (0, 0)),
        ],
        out_specs=[
            rows,
            rows,
            pl.BlockSpec((width, ROW), lambda i: (0, i)),
            pl.BlockSpec((1, 4, width), lambda i: (i, 0, 0)),
        ],
        out_shape=[
            shaped((tokens, width), F32),
            shaped((tokens, width), BF16),
            shaped((width, tokens), BF16),
            shaped((tiles, 4, width), F32),
        ],
    )(df, w1, x1, mod, top, a, wp)


class Wide:
    def __init__(self, *parts):
        self.parts = parts
        self.count = sum(rows for _, _, rows in parts)
        self.steps = 3

    def arrays(self):
        return [array for array, _, _ in self.parts]

    def specs(self, at):
        return [
            pl.BlockSpec(
                (1, rows, array.shape[2]),
                functools.partial(lambda j, at, index: (jnp.clip(j - at, 0, 2), index, 0), at=at, index=first // rows),
            )
            for array, first, rows in self.parts
        ]

    def value(self, refs):
        got = [ref[0] for ref in refs]
        return jnp.concatenate(got, axis=0) if len(got) > 1 else got[0]

    def product(self, left, right):
        return dot(left, right, TT)

    def sums(self, right):
        return dot(jnp.ones((8, right.shape[1]), BF16), right, NT)[:1]


class Plain:
    def __init__(self, array, first, count, steps):
        self.array, self.first, self.count, self.steps = array, first, count, steps

    def arrays(self):
        return [self.array]

    def specs(self, at):
        base, steps = self.first // self.count, self.steps
        index = functools.partial(
            lambda j, at, base, steps: (0, base + jnp.clip(j - at, 0, steps - 1)), at=at, base=base, steps=steps
        )
        return [pl.BlockSpec((self.array.shape[0], self.count), index)]

    def value(self, refs):
        return refs[0][...]

    def product(self, left, right):
        return dot(left, right, TN)

    def sums(self, right):
        return jnp.sum(right.astype(F32), axis=0, keepdims=True)


def columns_body(*refs, right, both):
    count = len(right.arrays())
    left_ref, right_refs, rest = refs[0], refs[1 : 1 + count], refs[1 + count :]
    value = right.value(right_refs)
    made = right.product(left_ref[...], value)
    if both:
        got_ref, send_ref, keep_ref = rest
        made = made + got_ref[...]
        rows = keep_ref.shape[0]
        send_ref[...] = made[rows:]
        keep_ref[...] = made[:rows]
    else:
        send_ref, sum_ref = rest
        send_ref[...] = made
        sum_ref[...] = right.sums(value)


def columns_call(left, right, name, got=None):
    tokens, half = left.shape
    count = right.count * right.steps
    both = got is not None
    wide = pl.BlockSpec((half, right.count), lambda j: (0, j))
    narrow = pl.BlockSpec((half // 2, right.count), lambda j: (0, j))
    made = call(
        functools.partial(columns_body, right=right, both=both),
        name,
        2 * tokens * half * count,
        2 * tokens * (count + half) + 8 * half * count,
        grid=(right.steps,),
        in_specs=[pl.BlockSpec(left.shape, lambda j: (0, 0)), *right.specs(0)] + [wide] * both,
        out_specs=[narrow, narrow] if both else [wide, pl.BlockSpec((1, right.count), lambda j: (0, j))],
        out_shape=[shaped((half // 2, count), F32)] * 2
        if both
        else [shaped((half, count), F32), shaped((1, count), F32)],
    )(left, *right.arrays(), *([got] if both else []))
    return [tuple(made)] if both else made


def pair_body(*refs, rights, both):
    counts = [len(right.arrays()) for right in rights]
    step = pl.program_id(0)
    at = 0
    rest = refs[2 + sum(counts) :]
    for number, (right, count) in enumerate(zip(rights, counts)):
        mine = (refs[at], *refs[at + 1 : at + 1 + count], *rest)
        when = step < rights[0].steps if number == 0 else step >= rights[0].steps
        pl.when(when)(functools.partial(columns_body, *mine, right=right, both=both))
        at += 1 + count


def pair_call(lefts, rights, name, got=None):
    tokens, half = lefts[0].shape
    step = rights[0].count
    steps = sum(right.steps for right in rights)
    count = step * steps
    both = got is not None
    wide = pl.BlockSpec((half, step), lambda j: (0, j))
    narrow = pl.BlockSpec((half // 2, step), lambda j: (0, j))
    operands, specs, at = [], [], 0
    for left, right in zip(lefts, rights):
        operands += [left, *right.arrays()]
        specs += [pl.BlockSpec(left.shape, lambda j: (0, 0)), *right.specs(at)]
        at += right.steps
    made = call(
        functools.partial(pair_body, rights=rights, both=both),
        name,
        2 * tokens * half * count,
        2 * tokens * (count + half) + 8 * half * count,
        grid=(steps,),
        in_specs=specs + [wide] * both,
        out_specs=[narrow, narrow] if both else [wide, pl.BlockSpec((1, step), lambda j: (0, j))],
        out_shape=[shaped((half // 2, count), F32)] * 2
        if both
        else [shaped((half, count), F32), shaped((1, count), F32)],
    )(*operands, *([got] if both else []))
    return [tuple(made)] if both else made


def moved_body(left_ref, away_ref, own_ref, left_away_ref, left_own_ref, *, dims):
    left = left_ref[...]
    left_away_ref[...] = dot(left, away_ref[...], dims).astype(BF16)
    left_own_ref[...] = dot(left, own_ref[...], dims).astype(BF16)


def moved_call(left, away, own, turned):
    width, half = away.shape
    tokens = left.shape[1] if turned else left.shape[0]
    block = tokens // 2
    fixed = pl.BlockSpec((width, half), lambda i: (0, 0))
    out = pl.BlockSpec((block, half), lambda i: (i, 0))
    side = pl.BlockSpec((width, block), lambda i: (0, i)) if turned else pl.BlockSpec((block, width), lambda i: (i, 0))
    return call(
        functools.partial(moved_body, dims=TN if turned else NN),
        "moved",
        2 * tokens * width * width,
        4 * tokens * width + 2 * width * width,
        grid=(2,),
        in_specs=[side, fixed, fixed],
        out_specs=[out] * 2,
        out_shape=[shaped((tokens, half), BF16)] * 2,
    )(left, away, own)


def first_back_body(low_ref, high_ref, w_ref, x_ref, mod_ref, dx_ref, out_ref, sum_ref):
    tile = pl.program_id(0)
    width = x_ref.shape[1]
    grad = None
    for third in range(3):
        rows = jnp.concatenate([low_ref[third], high_ref[third]], axis=0)
        part = dot(rows, w_ref[:, third * width : (third + 1) * width], TT)
        grad = part if grad is None else grad + part
    normal, inverse = normed(x_ref[...].astype(F32))
    out_ref[...] = dx_ref[...] + normed_back(grad * (1.0 + mod_ref[tile, 1:2]), normal, inverse)
    sum_ref[0, 0:1] = jnp.sum(grad, axis=0, keepdims=True)
    sum_ref[0, 1:2] = jnp.sum(grad * normal, axis=0, keepdims=True)


def first_back_call(low, high, w, x, mod, dx):
    tokens, width = x.shape
    wide = w.shape[1]
    half = pl.BlockSpec((3, width // 2, ROW), lambda i: (0, 0, i))
    tiles = tokens // ROW
    rows = pl.BlockSpec((ROW, width), lambda i: (i, 0))
    return call(
        first_back_body,
        "first_back",
        2 * tokens * width * wide,
        2 * tokens * wide + 2 * width * wide + 10 * tokens * width,
        grid=(tiles,),
        in_specs=[
            half,
            half,
            pl.BlockSpec((width, wide), lambda i: (0, 0)),
            rows,
            pl.BlockSpec(mod.shape, lambda i: (0, 0, 0)),
            rows,
        ],
        out_specs=[rows, pl.BlockSpec((1, 2, width), lambda i: (i, 0, 0))],
        out_shape=[shaped((tokens, width), F32), shaped((tiles, 2, width), F32)],
    )(low, high, w, x, mod, dx)


def payload_body(item_ref, one_ref, two_ref, gate_ref, dm_ref, df_ref, first_ref, last_ref, cond_ref, out_ref):
    tiles, _, width = one_ref.shape
    items = out_ref.shape[0]
    parts = [(one_ref, 0), (one_ref, 1), (two_ref, 0), (two_ref, 1), (two_ref, 2), (gate_ref, 0)]
    for number, (ref, row) in enumerate(parts):
        for item in range(items):
            total = jnp.zeros((1, width), F32)
            for tile in range(tiles):
                total = total + jnp.where(item_ref[tile] == item, ref[tile, row : row + 1], 0.0)
            out_ref[item : item + 1, number * width : (number + 1) * width] = total.astype(BF16).astype(F32)
    at = 6 * width
    hidden = df_ref.shape[1]
    out_ref[0:1, at : at + hidden // 2] = df_ref[:, : hidden // 2]
    out_ref[1:2, at : at + hidden // 2] = df_ref[:, hidden // 2 :]
    out_ref[2:3, at : at + width] = jnp.sum(dm_ref[:, 0], axis=0, keepdims=True)
    out_ref[2:3, at + width : at + 2 * width] = jnp.sum(two_ref[:, 3], axis=0, keepdims=True)
    rest = width - COLUMNS
    for number, third in enumerate((0, 2)):
        spot = at + number * width
        out_ref[3:4, spot : spot + COLUMNS] = first_ref[:, width + third * COLUMNS : width + (third + 1) * COLUMNS]
        out_ref[3:4, spot + COLUMNS : spot + width] = last_ref[:, third * rest : (third + 1) * rest]
    out_ref[:, at + 2 * width :] = cond_ref[...]


def payload_call(tile_item, *sums):
    items, width = sums[-1].shape
    out = shaped((items, 9 * width), F32)
    return call(
        payload_body,
        "payload",
        0,
        0,
        grid=(1,),
        in_specs=[pl.BlockSpec(memory_space=pltpu.SMEM)]
        + [pl.BlockSpec(part.shape, functools.partial(lambda j, rank: (0,) * rank, rank=part.ndim)) for part in sums],
        out_specs=pl.BlockSpec(out.shape, lambda j: (0, 0)),
        out_shape=out,
    )(tile_item, *sums)


def modulation_back_body(me_ref, *refs, count):
    part_refs, cond_refs, sum_refs = refs[:count], refs[count : 2 * count], refs[2 * count : 3 * count]
    label_ref, w_ref, grad_ref, bias_ref, table_ref, own_sums_ref, act_ref, own_ref, total_ref = refs[3 * count :]
    step = pl.program_id(0)
    width = act_ref.shape[1]
    shard = grad_ref.shape[0]
    items = own_sums_ref.shape[0]

    @pl.when(step == 0)
    def _():
        at = 0
        for cond_ref in cond_refs:
            cond = cond_ref[...]
            act_ref[at : at + cond.shape[0]] = (cond / (1.0 + jnp.exp(-cond))).astype(BF16)
            at += cond.shape[0]
        row = lax.broadcasted_iota(jnp.int32, (width, 128), 0)
        column = lax.broadcasted_iota(jnp.int32, (width, 128), 1)
        picked = jnp.where((column < shard) & (row == me_ref[0] * shard + column), 1.0, 0.0).astype(BF16)
        own_ref[...] = dot(act_ref[...], picked).astype(BF16)
        total_ref[...] = jnp.zeros_like(total_ref)
        sums = None
        for sum_ref in sum_refs:
            rows = sum_ref.shape[0]
            item = lax.broadcasted_iota(jnp.int32, (items, rows), 0)
            source = lax.broadcasted_iota(jnp.int32, (items, rows), 1)
            select = (lax.rem(source, jnp.full_like(source, items)) == item).astype(F32)
            part = dot(select, sum_ref[...], NN, HIGHEST)
            sums = part if sums is None else sums + part
        own_sums_ref[...] = sums

    mod = jnp.concatenate([part_ref[...] for part_ref in part_refs], axis=0)
    bias_ref[...] = jnp.sum(mod, axis=0, keepdims=True)
    mod = mod.astype(BF16)
    grad_ref[...] = dot(own_ref[...], mod, TN)[:shard]
    total_ref[...] += dot(w_ref[...], mod, NT)

    @pl.when(step == pl.num_programs(0) - 1)
    def _():
        cond = jnp.concatenate([cond_ref[...] for cond_ref in cond_refs], axis=0)
        gate = 1.0 / (1.0 + jnp.exp(-cond))
        grad = total_ref[...].T * (gate * (1.0 + cond * (1.0 - gate)))
        classes = table_ref.shape[0]
        select = (label_ref[...] == lax.broadcasted_iota(jnp.int32, (grad.shape[0], classes), 1)).astype(F32)
        table_ref[...] = dot(select, grad, TN, HIGHEST)


def modulation_back_call(me, parts, used, w, classes, shard, items):
    width, wide = w.shape
    block = 1152
    rows = sum(part.shape[0] for part in parts)
    extra = parts[0].shape[1] - wide - width
    at = (wide + extra) // width
    return call(
        functools.partial(modulation_back_body, count=len(parts)),
        "modulation_back",
        4 * rows * width * wide,
        2 * width * wide,
        grid=(wide // block,),
        in_specs=[
            pl.BlockSpec(memory_space=pltpu.SMEM),
            *[pl.BlockSpec((part.shape[0], block), lambda j: (0, j)) for part in parts],
            *[pl.BlockSpec((part.shape[0], width), lambda j: (0, at)) for part in parts],
            *[pl.BlockSpec((part.shape[0], extra), lambda j: (0, wide // extra)) for part in parts],
            pl.BlockSpec(used.shape, lambda j: (0, 0)),
            pl.BlockSpec((width, block), lambda j: (0, j)),
        ],
        out_specs=[
            pl.BlockSpec((shard, block), lambda j: (0, j)),
            pl.BlockSpec((1, block), lambda j: (0, j)),
            pl.BlockSpec((classes, width), lambda j: (0, 0)),
            pl.BlockSpec((items, extra), lambda j: (0, 0)),
        ],
        out_shape=[
            shaped((shard, wide), F32),
            shaped((1, wide), F32),
            shaped((classes, width), F32),
            shaped((items, extra), F32),
        ],
        scratch_shapes=[
            pltpu.VMEM((rows, width), BF16),
            pltpu.VMEM((rows, 128), BF16),
            pltpu.VMEM((width, rows), F32),
        ],
    )(me, *parts, *parts, *parts, used, w)


def add_body(*refs, plans):
    outs = refs[-len(plans) :]
    at = 0
    for out_ref, (count, first, rows) in zip(outs, plans):
        value = refs[at][first : first + rows]
        for term in range(1, count):
            value = value + refs[at + term][first : first + rows]
        out_ref[...] = value
        at += count


def add_call(jobs):
    steps = 1
    operands, specs, outs, shapes, plans = [], [], [], [], []
    moved = 0
    for terms, first, rows in jobs:
        wide = terms[0].shape[1]
        block = wide // steps
        for term in terms:
            size, index, at = rows, first // rows, 0
            while size % 8 and size < term.shape[0]:
                size, index, at = size * 2, 0, first
            operands.append(term)
            specs.append(pl.BlockSpec((size, block), functools.partial(lambda j, index: (index, j), index=index)))
        plans.append((len(terms), at, rows))
        outs.append(pl.BlockSpec((rows, block), lambda j: (0, j)))
        shapes.append(shaped((rows, wide), F32))
        moved += 4 * rows * wide * (len(terms) + 1)
    return call(
        functools.partial(add_body, plans=plans),
        "add",
        moved // 4,
        moved,
        grid=(steps,),
        in_specs=specs,
        out_specs=outs,
        out_shape=shapes,
    )(*operands)


def assemble_body(*refs, plans):
    outs = refs[-len(plans) :]
    for out_ref, (rows, blocks) in zip(outs, plans):
        for terms, source, target, count in blocks:
            value = refs[terms[0]][:rows, source : source + count]
            for term in terms[1:]:
                value = value + refs[term][:rows, source : source + count]
            out_ref[:, target : target + count] = value


def assemble_call(outputs):
    operands, specs, known, plans, shapes = [], [], {}, [], []
    for blocks in outputs:
        rows, target, made = blocks[0][0].rows, 0, []
        for chunk, source, count in blocks:
            if id(chunk) not in known:
                known[id(chunk)] = []
                for term in chunk.terms:
                    size = rows
                    while size % 8 and size < term.shape[0]:
                        size *= 2
                    known[id(chunk)].append(len(operands))
                    operands.append(term)
                    specs.append(pl.BlockSpec((size, term.shape[1]), lambda j: (0, 0)))
            made.append((known[id(chunk)], source, target, count))
            target += count
        plans.append((rows, made))
        shapes.append(shaped((rows, target), F32))
    return call(
        functools.partial(assemble_body, plans=plans),
        "assemble",
        0,
        sum(8 * 4 * shape.shape[0] * shape.shape[1] for shape in shapes),
        grid=(1,),
        in_specs=specs,
        out_specs=[pl.BlockSpec(shape.shape, lambda j: (0, 0)) for shape in shapes],
        out_shape=shapes,
    )(*operands)


def bit_order(bits, core, lead):
    order = list(range(bits))
    if bits >= 2 and core:
        order[:2] = [1, 0]
    if lead and lead < bits:
        order.remove(lead)
        order.insert(0, lead)
    return order


class Chunk:
    def __init__(self, send, kept, wait, lead):
        self.send, self.terms, self.wait, self.lead = send, [kept], wait, lead
        self.rows = kept.shape[0]
        self.stage = 0


class Spread:
    def __init__(self, rows):
        self.own, self.other = [rows], None
        self.stage = 0


class Flow:
    def __init__(self, bits):
        self.bits = bits
        self.fresh, self.crossing, self.chunks, self.last = [], [], [], []
        self.blocks = ([], [], [])
        self.spreads = []

    def emit(self, send, keep, store, waits=(0,), leads=(0,)):
        self.fresh.append((send, keep, store, waits, leads))

    def spread(self, rows):
        self.spreads.append(Spread(rows))
        return self.spreads[-1]

    def busy(self):
        moving = self.fresh or self.crossing or any(chunk.stage < self.bits for chunk in self.chunks)
        return moving or any(spread.stage <= self.bits for spread in self.spreads)

    def pairs(self, stage, lead):
        size = 1 << self.bits
        flips = [1 << bit_order(self.bits, core, lead)[stage] for core in range(2)]
        return [(core * size + i, core * size + (i ^ flips[core])) for core in range(2) for i in range(size)]

    def received(self, live):
        live, (cores, blocks, doubles) = lax.optimization_barrier((live, self.blocks))
        for spread, block in zip([spread for spread in self.spreads if spread.other is None and spread.stage], doubles):
            if spread.stage > self.bits:
                spread.other = block
            elif spread.stage == self.bits:
                spread.own += block
            else:
                spread.own = [jnp.concatenate(spread.own + block, axis=0)]
        jobs, waiting = [], []
        for chunk, block in zip(self.last, blocks):
            chunk.terms.append(block)
            if chunk.stage < self.bits:
                chunk.rows //= 2
                jobs.append((chunk.terms, chunk.rows, chunk.rows))
                waiting.append(chunk)
        for (_, keep, store, waits, leads), core in zip(self.crossing, cores):
            new = [Chunk(*pair, wait, lead) for pair, wait, lead in zip(keep(core), waits, leads)]
            store += new
            self.chunks += new
        for chunk, value in zip(waiting, add_call(jobs) if jobs else []):
            chunk.send = value
        return live

    def round(self, live):
        live = self.received(live)
        moving = [chunk for chunk in self.chunks if chunk.stage < self.bits and not chunk.wait]
        for chunk in self.chunks:
            chunk.wait = max(0, chunk.wait - 1)
        crossing, self.fresh = self.fresh, []
        doubling = [spread for spread in self.spreads if spread.stage <= self.bits]
        live, cores, sends, doubles = lax.optimization_barrier(
            (
                live,
                [entry[0] for entry in crossing],
                [chunk.send for chunk in moving],
                [spread.own for spread in doubling],
            )
        )
        blocks = []
        for chunk, send in zip(moving, sends):
            blocks.append(lax.ppermute(send, ("stream", "batch"), self.pairs(chunk.stage, chunk.lead)))
            chunk.stage += 1
        cores = [lax.ppermute(send, "stream", [(0, 1), (1, 0)]) for send in cores]
        for number, (spread, rows) in enumerate(zip(doubling, doubles)):
            spread.own = rows
            if spread.stage < self.bits:
                pairs = self.pairs(self.bits - 1 - spread.stage, 0)
                doubles[number] = [lax.ppermute(piece, ("stream", "batch"), pairs) for piece in rows]
            else:
                doubles[number] = [lax.ppermute(piece, "stream", [(0, 1), (1, 0)]) for piece in rows]
            spread.stage += 1
        self.crossing, self.last, self.blocks = crossing, moving, (cores, blocks, doubles)
        return live


def offsets_of(bits, side, lead):
    places = jnp.arange(1 << bits, dtype=jnp.int32)
    made = []
    for core in range(2):
        offset = jnp.zeros_like(places)
        for stage, bit in enumerate(bit_order(bits, core, lead)):
            offset = offset | (((places >> (bits - 1 - stage)) & 1) << bit)
        made.append(offset)
    return jnp.where(side == 0, made[0], made[1])


def places_of(bits, side, lead, offset):
    made = []
    for core in range(2):
        place = jnp.zeros_like(offset)
        for stage, bit in enumerate(bit_order(bits, core, lead)):
            place = place | (((offset >> bit) & 1) << (bits - 1 - stage))
        made.append(place)
    return jnp.where(side == 0, made[0], made[1])


def time_embed(steps_in, width):
    half_width = width // 2
    frequency = jnp.exp(-math.log(10000.0) * jnp.arange(half_width, dtype=F32) / half_width)
    angles = steps_in.astype(F32)[:, None] * frequency[None, :]
    return jnp.concatenate([jnp.cos(angles), jnp.sin(angles)], axis=1)


def per_device(
    tokens, segments, timesteps, labels, head_keep, token_keep, class_table, w_ada, b_ada,
    w_qkv, b_qv, w_proj, b_proj, w_fc1, b_fc1, w_fc2, b_fc2, out_grad, *, batch,
):
    x, top = tokens[0], out_grad[0]
    count, width = x.shape
    hidden = w_fc1.shape[1]
    heads = head_keep.shape[1]
    items = timesteps.shape[0]
    tiles = count // ROW
    groups = count // GROUP
    null_class = class_table.shape[0] - 1
    bits = batch.bit_length() - 1
    devices = 2 * batch
    stream = lax.axis_index("stream")
    index = lax.axis_index("batch")

    own_labels = lax.dynamic_slice_in_dim(labels, index * items, items)
    used = jnp.where(stream == 0, own_labels, null_class)
    cond = time_embed(timesteps, width) + jnp.take(class_table, used, axis=0).astype(F32)
    act = jax.nn.silu(cond).astype(BF16)
    modulation = dot(act, w_ada) + b_ada
    tile_item = segments[::ROW] - index * items
    chosen = tile_item[:, None] == jnp.arange(items, dtype=jnp.int32)[None, :]
    mod = jnp.sum(jnp.where(chosen[:, :, None], modulation[None], 0.0), axis=1)
    mod = mod.reshape(tiles, 6, width)
    tile_heads = jnp.sum(jnp.where(chosen[:, :, None], head_keep[None], 0), axis=1).astype(F32)
    head_columns = jnp.repeat(tile_heads.T, ROW, axis=1).reshape(heads, 1, count)
    keep = token_keep[0].astype(F32)[:, None]
    grouped = segments.reshape(groups, GROUP)
    flag = (grouped[:, 0] == grouped[:, -1]).astype(jnp.int32)

    shard = width // devices

    def picked(side):
        order = side * batch + (index ^ offsets_of(bits, side, 0))
        source = (order[:, None] * shard + jnp.arange(shard, dtype=jnp.int32)[None, :]).reshape(width // 2)
        return (jnp.arange(width, dtype=jnp.int32)[:, None] == source[None, :]).astype(BF16)

    def spots(side):
        return jnp.stack([index ^ offsets_of(bits, side, lead) for steps, lead in ROW_PARTS for _ in range(steps)])

    other = 1 - stream
    away, own = picked(other), picked(stream)

    bias_full = jnp.concatenate([b_qv[:width], jnp.zeros((width,), F32), b_qv[width:]])[None]
    h1, qkv = qkv_call(x, mod, w_qkv, bias_full)
    probs, mixed, om = attention_call(flag, qkv, head_columns, heads)
    a, x1, h2, h2_away, h2_own, dm, sum_dm = middle_call(om, w_proj, b_proj[None], x, mod, top, keep, away, own)

    flow = Flow(bits)
    fc1, fc2, wide = [], [], []

    filled, latest = (), {}
    for low, high in ((0, 2 * UNITS), (2 * UNITS, 5 * UNITS), (5 * UNITS, hidden)):
        *filled, send = hidden_call(h2, h2_away, dm, w_fc1, b_fc1[None], w_fc2, low, high - low, filled)
        latest["df"] = filled[1]

        def hidden_keep(got, low=low, count=high - low):
            return columns_call(h2_own, Plain(latest["df"], low, UNITS, count // UNITS), "hidden_keep", got)

        flow.emit(send, hidden_keep, fc1)
        h2, filled = flow.round((h2, filled))
        latest["df"] = filled[1]
    g, df, sum_df = filled

    rows_send = rows_send_call(other[None], spots(other), g, dm)
    flow.emit(
        rows_send.reshape(-1, width),
        lambda got: rows_keep_call(
            stream[None], spots(stream), g, dm, got.reshape(rows_send.shape), [steps for steps, _ in ROW_PARTS]
        ),
        fc2,
        [0] * len(ROW_PARTS),
        [lead for _, lead in ROW_PARTS],
    )
    om_away, om_own = moved_call(om, away, own, True)
    df, x1, om_away, om_own, h1 = flow.round((df, x1, om_away, om_own, h1))
    h1_away, h1_own = moved_call(h1, away, own, False)
    dx1, da, do, sums_two = middle_back_call(df, w_fc1, x1, mod, top, a, w_proj)

    me = stream * batch + index

    def used_labels(side):
        order = bit_order(bits, 0, 0)[::-1], bit_order(bits, 1, 0)[::-1]
        places = jnp.arange(batch, dtype=jnp.int32)
        offsets = [sum(((places >> n) & 1) << bit for n, bit in enumerate(bits_of)) for bits_of in order]
        from_device = index ^ jnp.where(side == 0, offsets[0], offsets[1])
        return jnp.where(side == 0, jnp.take(labels.reshape(batch, items), from_device, axis=0).reshape(-1), null_class)

    used_rows = jnp.concatenate([used_labels(stream), used_labels(other)])[:, None]
    dx1, da, do, sums_two, g, h1_away, h1_own = flow.round((dx1, da, do, sums_two, g, h1_away, h1_own))
    half = width // 2
    low = attention_back_call(flag, qkv, do, head_columns, probs, mixed, 0)
    rights = [Plain(da, 0, COLUMNS, width // COLUMNS), Wide((low, 0, COLUMNS))]
    send, first_sums = pair_call([om_away, h1_away], rights, "first_send")
    flow.emit(send, lambda got: pair_call([om_own, h1_own], rights, "first_keep", got), wide)
    result, sum_gate = result_call(g, w_fc2, b_fc2[None], x1, mod, top, keep)
    low, first_sums, result, sum_gate = flow.round((low, first_sums, result, sum_gate))
    high = attention_back_call(flag, qkv, do, head_columns, probs, mixed, 1)
    rest = Wide((low, COLUMNS, half - COLUMNS), (high, 0, half))
    send, high_sums = columns_call(h1_away, rest, "last_send")
    flow.emit(send, lambda got: columns_call(h1_own, rest, "last_keep", got), wide)
    low, high, dx1, high_sums = flow.round((low, high, dx1, high_sums))
    grad_tokens, sums_one = first_back_call(low, high, w_qkv, x, mod, dx1)

    spread = flow.spread(
        payload_call(tile_item, sums_one, sums_two, sum_gate, sum_dm, sum_df, first_sums, high_sums, cond)
    )
    while any(chunk.stage < bits for chunk in fc1 + fc2):
        result = flow.round(result)
    result = flow.round(result)
    grad_w_fc1, grad_w_fc2 = assemble_call(
        [[(chunk, 0, chunk.terms[0].shape[1]) for chunk in store] for store in (fc1, fc2)]
    )
    result, grad_w_fc1, grad_w_fc2 = flow.round((result, grad_w_fc1, grad_w_fc2))
    while any(chunk.stage < bits for chunk in wide):
        result = flow.round(result)
    result = flow.round(result)
    first, last = wide
    each = COLUMNS, width - COLUMNS
    blocks = [
        block
        for third in range(3)
        for block in ((first, width + third * each[0], each[0]), (last, third * each[1], each[1]))
    ]
    grad_w_proj, grad_w_qkv = assemble_call([[(first, 0, width)], blocks])
    while flow.busy():
        result = flow.round(result)
    result, grad_w_proj = flow.received((result, grad_w_proj))
    grad_w_ada, mod_sums, grad_table, own_sums = modulation_back_call(
        me[None], spread.own + spread.other, used_rows, w_ada, null_class + 1, shard, items
    )
    share = 6 * width // devices
    grad_b_ada = lax.dynamic_slice_in_dim(mod_sums[0], me * share, share)
    def own_sums_of(row, first, count):
        return lax.dynamic_slice(own_sums, (row, first), (1, count))[0]

    each = hidden // devices
    grad_b_fc1 = own_sums_of(me // (devices // 2), me % (devices // 2) * each, each)
    grad_b_fc2 = own_sums_of(2, me * shard, shard)
    grad_b_proj = own_sums_of(2, width + me * shard, shard)
    grad_b_qv = own_sums_of(3, me * 2 * shard, 2 * shard)

    return (
        result[None],
        grad_tokens[None],
        grad_table,
        grad_w_ada,
        grad_b_ada,
        grad_w_qkv,
        grad_b_qv,
        grad_w_proj,
        grad_b_proj,
        grad_w_fc1,
        grad_b_fc1,
        grad_w_fc2,
        grad_b_fc2,
    )


def solution(mesh):
    both = ("stream", "batch")
    return jax.shard_map(
        functools.partial(per_device, batch=mesh.shape["batch"]),
        mesh=mesh,
        in_specs=(
            P("stream", "batch", None),
            P("batch"),
            P("batch"),
            P(),
            P("batch", None),
            P("stream", "batch"),
            P(), P(), P(), P(), P(), P(), P(), P(), P(), P(), P(),
            P("stream", "batch", None),
        ),
        out_specs=(
            P("stream", "batch", None),
            P("stream", "batch", None),
            P(),
            P(both, None),
            P(both),
            P(both, None),
            P(both),
            P(both, None),
            P(both),
            P(both, None),
            P(both),
            P(both, None),
            P(both),
        ),
        check_vma=False,
    )
```

```python
import functools
import math

import jax
import jax.numpy as jnp
from jax import lax
from jax.experimental import pallas as pl
from jax.experimental.pallas import tpu as pltpu
from jax.sharding import PartitionSpec as P

F32 = jnp.float32
BF16 = jnp.bfloat16
HIGHEST = lax.Precision.HIGHEST
NORM_EPS = 1e-06
ROW_PARTS = ((2, 0), (1, 2))
ROW = 256
GROUP = 1024
NN = (((1,), (0,)), ((), ()))
NT = (((1,), (1,)), ((), ()))
TN = (((0,), (0,)), ((), ()))
TT = (((0,), (1,)), ((), ()))
VMEM_LIMIT = 60 << 20
COLUMNS = 384
UNITS = 512


def dot(left, right, dims=NN, precision=None):
    return lax.dot_general(left, right, dims, precision=precision, preferred_element_type=F32)


def call(body, name, flops, moved, **kwargs):
    return pl.pallas_call(
        body,
        name=name,
        compiler_params=pltpu.CompilerParams(vmem_limit_bytes=VMEM_LIMIT),
        cost_estimate=pl.CostEstimate(flops=flops // 8, bytes_accessed=moved // 8, transcendentals=0),
        **kwargs,
    )


def shaped(shape, kind):
    return jax.ShapeDtypeStruct(shape, kind)


def normed(values):
    centre = values - jnp.mean(values, axis=-1, keepdims=True)
    spread = jnp.mean(centre * centre, axis=-1, keepdims=True)
    inverse = lax.rsqrt(spread + NORM_EPS)
    return centre * inverse, inverse


def normed_back(grad, normal, inverse):
    first = jnp.mean(grad, axis=-1, keepdims=True)
    second = jnp.mean(grad * normal, axis=-1, keepdims=True)
    return inverse * (grad - first - normal * second)


def qkv_body(x_ref, mod_ref, w_ref, b_ref, h_ref, out_ref):
    @pl.when(pl.program_id(0) == 0)
    def _():
        for tile in range(x_ref.shape[0] // ROW):
            rows = slice(tile * ROW, tile * ROW + ROW)
            normal, _ = normed(x_ref[rows].astype(F32))
            h_ref[rows] = (normal * (1.0 + mod_ref[tile, 1:2]) + mod_ref[tile, 0:1]).astype(BF16)

    out_ref[...] = (dot(w_ref[...], h_ref[...], TT) + b_ref[...].T).astype(BF16)


def qkv_call(x, mod, w, bias):
    tokens, width = x.shape
    wide = w.shape[1]
    block = width
    return call(
        qkv_body,
        "qkv",
        2 * tokens * width * wide,
        2 * (2 * tokens * width + width * wide + tokens * wide),
        grid=(wide // block,),
        in_specs=[
            pl.BlockSpec((tokens, width), lambda j: (0, 0)),
            pl.BlockSpec(mod.shape, lambda j: (0, 0, 0)),
            pl.BlockSpec((width, block), lambda j: (0, j)),
            pl.BlockSpec((1, block), lambda j: (0, j)),
        ],
        out_specs=[
            pl.BlockSpec((tokens, width), lambda j: (0, 0)),
            pl.BlockSpec((block, tokens), lambda j: (j, 0)),
        ],
        out_shape=[shaped((tokens, width), BF16), shaped((wide, tokens), BF16)],
    )(x, mod, w, bias)


def heads_of(ref, head_width):
    values = ref[...].astype(F32)
    return [values[head * head_width : (head + 1) * head_width] for head in range(2)]


def attention_body(flag_ref, q_ref, k_ref, v_ref, keep_ref, p_ref, ot_ref, om_ref):
    head_width = ot_ref.shape[1]
    scale = math.log2(math.e) / math.sqrt(head_width)
    tokens = q_ref.shape[1]
    q, k = [[part.astype(BF16) for part in heads_of(ref, head_width)] for ref in (q_ref, k_ref)]
    v = [jnp.concatenate([part, jnp.ones((8, tokens), F32)], axis=0).astype(BF16) for part in heads_of(v_ref, head_width)]

    def part(head, first, count):
        rows = slice(first, first + count)
        scores = dot(k[head][:, rows], q[head][:, rows], TN)
        top = jnp.max(scores, axis=0, keepdims=True)
        expo = jnp.exp2((scores - top) * scale)
        total = jnp.sum(expo, axis=0, keepdims=True)
        probs = (expo * (1.0 / total)).astype(BF16)
        p_ref[head, rows, rows] = probs
        mixed = dot(v[head][:, rows], probs)
        ot_ref[head, :, rows] = mixed[:head_width] * (1.0 / mixed[head_width : head_width + 1])
        return mixed[:head_width] * keep_ref[head, :, rows]

    def run(count):
        made = [
            jnp.concatenate([part(head, at, count) for at in range(0, tokens, count)], axis=1) for head in range(2)
        ]
        om_ref[...] = jnp.concatenate(made, axis=0).astype(BF16)

    whole = flag_ref[pl.program_id(0)] == 1
    pl.when(whole)(lambda: run(tokens))
    pl.when(jnp.logical_not(whole))(lambda: run(ROW))


def attention_call(flag, qkv, keep, heads):
    wide, tokens = qkv.shape
    width = wide // 3
    head_width = width // heads
    groups = tokens // GROUP
    pairs = heads // 2
    rows = 2 * head_width

    def third(number):
        return pl.BlockSpec((rows, GROUP), functools.partial(lambda g, h, base: (base + h, g), base=number * pairs))

    return call(
        attention_body,
        "attention",
        2 * 2 * heads * tokens * GROUP * 256,
        2 * tokens * wide + 2 * heads * tokens * GROUP + 6 * tokens * width,
        grid=(groups, pairs),
        in_specs=[
            pl.BlockSpec(memory_space=pltpu.SMEM),
            third(0),
            third(1),
            third(2),
            pl.BlockSpec((2, 1, GROUP), lambda g, h: (h, 0, g)),
        ],
        out_specs=[
            pl.BlockSpec((2, GROUP, GROUP), lambda g, h: (h, 0, g)),
            pl.BlockSpec((2, head_width, GROUP), lambda g, h: (h, 0, g)),
            third(0),
        ],
        out_shape=[
            shaped((heads, GROUP, tokens), BF16),
            shaped((heads, head_width, tokens), F32),
            shaped((width, tokens), BF16),
        ],
    )(flag, qkv, qkv, qkv, keep)


def attention_back_body(flag_ref, q_ref, k_ref, v_ref, do_ref, keep_ref, p_ref, ot_ref, out_ref, ds_ref):
    head_width = ot_ref.shape[1]
    scale = 1.0 / math.sqrt(head_width)
    tokens = q_ref.shape[1]
    q, k, v = [[part.astype(BF16) for part in heads_of(ref, head_width)] for ref in (q_ref, k_ref, v_ref)]
    kept = [part * keep_ref[head] for head, part in enumerate(heads_of(do_ref, head_width))]
    do = [part.astype(BF16) for part in kept]
    delta = [jnp.sum(kept[head] * ot_ref[head], axis=0, keepdims=True) for head in range(2)]

    def run(count):
        made = [[], [], []]
        for head in range(2):
            row = [[], [], []]
            for first in range(0, tokens, count):
                rows = slice(first, first + count)
                dp = dot(v[head][:, rows], do[head][:, rows], TN)
                probs = p_ref[head, rows, rows].astype(F32)
                ds = (probs * (dp - delta[head][:, rows])).astype(BF16)
                if count == tokens:
                    ds_ref[head] = ds
                    ds = ds_ref[head]
                row[0].append(dot(k[head][:, rows], ds) * scale)
                row[1].append(dot(q[head][:, rows], ds, NT) * scale)
                row[2].append(dot(do[head][:, rows], p_ref[head, rows, rows], NT))
            for third in range(3):
                made[third].append(jnp.concatenate(row[third], axis=1))
        for third in range(3):
            out_ref[third] = jnp.concatenate(made[third], axis=0).astype(BF16)

    whole = flag_ref[pl.program_id(0)] == 1
    pl.when(whole)(lambda: run(tokens))
    pl.when(jnp.logical_not(whole))(lambda: run(ROW))


def attention_back_call(flag, qkv, do, keep, probs, mixed, part):
    wide, tokens = qkv.shape
    width = wide // 3
    heads, head_width = mixed.shape[:2]
    groups = tokens // GROUP
    pairs = heads // 4
    base = part * pairs
    rows = 2 * head_width

    def third(number):
        first = number * heads // 2 + base
        return pl.BlockSpec((rows, GROUP), functools.partial(lambda g, h, first: (first + h, g), first=first))

    return call(
        attention_back_body,
        "attention_back",
        2 * 2 * heads * tokens * GROUP * 256,
        2 * tokens * wide + heads * tokens * GROUP + 6 * tokens * width,
        grid=(groups, pairs),
        in_specs=[
            pl.BlockSpec(memory_space=pltpu.SMEM),
            third(0),
            third(1),
            third(2),
            third(0),
            pl.BlockSpec((2, 1, GROUP), lambda g, h: (base + h, 0, g)),
            pl.BlockSpec((2, GROUP, GROUP), lambda g, h: (base + h, 0, g)),
            pl.BlockSpec((2, head_width, GROUP), lambda g, h: (base + h, 0, g)),
        ],
        out_specs=pl.BlockSpec((3, rows, GROUP), lambda g, h: (0, h, g)),
        out_shape=shaped((3, width // 2, tokens), BF16),
        scratch_shapes=[pltpu.VMEM((2, GROUP, GROUP), BF16)],
    )(flag, qkv, qkv, qkv, do, keep, probs, mixed)


def middle_body(
    om_ref, w_ref, b_ref, x_ref, mod_ref, top_ref, keep_ref, away_ref, own_ref,
    a_ref, x1_ref, h_ref, h_away_ref, h_own_ref, dm_ref, sum_ref,
):
    tile = pl.program_id(0)
    branch = dot(om_ref[...], w_ref[...], TN) + b_ref[...]
    a_ref[...] = branch
    middle = x_ref[...].astype(F32) + mod_ref[tile, 2:3] * branch
    x1_ref[...] = middle
    normal, _ = normed(middle)
    hidden = (normal * (1.0 + mod_ref[tile, 4:5]) + mod_ref[tile, 3:4]).astype(BF16)
    h_ref[...] = hidden
    h_away_ref[...] = dot(hidden, away_ref[...]).astype(BF16)
    h_own_ref[...] = dot(hidden, own_ref[...]).astype(BF16)
    grad = (top_ref[...].astype(F32) * mod_ref[tile, 5:6] * keep_ref[...]).astype(BF16)
    dm_ref[...] = grad
    sum_ref[0] = jnp.sum(grad.astype(F32), axis=0, keepdims=True)


def middle_call(om, w, bias, x, mod, top, keep, away, own):
    tokens, width = x.shape
    tiles = tokens // ROW
    rows = pl.BlockSpec((ROW, width), lambda i: (i, 0))
    half = pl.BlockSpec((ROW, width // 2), lambda i: (i, 0))
    fixed = pl.BlockSpec((width, width), lambda i: (0, 0))
    return call(
        middle_body,
        "middle",
        4 * tokens * width * width,
        26 * tokens * width,
        grid=(tiles,),
        in_specs=[
            pl.BlockSpec((width, ROW), lambda i: (0, i)),
            fixed,
            pl.BlockSpec((1, width), lambda i: (0, 0)),
            rows,
            pl.BlockSpec(mod.shape, lambda i: (0, 0, 0)),
            rows,
            pl.BlockSpec((ROW, 1), lambda i: (i, 0)),
            pl.BlockSpec((width, width // 2), lambda i: (0, 0)),
            pl.BlockSpec((width, width // 2), lambda i: (0, 0)),
        ],
        out_specs=[rows, rows, rows, half, half, rows, pl.BlockSpec((1, 1, width), lambda i: (i, 0, 0))],
        out_shape=[
            shaped((tokens, width), F32),
            shaped((tokens, width), F32),
            shaped((tokens, width), BF16),
            shaped((tokens, width // 2), BF16),
            shaped((tokens, width // 2), BF16),
            shaped((tokens, width), BF16),
            shaped((tiles, 1, width), F32),
        ],
    )(om, w, bias, x, mod, top, keep, away, own)


def hidden_body(h_ref, away_ref, dm_ref, w1_ref, b1_ref, w2_ref, *refs):
    g_ref, df_ref, sum_ref, send_ref = refs[-4:]
    first, second = math.sqrt(2.0 / math.pi), 0.044715
    pre = dot(h_ref[...], w1_ref[...]) + b1_ref[...]
    square = pre * pre
    tanh = jnp.tanh(first * pre * (1.0 + second * square))
    half = 0.5 * (1.0 + tanh)
    g_ref[...] = (pre * half).astype(BF16)
    slope = half + (0.5 * first) * pre * (1.0 - tanh * tanh) * (1.0 + (3.0 * second) * square)
    grad = (dot(dm_ref[...], w2_ref[...], NT) * slope).astype(BF16)
    df_ref[...] = grad
    sum_ref[...] = jnp.sum(grad.astype(F32), axis=0, keepdims=True)
    send_ref[...] = dot(away_ref[...], grad, TN)


def hidden_call(h, away, dm, w1, b1, w2, first, count, before):
    tokens, width = h.shape
    hidden = w1.shape[1]
    block = UNITS
    base = first // block
    full = pl.BlockSpec((tokens, width), lambda j: (0, 0))
    half = width // 2
    place = pl.BlockSpec(memory_space=pl.ANY)
    return call(
        hidden_body,
        "hidden",
        6 * tokens * width * count,
        6 * tokens * width + 4 * tokens * count + 8 * width * count,
        grid=(count // block,),
        in_specs=[
            full,
            pl.BlockSpec((tokens, half), lambda j: (0, 0)),
            full,
            pl.BlockSpec((width, block), lambda j: (0, base + j)),
            pl.BlockSpec((1, block), lambda j: (0, base + j)),
            pl.BlockSpec((block, width), lambda j: (base + j, 0)),
        ]
        + [place] * len(before),
        out_specs=[
            pl.BlockSpec((tokens, block), lambda j: (0, base + j)),
            pl.BlockSpec((tokens, block), lambda j: (0, base + j)),
            pl.BlockSpec((1, block), lambda j: (0, base + j)),
            pl.BlockSpec((half, block), lambda j: (0, j)),
        ],
        out_shape=[
            shaped((tokens, hidden), BF16),
            shaped((tokens, hidden), BF16),
            shaped((1, hidden), F32),
            shaped((half, count), F32),
        ],
        input_output_aliases={6 + n: n for n in range(len(before))},
    )(h, away, dm, w1, b1, w2, *before)


def shard_rows(spot_ref, g_ref, grad, made_ref):
    shards = spot_ref.shape[1]
    rows = g_ref.shape[1] // 2
    shard = g_ref.shape[1] // shards
    part = pl.program_id(0)
    for piece in range(2):
        made = dot(g_ref[:, piece * rows : (piece + 1) * rows], grad, TN)
        for number in range(shards // 2):
            made_ref[piece * (shards // 2) + number] = made[number * shard : (number + 1) * shard]

    def rows_of(place):
        return made_ref[spot_ref[part, place]]

    return rows_of


def rows_send_body(side_ref, spot_ref, g_ref, dm_ref, out_ref, made_ref):
    rows_of = shard_rows(spot_ref, g_ref, dm_ref[...], made_ref)
    for place in range(out_ref.shape[0]):
        out_ref[place] = rows_of(place)


def rows_send_call(side, spots, g, dm):
    tokens, hidden = g.shape
    width = dm.shape[1]
    half = hidden // 2
    shards = spots.shape[1]
    return call(
        rows_send_body,
        "rows_send",
        2 * tokens * half * width,
        2 * tokens * (half + width) + 4 * half * width,
        grid_spec=pltpu.PrefetchScalarGridSpec(
            num_scalar_prefetch=2,
            grid=(width // COLUMNS,),
            in_specs=[
                pl.BlockSpec((tokens, half), lambda j, side, spots: (0, side[0])),
                pl.BlockSpec((tokens, COLUMNS), lambda j, side, spots: (0, j)),
            ],
            out_specs=pl.BlockSpec((shards, half // shards, COLUMNS), lambda j, side, spots: (0, 0, j)),
            scratch_shapes=[pltpu.VMEM((shards, half // shards, COLUMNS), F32)],
        ),
        out_shape=shaped((shards, half // shards, width), F32),
    )(side, spots, g, dm)


def rows_keep_body(side_ref, spot_ref, g_ref, dm_ref, got_ref, *outs, bounds):
    *outs, made_ref = outs
    half = spot_ref.shape[1] // 2
    step = pl.program_id(0)
    rows_of = shard_rows(spot_ref, g_ref, dm_ref[...], made_ref)
    for part in range(len(bounds) - 1):

        @pl.when((step >= bounds[part]) & (step < bounds[part + 1]))
        def _():
            for place in range(half):
                outs[2 * part + 1][place] = rows_of(place) + got_ref[place]
                outs[2 * part][place] = rows_of(half + place) + got_ref[half + place]


def rows_keep_call(side, spots, g, dm, got, counts):
    tokens, hidden = g.shape
    width = dm.shape[1]
    half = hidden // 2
    steps, shards = spots.shape
    bounds = [sum(counts[:n]) for n in range(len(counts) + 1)]
    specs, shapes = [], []
    for part, count in enumerate(counts):
        for _ in range(2):
            specs.append(
                pl.BlockSpec(
                    (shards // 2, half // shards, COLUMNS),
                    functools.partial(
                        lambda j, side, spots, first, count: (0, 0, jnp.clip(j - first, 0, count - 1)),
                        first=bounds[part],
                        count=count,
                    ),
                )
            )
            shapes.append(shaped((shards // 2, half // shards, count * COLUMNS), F32))
    made = call(
        functools.partial(rows_keep_body, bounds=bounds),
        "rows_keep",
        2 * tokens * half * width,
        2 * tokens * (half + width) + 8 * half * width,
        grid_spec=pltpu.PrefetchScalarGridSpec(
            num_scalar_prefetch=2,
            grid=(steps,),
            in_specs=[
                pl.BlockSpec((tokens, half), lambda j, side, spots: (0, side[0])),
                pl.BlockSpec((tokens, COLUMNS), lambda j, side, spots: (0, j)),
                pl.BlockSpec((shards, half // shards, COLUMNS), lambda j, side, spots: (0, 0, j)),
            ],
            out_specs=specs,
            scratch_shapes=[pltpu.VMEM((shards, half // shards, COLUMNS), F32)],
        ),
        out_shape=shapes,
    )(side, spots, g, dm, got)
    made = [array.reshape(-1, array.shape[2]) for array in made]
    return list(zip(made[::2], made[1::2]))


def result_body(g_ref, w_ref, b_ref, x1_ref, mod_ref, top_ref, keep_ref, out_ref, sum_ref):
    tile = pl.program_id(0)
    branch = dot(g_ref[...], w_ref[...]) + b_ref[...]
    out_ref[...] = (x1_ref[...] + mod_ref[tile, 5:6] * keep_ref[...] * branch).astype(BF16)
    sum_ref[0] = jnp.sum(top_ref[...].astype(F32) * keep_ref[...] * branch, axis=0, keepdims=True)


def result_call(g, w, bias, x1, mod, top, keep):
    tokens, width = x1.shape
    hidden = g.shape[1]
    tiles = tokens // ROW
    rows = pl.BlockSpec((ROW, width), lambda i: (i, 0))
    return call(
        result_body,
        "result",
        2 * tokens * width * hidden,
        2 * tokens * hidden + 2 * hidden * width + 8 * tokens * width,
        grid=(tiles,),
        in_specs=[
            pl.BlockSpec((ROW, hidden), lambda i: (i, 0)),
            pl.BlockSpec((hidden, width), lambda i: (0, 0)),
            pl.BlockSpec((1, width), lambda i: (0, 0)),
            rows,
            pl.BlockSpec(mod.shape, lambda i: (0, 0, 0)),
            rows,
            pl.BlockSpec((ROW, 1), lambda i: (i, 0)),
        ],
        out_specs=[rows, pl.BlockSpec((1, 1, width), lambda i: (i, 0, 0))],
        out_shape=[shaped((tokens, width), BF16), shaped((tiles, 1, width), F32)],
    )(g, w, bias, x1, mod, top, keep)


def middle_back_body(
    df_ref, w1_ref, x1_ref, mod_ref, top_ref, a_ref, wp_ref,
    dx_ref, da_ref, do_ref, sum_ref,
):
    tile = pl.program_id(0)
    grad = dot(df_ref[...], w1_ref[...], NT)
    normal, inverse = normed(x1_ref[...])
    back = normed_back(grad * (1.0 + mod_ref[tile, 4:5]), normal, inverse)
    dx = top_ref[...].astype(F32) + back
    dx_ref[...] = dx
    da = (dx * mod_ref[tile, 2:3]).astype(BF16)
    da_ref[...] = da
    do_ref[...] = dot(wp_ref[...], da, NT).astype(BF16)
    sum_ref[0, 0:1] = jnp.sum(dx * a_ref[...], axis=0, keepdims=True)
    sum_ref[0, 1:2] = jnp.sum(grad, axis=0, keepdims=True)
    sum_ref[0, 2:3] = jnp.sum(grad * normal, axis=0, keepdims=True)
    sum_ref[0, 3:4] = jnp.sum(da.astype(F32), axis=0, keepdims=True)


def middle_back_call(df, w1, x1, mod, top, a, wp):
    tokens, width = x1.shape
    hidden = df.shape[1]
    tiles = tokens // ROW
    rows = pl.BlockSpec((ROW, width), lambda i: (i, 0))
    return call(
        middle_back_body,
        "middle_back",
        2 * tokens * width * (hidden + width),
        2 * tokens * hidden + 2 * hidden * width + 18 * tokens * width,
        grid=(tiles,),
        in_specs=[
            pl.BlockSpec((ROW, hidden), lambda i: (i, 0)),
            pl.BlockSpec((width, hidden), lambda i: (0, 0)),
            rows,
            pl.BlockSpec(mod.shape, lambda i: (0, 0, 0)),
            rows,
            rows,
            pl.BlockSpec((width, width), lambda i: (0, 0)),
        ],
        out_specs=[
            rows,
            rows,
            pl.BlockSpec((width, ROW), lambda i: (0, i)),
            pl.BlockSpec((1, 4, width), lambda i: (i, 0, 0)),
        ],
        out_shape=[
            shaped((tokens, width), F32),
            shaped((tokens, width), BF16),
            shaped((width, tokens), BF16),
            shaped((tiles, 4, width), F32),
        ],
    )(df, w1, x1, mod, top, a, wp)


class Wide:
    def __init__(self, *parts):
        self.parts = parts
        self.count = sum(rows for _, _, rows in parts)
        self.steps = 3

    def arrays(self):
        return [array for array, _, _ in self.parts]

    def specs(self, at):
        return [
            pl.BlockSpec(
                (1, rows, array.shape[2]),
                functools.partial(lambda j, at, index: (jnp.clip(j - at, 0, 2), index, 0), at=at, index=first // rows),
            )
            for array, first, rows in self.parts
        ]

    def value(self, refs):
        got = [ref[0] for ref in refs]
        return jnp.concatenate(got, axis=0) if len(got) > 1 else got[0]

    def product(self, left, right):
        return dot(left, right, TT)

    def sums(self, right):
        return dot(jnp.ones((8, right.shape[1]), BF16), right, NT)[:1]


class Plain:
    def __init__(self, array, first, count, steps):
        self.array, self.first, self.count, self.steps = array, first, count, steps

    def arrays(self):
        return [self.array]

    def specs(self, at):
        base, steps = self.first // self.count, self.steps
        index = functools.partial(
            lambda j, at, base, steps: (0, base + jnp.clip(j - at, 0, steps - 1)), at=at, base=base, steps=steps
        )
        return [pl.BlockSpec((self.array.shape[0], self.count), index)]

    def value(self, refs):
        return refs[0][...]

    def product(self, left, right):
        return dot(left, right, TN)

    def sums(self, right):
        return jnp.sum(right.astype(F32), axis=0, keepdims=True)


def columns_body(*refs, right, both):
    count = len(right.arrays())
    left_ref, right_refs, rest = refs[0], refs[1 : 1 + count], refs[1 + count :]
    value = right.value(right_refs)
    made = right.product(left_ref[...], value)
    if both:
        got_ref, send_ref, keep_ref = rest
        made = made + got_ref[...]
        rows = keep_ref.shape[0]
        send_ref[...] = made[rows:]
        keep_ref[...] = made[:rows]
    else:
        send_ref, sum_ref = rest
        send_ref[...] = made
        sum_ref[...] = right.sums(value)


def columns_call(left, right, name, got=None):
    tokens, half = left.shape
    count = right.count * right.steps
    both = got is not None
    wide = pl.BlockSpec((half, right.count), lambda j: (0, j))
    narrow = pl.BlockSpec((half // 2, right.count), lambda j: (0, j))
    made = call(
        functools.partial(columns_body, right=right, both=both),
        name,
        2 * tokens * half * count,
        2 * tokens * (count + half) + 8 * half * count,
        grid=(right.steps,),
        in_specs=[pl.BlockSpec(left.shape, lambda j: (0, 0)), *right.specs(0)] + [wide] * both,
        out_specs=[narrow, narrow] if both else [wide, pl.BlockSpec((1, right.count), lambda j: (0, j))],
        out_shape=[shaped((half // 2, count), F32)] * 2
        if both
        else [shaped((half, count), F32), shaped((1, count), F32)],
    )(left, *right.arrays(), *([got] if both else []))
    return [tuple(made)] if both else made


def pair_body(*refs, rights, both):
    counts = [len(right.arrays()) for right in rights]
    step = pl.program_id(0)
    at = 0
    rest = refs[2 + sum(counts) :]
    for number, (right, count) in enumerate(zip(rights, counts)):
        mine = (refs[at], *refs[at + 1 : at + 1 + count], *rest)
        when = step < rights[0].steps if number == 0 else step >= rights[0].steps
        pl.when(when)(functools.partial(columns_body, *mine, right=right, both=both))
        at += 1 + count


def pair_call(lefts, rights, name, got=None):
    tokens, half = lefts[0].shape
    step = rights[0].count
    steps = sum(right.steps for right in rights)
    count = step * steps
    both = got is not None
    wide = pl.BlockSpec((half, step), lambda j: (0, j))
    narrow = pl.BlockSpec((half // 2, step), lambda j: (0, j))
    operands, specs, at = [], [], 0
    for left, right in zip(lefts, rights):
        operands += [left, *right.arrays()]
        specs += [pl.BlockSpec(left.shape, lambda j: (0, 0)), *right.specs(at)]
        at += right.steps
    made = call(
        functools.partial(pair_body, rights=rights, both=both),
        name,
        2 * tokens * half * count,
        2 * tokens * (count + half) + 8 * half * count,
        grid=(steps,),
        in_specs=specs + [wide] * both,
        out_specs=[narrow, narrow] if both else [wide, pl.BlockSpec((1, step), lambda j: (0, j))],
        out_shape=[shaped((half // 2, count), F32)] * 2
        if both
        else [shaped((half, count), F32), shaped((1, count), F32)],
    )(*operands, *([got] if both else []))
    return [tuple(made)] if both else made


def moved_body(left_ref, away_ref, own_ref, left_away_ref, left_own_ref, *, dims):
    left = left_ref[...]
    left_away_ref[...] = dot(left, away_ref[...], dims).astype(BF16)
    left_own_ref[...] = dot(left, own_ref[...], dims).astype(BF16)


def moved_call(left, away, own, turned):
    width, half = away.shape
    tokens = left.shape[1] if turned else left.shape[0]
    block = tokens // 2
    fixed = pl.BlockSpec((width, half), lambda i: (0, 0))
    out = pl.BlockSpec((block, half), lambda i: (i, 0))
    side = pl.BlockSpec((width, block), lambda i: (0, i)) if turned else pl.BlockSpec((block, width), lambda i: (i, 0))
    return call(
        functools.partial(moved_body, dims=TN if turned else NN),
        "moved",
        2 * tokens * width * width,
        4 * tokens * width + 2 * width * width,
        grid=(2,),
        in_specs=[side, fixed, fixed],
        out_specs=[out] * 2,
        out_shape=[shaped((tokens, half), BF16)] * 2,
    )(left, away, own)


def first_back_body(low_ref, high_ref, w_ref, x_ref, mod_ref, dx_ref, out_ref, sum_ref):
    tile = pl.program_id(0)
    width = x_ref.shape[1]
    grad = None
    for third in range(3):
        rows = jnp.concatenate([low_ref[third], high_ref[third]], axis=0)
        part = dot(rows, w_ref[:, third * width : (third + 1) * width], TT)
        grad = part if grad is None else grad + part
    normal, inverse = normed(x_ref[...].astype(F32))
    out_ref[...] = dx_ref[...] + normed_back(grad * (1.0 + mod_ref[tile, 1:2]), normal, inverse)
    sum_ref[0, 0:1] = jnp.sum(grad, axis=0, keepdims=True)
    sum_ref[0, 1:2] = jnp.sum(grad * normal, axis=0, keepdims=True)


def first_back_call(low, high, w, x, mod, dx):
    tokens, width = x.shape
    wide = w.shape[1]
    half = pl.BlockSpec((3, width // 2, ROW), lambda i: (0, 0, i))
    tiles = tokens // ROW
    rows = pl.BlockSpec((ROW, width), lambda i: (i, 0))
    return call(
        first_back_body,
        "first_back",
        2 * tokens * width * wide,
        2 * tokens * wide + 2 * width * wide + 10 * tokens * width,
        grid=(tiles,),
        in_specs=[
            half,
            half,
            pl.BlockSpec((width, wide), lambda i: (0, 0)),
            rows,
            pl.BlockSpec(mod.shape, lambda i: (0, 0, 0)),
            rows,
        ],
        out_specs=[rows, pl.BlockSpec((1, 2, width), lambda i: (i, 0, 0))],
        out_shape=[shaped((tokens, width), F32), shaped((tiles, 2, width), F32)],
    )(low, high, w, x, mod, dx)


def payload_body(item_ref, one_ref, two_ref, gate_ref, dm_ref, df_ref, first_ref, last_ref, cond_ref, out_ref):
    tiles, _, width = one_ref.shape
    items = out_ref.shape[0]
    parts = [(one_ref, 0), (one_ref, 1), (two_ref, 0), (two_ref, 1), (two_ref, 2), (gate_ref, 0)]
    for number, (ref, row) in enumerate(parts):
        for item in range(items):
            total = jnp.zeros((1, width), F32)
            for tile in range(tiles):
                total = total + jnp.where(item_ref[tile] == item, ref[tile, row : row + 1], 0.0)
            out_ref[item : item + 1, number * width : (number + 1) * width] = total.astype(BF16).astype(F32)
    at = 6 * width
    hidden = df_ref.shape[1]
    out_ref[0:1, at : at + hidden // 2] = df_ref[:, : hidden // 2]
    out_ref[1:2, at : at + hidden // 2] = df_ref[:, hidden // 2 :]
    out_ref[2:3, at : at + width] = jnp.sum(dm_ref[:, 0], axis=0, keepdims=True)
    out_ref[2:3, at + width : at + 2 * width] = jnp.sum(two_ref[:, 3], axis=0, keepdims=True)
    rest = width - COLUMNS
    for number, third in enumerate((0, 2)):
        spot = at + number * width
        out_ref[3:4, spot : spot + COLUMNS] = first_ref[:, width + third * COLUMNS : width + (third + 1) * COLUMNS]
        out_ref[3:4, spot + COLUMNS : spot + width] = last_ref[:, third * rest : (third + 1) * rest]
    out_ref[:, at + 2 * width :] = cond_ref[...]


def payload_call(tile_item, *sums):
    items, width = sums[-1].shape
    out = shaped((items, 9 * width), F32)
    return call(
        payload_body,
        "payload",
        0,
        0,
        grid=(1,),
        in_specs=[pl.BlockSpec(memory_space=pltpu.SMEM)]
        + [pl.BlockSpec(part.shape, functools.partial(lambda j, rank: (0,) * rank, rank=part.ndim)) for part in sums],
        out_specs=pl.BlockSpec(out.shape, lambda j: (0, 0)),
        out_shape=out,
    )(tile_item, *sums)


def modulation_back_body(me_ref, *refs, count):
    part_refs, cond_refs, sum_refs = refs[:count], refs[count : 2 * count], refs[2 * count : 3 * count]
    label_ref, w_ref, grad_ref, bias_ref, table_ref, own_sums_ref, act_ref, own_ref, total_ref = refs[3 * count :]
    step = pl.program_id(0)
    width = act_ref.shape[1]
    shard = grad_ref.shape[0]
    items = own_sums_ref.shape[0]

    @pl.when(step == 0)
    def _():
        at = 0
        for cond_ref in cond_refs:
            cond = cond_ref[...]
            act_ref[at : at + cond.shape[0]] = (cond / (1.0 + jnp.exp(-cond))).astype(BF16)
            at += cond.shape[0]
        row = lax.broadcasted_iota(jnp.int32, (width, 128), 0)
        column = lax.broadcasted_iota(jnp.int32, (width, 128), 1)
        picked = jnp.where((column < shard) & (row == me_ref[0] * shard + column), 1.0, 0.0).astype(BF16)
        own_ref[...] = dot(act_ref[...], picked).astype(BF16)
        total_ref[...] = jnp.zeros_like(total_ref)
        sums = None
        for sum_ref in sum_refs:
            rows = sum_ref.shape[0]
            item = lax.broadcasted_iota(jnp.int32, (items, rows), 0)
            source = lax.broadcasted_iota(jnp.int32, (items, rows), 1)
            select = (lax.rem(source, jnp.full_like(source, items)) == item).astype(F32)
            part = dot(select, sum_ref[...], NN, HIGHEST)
            sums = part if sums is None else sums + part
        own_sums_ref[...] = sums

    mod = jnp.concatenate([part_ref[...] for part_ref in part_refs], axis=0)
    bias_ref[...] = jnp.sum(mod, axis=0, keepdims=True)
    mod = mod.astype(BF16)
    grad_ref[...] = dot(own_ref[...], mod, TN)[:shard]
    total_ref[...] += dot(w_ref[...], mod, NT)

    @pl.when(step == pl.num_programs(0) - 1)
    def _():
        cond = jnp.concatenate([cond_ref[...] for cond_ref in cond_refs], axis=0)
        gate = 1.0 / (1.0 + jnp.exp(-cond))
        grad = total_ref[...].T * (gate * (1.0 + cond * (1.0 - gate)))
        classes = table_ref.shape[0]
        select = (label_ref[...] == lax.broadcasted_iota(jnp.int32, (grad.shape[0], classes), 1)).astype(F32).astype(BF16)
        high = grad.astype(BF16)
        rest = grad - high.astype(F32)
        middle = rest.astype(BF16)
        low = (rest - middle.astype(F32)).astype(BF16)
        table_ref[...] = dot(select, high, TN) + (dot(select, middle, TN) + dot(select, low, TN))


def modulation_back_call(me, parts, used, w, classes, shard, items):
    width, wide = w.shape
    block = 2 * width
    rows = sum(part.shape[0] for part in parts)
    extra = parts[0].shape[1] - wide - width
    at = (wide + extra) // width
    return call(
        functools.partial(modulation_back_body, count=len(parts)),
        "modulation_back",
        4 * rows * width * wide,
        2 * width * wide,
        grid=(wide // block,),
        in_specs=[
            pl.BlockSpec(memory_space=pltpu.SMEM),
            *[pl.BlockSpec((part.shape[0], block), lambda j: (0, j)) for part in parts],
            *[pl.BlockSpec((part.shape[0], width), lambda j: (0, at)) for part in parts],
            *[pl.BlockSpec((part.shape[0], extra), lambda j: (0, wide // extra)) for part in parts],
            pl.BlockSpec(used.shape, lambda j: (0, 0)),
            pl.BlockSpec((width, block), lambda j: (0, j)),
        ],
        out_specs=[
            pl.BlockSpec((shard, block), lambda j: (0, j)),
            pl.BlockSpec((1, block), lambda j: (0, j)),
            pl.BlockSpec((classes, width), lambda j: (0, 0)),
            pl.BlockSpec((items, extra), lambda j: (0, 0)),
        ],
        out_shape=[
            shaped((shard, wide), F32),
            shaped((1, wide), F32),
            shaped((classes, width), F32),
            shaped((items, extra), F32),
        ],
        scratch_shapes=[
            pltpu.VMEM((rows, width), BF16),
            pltpu.VMEM((rows, 128), BF16),
            pltpu.VMEM((width, rows), F32),
        ],
    )(me, *parts, *parts, *parts, used, w)


def add_body(*refs, plans):
    outs = refs[-len(plans) :]
    at = 0
    for out_ref, (count, first, rows) in zip(outs, plans):
        value = refs[at][first : first + rows]
        for term in range(1, count):
            value = value + refs[at + term][first : first + rows]
        out_ref[...] = value
        at += count


def add_call(jobs):
    steps = 1
    operands, specs, outs, shapes, plans = [], [], [], [], []
    moved = 0
    for terms, first, rows in jobs:
        wide = terms[0].shape[1]
        block = wide // steps
        for term in terms:
            size, index, at = rows, first // rows, 0
            while size % 8 and size < term.shape[0]:
                size, index, at = size * 2, 0, first
            operands.append(term)
            specs.append(pl.BlockSpec((size, block), functools.partial(lambda j, index: (index, j), index=index)))
        plans.append((len(terms), at, rows))
        outs.append(pl.BlockSpec((rows, block), lambda j: (0, j)))
        shapes.append(shaped((rows, wide), F32))
        moved += 4 * rows * wide * (len(terms) + 1)
    return call(
        functools.partial(add_body, plans=plans),
        "add",
        moved // 4,
        moved,
        grid=(steps,),
        in_specs=specs,
        out_specs=outs,
        out_shape=shapes,
    )(*operands)


def assemble_body(*refs, plans):
    outs = refs[-len(plans) :]
    for out_ref, (rows, blocks) in zip(outs, plans):
        for terms, source, target, count in blocks:
            value = refs[terms[0]][:rows, source : source + count]
            for term in terms[1:]:
                value = value + refs[term][:rows, source : source + count]
            out_ref[:, target : target + count] = value


def assemble_call(outputs):
    operands, specs, known, plans, shapes = [], [], {}, [], []
    for blocks in outputs:
        rows, target, made = blocks[0][0].rows, 0, []
        for chunk, source, count in blocks:
            if id(chunk) not in known:
                known[id(chunk)] = []
                for term in chunk.terms:
                    size = rows
                    while size % 8 and size < term.shape[0]:
                        size *= 2
                    known[id(chunk)].append(len(operands))
                    operands.append(term)
                    specs.append(pl.BlockSpec((size, term.shape[1]), lambda j: (0, 0)))
            made.append((known[id(chunk)], source, target, count))
            target += count
        plans.append((rows, made))
        shapes.append(shaped((rows, target), F32))
    return call(
        functools.partial(assemble_body, plans=plans),
        "assemble",
        0,
        sum(8 * 4 * shape.shape[0] * shape.shape[1] for shape in shapes),
        grid=(1,),
        in_specs=specs,
        out_specs=[pl.BlockSpec(shape.shape, lambda j: (0, 0)) for shape in shapes],
        out_shape=shapes,
    )(*operands)


def bit_order(bits, core, lead):
    order = list(range(bits))
    if bits >= 2 and core:
        order[:2] = [1, 0]
    if lead and lead < bits:
        order.remove(lead)
        order.insert(0, lead)
    return order


class Chunk:
    def __init__(self, send, kept, wait, lead):
        self.send, self.terms, self.wait, self.lead = send, [kept], wait, lead
        self.rows = kept.shape[0]
        self.stage = 0


class Spread:
    def __init__(self, rows):
        self.own, self.other = [rows], None
        self.stage = 0


class Flow:
    def __init__(self, bits):
        self.bits = bits
        self.fresh, self.crossing, self.chunks, self.last = [], [], [], []
        self.blocks = ([], [], [])
        self.spreads = []

    def emit(self, send, keep, store, waits=(0,), leads=(0,)):
        self.fresh.append((send, keep, store, waits, leads))

    def spread(self, rows):
        self.spreads.append(Spread(rows))
        return self.spreads[-1]

    def busy(self):
        moving = self.fresh or self.crossing or any(chunk.stage < self.bits for chunk in self.chunks)
        return moving or any(spread.stage <= self.bits for spread in self.spreads)

    def pairs(self, stage, lead):
        size = 1 << self.bits
        flips = [1 << bit_order(self.bits, core, lead)[stage] for core in range(2)]
        return [(core * size + i, core * size + (i ^ flips[core])) for core in range(2) for i in range(size)]

    def received(self, live):
        live, (cores, blocks, doubles) = lax.optimization_barrier((live, self.blocks))
        for spread, block in zip([spread for spread in self.spreads if spread.other is None and spread.stage], doubles):
            if spread.stage > self.bits:
                spread.other = block
            elif spread.stage == self.bits:
                spread.own += block
            else:
                spread.own = [jnp.concatenate(spread.own + block, axis=0)]
        jobs, waiting = [], []
        for chunk, block in zip(self.last, blocks):
            chunk.terms.append(block)
            if chunk.stage < self.bits:
                chunk.rows //= 2
                jobs.append((chunk.terms, chunk.rows, chunk.rows))
                waiting.append(chunk)
        for (_, keep, store, waits, leads), core in zip(self.crossing, cores):
            new = [Chunk(*pair, wait, lead) for pair, wait, lead in zip(keep(core), waits, leads)]
            store += new
            self.chunks += new
        for chunk, value in zip(waiting, add_call(jobs) if jobs else []):
            chunk.send = value
        return live

    def round(self, live):
        live = self.received(live)
        moving = [chunk for chunk in self.chunks if chunk.stage < self.bits and not chunk.wait]
        for chunk in self.chunks:
            chunk.wait = max(0, chunk.wait - 1)
        crossing, self.fresh = self.fresh, []
        doubling = [spread for spread in self.spreads if spread.stage <= self.bits]
        live, cores, sends, doubles = lax.optimization_barrier(
            (
                live,
                [entry[0] for entry in crossing],
                [chunk.send for chunk in moving],
                [spread.own for spread in doubling],
            )
        )
        blocks = []
        for chunk, send in zip(moving, sends):
            blocks.append(lax.ppermute(send, ("stream", "batch"), self.pairs(chunk.stage, chunk.lead)))
            chunk.stage += 1
        cores = [lax.ppermute(send, "stream", [(0, 1), (1, 0)]) for send in cores]
        for number, (spread, rows) in enumerate(zip(doubling, doubles)):
            spread.own = rows
            if spread.stage < self.bits:
                pairs = self.pairs(self.bits - 1 - spread.stage, 0)
                doubles[number] = [lax.ppermute(piece, ("stream", "batch"), pairs) for piece in rows]
            else:
                doubles[number] = [lax.ppermute(piece, "stream", [(0, 1), (1, 0)]) for piece in rows]
            spread.stage += 1
        self.crossing, self.last, self.blocks = crossing, moving, (cores, blocks, doubles)
        return live


def offsets_of(bits, side, lead):
    places = jnp.arange(1 << bits, dtype=jnp.int32)
    made = []
    for core in range(2):
        offset = jnp.zeros_like(places)
        for stage, bit in enumerate(bit_order(bits, core, lead)):
            offset = offset | (((places >> (bits - 1 - stage)) & 1) << bit)
        made.append(offset)
    return jnp.where(side == 0, made[0], made[1])


def places_of(bits, side, lead, offset):
    made = []
    for core in range(2):
        place = jnp.zeros_like(offset)
        for stage, bit in enumerate(bit_order(bits, core, lead)):
            place = place | (((offset >> bit) & 1) << (bits - 1 - stage))
        made.append(place)
    return jnp.where(side == 0, made[0], made[1])


def time_embed(steps_in, width):
    half_width = width // 2
    frequency = jnp.exp(-math.log(10000.0) * jnp.arange(half_width, dtype=F32) / half_width)
    angles = steps_in.astype(F32)[:, None] * frequency[None, :]
    return jnp.concatenate([jnp.cos(angles), jnp.sin(angles)], axis=1)


def per_device(
    tokens, segments, timesteps, labels, head_keep, token_keep, class_table, w_ada, b_ada,
    w_qkv, b_qv, w_proj, b_proj, w_fc1, b_fc1, w_fc2, b_fc2, out_grad, *, batch,
):
    x, top = tokens[0], out_grad[0]
    count, width = x.shape
    hidden = w_fc1.shape[1]
    heads = head_keep.shape[1]
    items = timesteps.shape[0]
    tiles = count // ROW
    groups = count // GROUP
    null_class = class_table.shape[0] - 1
    bits = batch.bit_length() - 1
    devices = 2 * batch
    stream = lax.axis_index("stream")
    index = lax.axis_index("batch")

    own_labels = lax.dynamic_slice_in_dim(labels, index * items, items)
    used = jnp.where(stream == 0, own_labels, null_class)
    cond = time_embed(timesteps, width) + jnp.take(class_table, used, axis=0).astype(F32)
    act = jax.nn.silu(cond).astype(BF16)
    modulation = dot(act, w_ada) + b_ada
    tile_item = segments[::ROW] - index * items
    chosen = tile_item[:, None] == jnp.arange(items, dtype=jnp.int32)[None, :]
    mod = jnp.sum(jnp.where(chosen[:, :, None], modulation[None], 0.0), axis=1)
    mod = mod.reshape(tiles, 6, width)
    tile_heads = jnp.sum(jnp.where(chosen[:, :, None], head_keep[None], 0), axis=1).astype(F32)
    head_columns = jnp.repeat(tile_heads.T, ROW, axis=1).reshape(heads, 1, count)
    keep = token_keep[0].astype(F32)[:, None]
    grouped = segments.reshape(groups, GROUP)
    flag = (grouped[:, 0] == grouped[:, -1]).astype(jnp.int32)

    shard = width // devices

    def picked(side):
        order = side * batch + (index ^ offsets_of(bits, side, 0))
        source = (order[:, None] * shard + jnp.arange(shard, dtype=jnp.int32)[None, :]).reshape(width // 2)
        return (jnp.arange(width, dtype=jnp.int32)[:, None] == source[None, :]).astype(BF16)

    def spots(side):
        return jnp.stack([index ^ offsets_of(bits, side, lead) for steps, lead in ROW_PARTS for _ in range(steps)])

    other = 1 - stream
    away, own = picked(other), picked(stream)

    bias_full = jnp.concatenate([b_qv[:width], jnp.zeros((width,), F32), b_qv[width:]])[None]
    h1, qkv = qkv_call(x, mod, w_qkv, bias_full)
    probs, mixed, om = attention_call(flag, qkv, head_columns, heads)
    a, x1, h2, h2_away, h2_own, dm, sum_dm = middle_call(om, w_proj, b_proj[None], x, mod, top, keep, away, own)

    flow = Flow(bits)
    fc1, fc2, wide = [], [], []

    filled, latest = (), {}
    for low, high in ((0, 2 * UNITS), (2 * UNITS, 5 * UNITS), (5 * UNITS, hidden)):
        *filled, send = hidden_call(h2, h2_away, dm, w_fc1, b_fc1[None], w_fc2, low, high - low, filled)
        latest["df"] = filled[1]

        def hidden_keep(got, low=low, count=high - low):
            return columns_call(h2_own, Plain(latest["df"], low, UNITS, count // UNITS), "hidden_keep", got)

        flow.emit(send, hidden_keep, fc1)
        h2, filled = flow.round((h2, filled))
        latest["df"] = filled[1]
    g, df, sum_df = filled

    rows_send = rows_send_call(other[None], spots(other), g, dm)
    flow.emit(
        rows_send.reshape(-1, width),
        lambda got: rows_keep_call(
            stream[None], spots(stream), g, dm, got.reshape(rows_send.shape), [steps for steps, _ in ROW_PARTS]
        ),
        fc2,
        [0] * len(ROW_PARTS),
        [lead for _, lead in ROW_PARTS],
    )
    om_away, om_own = moved_call(om, away, own, True)
    df, x1, om_away, om_own, h1 = flow.round((df, x1, om_away, om_own, h1))
    h1_away, h1_own = moved_call(h1, away, own, False)
    dx1, da, do, sums_two = middle_back_call(df, w_fc1, x1, mod, top, a, w_proj)

    me = stream * batch + index

    def used_labels(side):
        order = bit_order(bits, 0, 0)[::-1], bit_order(bits, 1, 0)[::-1]
        places = jnp.arange(batch, dtype=jnp.int32)
        offsets = [sum(((places >> n) & 1) << bit for n, bit in enumerate(bits_of)) for bits_of in order]
        from_device = index ^ jnp.where(side == 0, offsets[0], offsets[1])
        return jnp.where(side == 0, jnp.take(labels.reshape(batch, items), from_device, axis=0).reshape(-1), null_class)

    used_rows = jnp.concatenate([used_labels(stream), used_labels(other)])[:, None]
    dx1, da, do, sums_two, g, h1_away, h1_own = flow.round((dx1, da, do, sums_two, g, h1_away, h1_own))
    half = width // 2
    low = attention_back_call(flag, qkv, do, head_columns, probs, mixed, 0)
    rights = [Plain(da, 0, COLUMNS, width // COLUMNS), Wide((low, 0, COLUMNS))]
    send, first_sums = pair_call([om_away, h1_away], rights, "first_send")
    flow.emit(send, lambda got: pair_call([om_own, h1_own], rights, "first_keep", got), wide)
    result, sum_gate = result_call(g, w_fc2, b_fc2[None], x1, mod, top, keep)
    low, first_sums, result, sum_gate = flow.round((low, first_sums, result, sum_gate))
    high = attention_back_call(flag, qkv, do, head_columns, probs, mixed, 1)
    rest = Wide((low, COLUMNS, half - COLUMNS), (high, 0, half))
    send, high_sums = columns_call(h1_away, rest, "last_send")
    flow.emit(send, lambda got: columns_call(h1_own, rest, "last_keep", got), wide)
    low, high, dx1, high_sums = flow.round((low, high, dx1, high_sums))
    grad_tokens, sums_one = first_back_call(low, high, w_qkv, x, mod, dx1)

    spread = flow.spread(
        payload_call(tile_item, sums_one, sums_two, sum_gate, sum_dm, sum_df, first_sums, high_sums, cond)
    )
    while any(chunk.stage < bits for chunk in fc1 + fc2):
        result = flow.round(result)
    result = flow.round(result)
    grad_w_fc1, grad_w_fc2 = assemble_call(
        [[(chunk, 0, chunk.terms[0].shape[1]) for chunk in store] for store in (fc1, fc2)]
    )
    result, grad_w_fc1, grad_w_fc2, used_rows = flow.round((result, grad_w_fc1, grad_w_fc2, used_rows))
    while any(chunk.stage < bits for chunk in wide):
        result = flow.round(result)
    result = flow.round(result)
    first, last = wide
    each = COLUMNS, width - COLUMNS
    blocks = [
        block
        for third in range(3)
        for block in ((first, width + third * each[0], each[0]), (last, third * each[1], each[1]))
    ]
    grad_w_proj, grad_w_qkv = assemble_call([[(first, 0, width)], blocks])
    while flow.busy():
        result = flow.round(result)
    result, grad_w_proj = flow.received((result, grad_w_proj))
    grad_w_ada, mod_sums, grad_table, own_sums = modulation_back_call(
        me[None], spread.own + spread.other, used_rows, w_ada, null_class + 1, shard, items
    )
    share = 6 * width // devices
    grad_b_ada = lax.dynamic_slice_in_dim(mod_sums[0], me * share, share)
    def own_sums_of(row, first, count):
        return lax.dynamic_slice(own_sums, (row, first), (1, count))[0]

    each = hidden // devices
    grad_b_fc1 = own_sums_of(me // (devices // 2), me % (devices // 2) * each, each)
    grad_b_fc2 = own_sums_of(2, me * shard, shard)
    grad_b_proj = own_sums_of(2, width + me * shard, shard)
    grad_b_qv = own_sums_of(3, me * 2 * shard, 2 * shard)

    return (
        result[None],
        grad_tokens[None],
        grad_table,
        grad_w_ada,
        grad_b_ada,
        grad_w_qkv,
        grad_b_qv,
        grad_w_proj,
        grad_b_proj,
        grad_w_fc1,
        grad_b_fc1,
        grad_w_fc2,
        grad_b_fc2,
    )


def solution(mesh):
    both = ("stream", "batch")
    return jax.shard_map(
        functools.partial(per_device, batch=mesh.shape["batch"]),
        mesh=mesh,
        in_specs=(
            P("stream", "batch", None),
            P("batch"),
            P("batch"),
            P(),
            P("batch", None),
            P("stream", "batch"),
            P(), P(), P(), P(), P(), P(), P(), P(), P(), P(), P(),
            P("stream", "batch", None),
        ),
        out_specs=(
            P("stream", "batch", None),
            P("stream", "batch", None),
            P(),
            P(both, None),
            P(both),
            P(both, None),
            P(both),
            P(both, None),
            P(both),
            P(both, None),
            P(both),
            P(both, None),
            P(both),
        ),
        check_vma=False,
    )
```

```python
import functools
import math

import jax
import jax.numpy as jnp
from jax import lax
from jax.experimental import pallas as pl
from jax.experimental.pallas import tpu as pltpu
from jax.sharding import PartitionSpec as P

F32 = jnp.float32
BF16 = jnp.bfloat16
HIGHEST = lax.Precision.HIGHEST
NORM_EPS = 1e-06
ROW_PARTS = ((2, 0), (1, 2))
ROW = 256
GROUP = 1024
NN = (((1,), (0,)), ((), ()))
NT = (((1,), (1,)), ((), ()))
TN = (((0,), (0,)), ((), ()))
TT = (((0,), (1,)), ((), ()))
VMEM_LIMIT = 60 << 20
COLUMNS = 384
UNITS = 512


def dot(left, right, dims=NN, precision=None):
    return lax.dot_general(left, right, dims, precision=precision, preferred_element_type=F32)


def call(body, name, flops, moved, **kwargs):
    return pl.pallas_call(
        body,
        name=name,
        compiler_params=pltpu.CompilerParams(vmem_limit_bytes=VMEM_LIMIT),
        cost_estimate=pl.CostEstimate(flops=flops // 8, bytes_accessed=moved // 8, transcendentals=0),
        **kwargs,
    )


def shaped(shape, kind):
    return jax.ShapeDtypeStruct(shape, kind)


def normed(values):
    centre = values - jnp.mean(values, axis=-1, keepdims=True)
    spread = jnp.mean(centre * centre, axis=-1, keepdims=True)
    inverse = lax.rsqrt(spread + NORM_EPS)
    return centre * inverse, inverse


def normed_back(grad, normal, inverse):
    first = jnp.mean(grad, axis=-1, keepdims=True)
    second = jnp.mean(grad * normal, axis=-1, keepdims=True)
    return inverse * (grad - first - normal * second)


def qkv_body(x_ref, mod_ref, w_ref, b_ref, h_ref, out_ref):
    @pl.when(pl.program_id(0) == 0)
    def _():
        for tile in range(x_ref.shape[0] // ROW):
            rows = slice(tile * ROW, tile * ROW + ROW)
            normal, _ = normed(x_ref[rows].astype(F32))
            h_ref[rows] = (normal * (1.0 + mod_ref[tile, 1:2]) + mod_ref[tile, 0:1]).astype(BF16)

    out_ref[...] = (dot(w_ref[...], h_ref[...], TT) + b_ref[...].T).astype(BF16)


def qkv_call(x, mod, w, bias):
    tokens, width = x.shape
    wide = w.shape[1]
    block = width
    return call(
        qkv_body,
        "qkv",
        2 * tokens * width * wide,
        2 * (2 * tokens * width + width * wide + tokens * wide),
        grid=(wide // block,),
        in_specs=[
            pl.BlockSpec((tokens, width), lambda j: (0, 0)),
            pl.BlockSpec(mod.shape, lambda j: (0, 0, 0)),
            pl.BlockSpec((width, block), lambda j: (0, j)),
            pl.BlockSpec((1, block), lambda j: (0, j)),
        ],
        out_specs=[
            pl.BlockSpec((tokens, width), lambda j: (0, 0)),
            pl.BlockSpec((block, tokens), lambda j: (j, 0)),
        ],
        out_shape=[shaped((tokens, width), BF16), shaped((wide, tokens), BF16)],
    )(x, mod, w, bias)


def heads_of(ref, head_width):
    values = ref[...].astype(F32)
    return [values[head * head_width : (head + 1) * head_width] for head in range(2)]


def attention_body(flag_ref, q_ref, k_ref, v_ref, keep_ref, p_ref, ot_ref, om_ref):
    head_width = ot_ref.shape[1]
    scale = math.log2(math.e) / math.sqrt(head_width)
    tokens = q_ref.shape[1]
    q, k = [[part.astype(BF16) for part in heads_of(ref, head_width)] for ref in (q_ref, k_ref)]
    v = [jnp.concatenate([part, jnp.ones((8, tokens), F32)], axis=0).astype(BF16) for part in heads_of(v_ref, head_width)]

    def part(head, first, count):
        rows = slice(first, first + count)
        scores = dot(k[head][:, rows], q[head][:, rows], TN)
        top = jnp.max(scores, axis=0, keepdims=True)
        expo = jnp.exp2((scores - top) * scale)
        total = jnp.sum(expo, axis=0, keepdims=True)
        probs = (expo * (1.0 / total)).astype(BF16)
        p_ref[head, rows, rows] = probs
        mixed = dot(v[head][:, rows], probs)
        ot_ref[head, :, rows] = mixed[:head_width] * (1.0 / mixed[head_width : head_width + 1])
        return mixed[:head_width] * keep_ref[head, :, rows]

    def run(count):
        made = [
            jnp.concatenate([part(head, at, count) for at in range(0, tokens, count)], axis=1) for head in range(2)
        ]
        om_ref[...] = jnp.concatenate(made, axis=0).astype(BF16)

    whole = flag_ref[pl.program_id(0)] == 1
    pl.when(whole)(lambda: run(tokens))
    pl.when(jnp.logical_not(whole))(lambda: run(ROW))


def attention_call(flag, qkv, keep, heads):
    wide, tokens = qkv.shape
    width = wide // 3
    head_width = width // heads
    groups = tokens // GROUP
    pairs = heads // 2
    rows = 2 * head_width

    def third(number):
        return pl.BlockSpec((rows, GROUP), functools.partial(lambda g, h, base: (base + h, g), base=number * pairs))

    return call(
        attention_body,
        "attention",
        2 * 2 * heads * tokens * GROUP * 256,
        2 * tokens * wide + 2 * heads * tokens * GROUP + 6 * tokens * width,
        grid=(groups, pairs),
        in_specs=[
            pl.BlockSpec(memory_space=pltpu.SMEM),
            third(0),
            third(1),
            third(2),
            pl.BlockSpec((2, 1, GROUP), lambda g, h: (h, 0, g)),
        ],
        out_specs=[
            pl.BlockSpec((2, GROUP, GROUP), lambda g, h: (h, 0, g)),
            pl.BlockSpec((2, head_width, GROUP), lambda g, h: (h, 0, g)),
            third(0),
        ],
        out_shape=[
            shaped((heads, GROUP, tokens), BF16),
            shaped((heads, head_width, tokens), F32),
            shaped((width, tokens), BF16),
        ],
    )(flag, qkv, qkv, qkv, keep)


def attention_back_body(flag_ref, q_ref, k_ref, v_ref, do_ref, keep_ref, p_ref, ot_ref, out_ref, ds_ref):
    head_width = ot_ref.shape[1]
    scale = 1.0 / math.sqrt(head_width)
    tokens = q_ref.shape[1]
    q, k, v = [[part.astype(BF16) for part in heads_of(ref, head_width)] for ref in (q_ref, k_ref, v_ref)]
    kept = [part * keep_ref[head] for head, part in enumerate(heads_of(do_ref, head_width))]
    do = [part.astype(BF16) for part in kept]
    delta = [jnp.sum(kept[head] * ot_ref[head], axis=0, keepdims=True) for head in range(2)]

    def run(count):
        made = [[], [], []]
        for head in range(2):
            row = [[], [], []]
            for first in range(0, tokens, count):
                rows = slice(first, first + count)
                dp = dot(v[head][:, rows], do[head][:, rows], TN)
                probs = p_ref[head, rows, rows].astype(F32)
                ds = (probs * (dp - delta[head][:, rows])).astype(BF16)
                if count == tokens:
                    ds_ref[head] = ds
                    ds = ds_ref[head]
                row[0].append(dot(k[head][:, rows], ds) * scale)
                row[1].append(dot(q[head][:, rows], ds, NT) * scale)
                row[2].append(dot(do[head][:, rows], p_ref[head, rows, rows], NT))
            for third in range(3):
                made[third].append(jnp.concatenate(row[third], axis=1))
        for third in range(3):
            out_ref[third] = jnp.concatenate(made[third], axis=0).astype(BF16)

    whole = flag_ref[pl.program_id(0)] == 1
    pl.when(whole)(lambda: run(tokens))
    pl.when(jnp.logical_not(whole))(lambda: run(ROW))


def attention_back_call(flag, qkv, do, keep, probs, mixed, part):
    wide, tokens = qkv.shape
    width = wide // 3
    heads, head_width = mixed.shape[:2]
    groups = tokens // GROUP
    pairs = heads // 4
    base = part * pairs
    rows = 2 * head_width

    def third(number):
        first = number * heads // 2 + base
        return pl.BlockSpec((rows, GROUP), functools.partial(lambda g, h, first: (first + h, g), first=first))

    return call(
        attention_back_body,
        "attention_back",
        2 * 2 * heads * tokens * GROUP * 256,
        2 * tokens * wide + heads * tokens * GROUP + 6 * tokens * width,
        grid=(groups, pairs),
        in_specs=[
            pl.BlockSpec(memory_space=pltpu.SMEM),
            third(0),
            third(1),
            third(2),
            third(0),
            pl.BlockSpec((2, 1, GROUP), lambda g, h: (base + h, 0, g)),
            pl.BlockSpec((2, GROUP, GROUP), lambda g, h: (base + h, 0, g)),
            pl.BlockSpec((2, head_width, GROUP), lambda g, h: (base + h, 0, g)),
        ],
        out_specs=pl.BlockSpec((3, rows, GROUP), lambda g, h: (0, h, g)),
        out_shape=shaped((3, width // 2, tokens), BF16),
        scratch_shapes=[pltpu.VMEM((2, GROUP, GROUP), BF16)],
    )(flag, qkv, qkv, qkv, do, keep, probs, mixed)


def middle_body(
    om_ref, w_ref, b_ref, x_ref, mod_ref, top_ref, keep_ref, away_ref, own_ref,
    a_ref, x1_ref, h_ref, h_away_ref, h_own_ref, dm_ref, sum_ref,
):
    tile = pl.program_id(0)
    branch = dot(om_ref[...], w_ref[...], TN) + b_ref[...]
    a_ref[...] = branch
    middle = x_ref[...].astype(F32) + mod_ref[tile, 2:3] * branch
    x1_ref[...] = middle
    normal, _ = normed(middle)
    hidden = (normal * (1.0 + mod_ref[tile, 4:5]) + mod_ref[tile, 3:4]).astype(BF16)
    h_ref[...] = hidden
    h_away_ref[...] = dot(hidden, away_ref[...]).astype(BF16)
    h_own_ref[...] = dot(hidden, own_ref[...]).astype(BF16)
    grad = (top_ref[...].astype(F32) * mod_ref[tile, 5:6] * keep_ref[...]).astype(BF16)
    dm_ref[...] = grad
    sum_ref[0] = jnp.sum(grad.astype(F32), axis=0, keepdims=True)


def middle_call(om, w, bias, x, mod, top, keep, away, own):
    tokens, width = x.shape
    tiles = tokens // ROW
    rows = pl.BlockSpec((ROW, width), lambda i: (i, 0))
    half = pl.BlockSpec((ROW, width // 2), lambda i: (i, 0))
    fixed = pl.BlockSpec((width, width), lambda i: (0, 0))
    return call(
        middle_body,
        "middle",
        4 * tokens * width * width,
        26 * tokens * width,
        grid=(tiles,),
        in_specs=[
            pl.BlockSpec((width, ROW), lambda i: (0, i)),
            fixed,
            pl.BlockSpec((1, width), lambda i: (0, 0)),
            rows,
            pl.BlockSpec(mod.shape, lambda i: (0, 0, 0)),
            rows,
            pl.BlockSpec((ROW, 1), lambda i: (i, 0)),
            pl.BlockSpec((width, width // 2), lambda i: (0, 0)),
            pl.BlockSpec((width, width // 2), lambda i: (0, 0)),
        ],
        out_specs=[rows, rows, rows, half, half, rows, pl.BlockSpec((1, 1, width), lambda i: (i, 0, 0))],
        out_shape=[
            shaped((tokens, width), F32),
            shaped((tokens, width), F32),
            shaped((tokens, width), BF16),
            shaped((tokens, width // 2), BF16),
            shaped((tokens, width // 2), BF16),
            shaped((tokens, width), BF16),
            shaped((tiles, 1, width), F32),
        ],
    )(om, w, bias, x, mod, top, keep, away, own)


def hidden_body(h_ref, away_ref, dm_ref, w1_ref, b1_ref, w2_ref, *refs):
    g_ref, df_ref, sum_ref, send_ref = refs[-4:]
    first, second = math.sqrt(2.0 / math.pi), 0.044715
    pre = dot(h_ref[...], w1_ref[...]) + b1_ref[...]
    square = pre * pre
    tanh = jnp.tanh(first * pre * (1.0 + second * square))
    half = 0.5 * (1.0 + tanh)
    g_ref[...] = (pre * half).astype(BF16)
    slope = half + (0.5 * first) * pre * (1.0 - tanh * tanh) * (1.0 + (3.0 * second) * square)
    grad = (dot(dm_ref[...], w2_ref[...], NT) * slope).astype(BF16)
    df_ref[...] = grad
    sum_ref[...] = jnp.sum(grad.astype(F32), axis=0, keepdims=True)
    send_ref[...] = dot(away_ref[...], grad, TN)


def hidden_call(h, away, dm, w1, b1, w2, first, count, before):
    tokens, width = h.shape
    hidden = w1.shape[1]
    block = UNITS
    base = first // block
    full = pl.BlockSpec((tokens, width), lambda j: (0, 0))
    half = width // 2
    place = pl.BlockSpec(memory_space=pl.ANY)
    return call(
        hidden_body,
        "hidden",
        6 * tokens * width * count,
        6 * tokens * width + 4 * tokens * count + 8 * width * count,
        grid=(count // block,),
        in_specs=[
            full,
            pl.BlockSpec((tokens, half), lambda j: (0, 0)),
            full,
            pl.BlockSpec((width, block), lambda j: (0, base + j)),
            pl.BlockSpec((1, block), lambda j: (0, base + j)),
            pl.BlockSpec((block, width), lambda j: (base + j, 0)),
        ]
        + [place] * len(before),
        out_specs=[
            pl.BlockSpec((tokens, block), lambda j: (0, base + j)),
            pl.BlockSpec((tokens, block), lambda j: (0, base + j)),
            pl.BlockSpec((1, block), lambda j: (0, base + j)),
            pl.BlockSpec((half, block), lambda j: (0, j)),
        ],
        out_shape=[
            shaped((tokens, hidden), BF16),
            shaped((tokens, hidden), BF16),
            shaped((1, hidden), F32),
            shaped((half, count), F32),
        ],
        input_output_aliases={6 + n: n for n in range(len(before))},
    )(h, away, dm, w1, b1, w2, *before)


def shard_rows(spot_ref, g_ref, grad, made_ref):
    shards = spot_ref.shape[1]
    rows = g_ref.shape[1] // 2
    shard = g_ref.shape[1] // shards
    part = pl.program_id(0)
    for piece in range(2):
        made = dot(g_ref[:, piece * rows : (piece + 1) * rows], grad, TN)
        for number in range(shards // 2):
            made_ref[piece * (shards // 2) + number] = made[number * shard : (number + 1) * shard]

    def rows_of(place):
        return made_ref[spot_ref[part, place]]

    return rows_of


def rows_send_body(side_ref, spot_ref, g_ref, dm_ref, out_ref, made_ref):
    rows_of = shard_rows(spot_ref, g_ref, dm_ref[...], made_ref)
    for place in range(out_ref.shape[0]):
        out_ref[place] = rows_of(place)


def rows_send_call(side, spots, g, dm):
    tokens, hidden = g.shape
    width = dm.shape[1]
    half = hidden // 2
    shards = spots.shape[1]
    return call(
        rows_send_body,
        "rows_send",
        2 * tokens * half * width,
        2 * tokens * (half + width) + 4 * half * width,
        grid_spec=pltpu.PrefetchScalarGridSpec(
            num_scalar_prefetch=2,
            grid=(width // COLUMNS,),
            in_specs=[
                pl.BlockSpec((tokens, half), lambda j, side, spots: (0, side[0])),
                pl.BlockSpec((tokens, COLUMNS), lambda j, side, spots: (0, j)),
            ],
            out_specs=pl.BlockSpec((shards, half // shards, COLUMNS), lambda j, side, spots: (0, 0, j)),
            scratch_shapes=[pltpu.VMEM((shards, half // shards, COLUMNS), F32)],
        ),
        out_shape=shaped((shards, half // shards, width), F32),
    )(side, spots, g, dm)


def rows_keep_body(side_ref, spot_ref, g_ref, dm_ref, got_ref, *outs, bounds):
    *outs, made_ref = outs
    half = spot_ref.shape[1] // 2
    step = pl.program_id(0)
    rows_of = shard_rows(spot_ref, g_ref, dm_ref[...], made_ref)
    for part in range(len(bounds) - 1):

        @pl.when((step >= bounds[part]) & (step < bounds[part + 1]))
        def _():
            for place in range(half):
                outs[2 * part + 1][place] = rows_of(place) + got_ref[place]
                outs[2 * part][place] = rows_of(half + place) + got_ref[half + place]


def rows_keep_call(side, spots, g, dm, got, counts):
    tokens, hidden = g.shape
    width = dm.shape[1]
    half = hidden // 2
    steps, shards = spots.shape
    bounds = [sum(counts[:n]) for n in range(len(counts) + 1)]
    specs, shapes = [], []
    for part, count in enumerate(counts):
        for _ in range(2):
            specs.append(
                pl.BlockSpec(
                    (shards // 2, half // shards, COLUMNS),
                    functools.partial(
                        lambda j, side, spots, first, count: (0, 0, jnp.clip(j - first, 0, count - 1)),
                        first=bounds[part],
                        count=count,
                    ),
                )
            )
            shapes.append(shaped((shards // 2, half // shards, count * COLUMNS), F32))
    made = call(
        functools.partial(rows_keep_body, bounds=bounds),
        "rows_keep",
        2 * tokens * half * width,
        2 * tokens * (half + width) + 8 * half * width,
        grid_spec=pltpu.PrefetchScalarGridSpec(
            num_scalar_prefetch=2,
            grid=(steps,),
            in_specs=[
                pl.BlockSpec((tokens, half), lambda j, side, spots: (0, side[0])),
                pl.BlockSpec((tokens, COLUMNS), lambda j, side, spots: (0, j)),
                pl.BlockSpec((shards, half // shards, COLUMNS), lambda j, side, spots: (0, 0, j)),
            ],
            out_specs=specs,
            scratch_shapes=[pltpu.VMEM((shards, half // shards, COLUMNS), F32)],
        ),
        out_shape=shapes,
    )(side, spots, g, dm, got)
    made = [array.reshape(-1, array.shape[2]) for array in made]
    return list(zip(made[::2], made[1::2]))


def result_body(g_ref, w_ref, b_ref, x1_ref, mod_ref, top_ref, keep_ref, out_ref, sum_ref):
    tile = pl.program_id(0)
    branch = dot(g_ref[...], w_ref[...]) + b_ref[...]
    out_ref[...] = (x1_ref[...] + mod_ref[tile, 5:6] * keep_ref[...] * branch).astype(BF16)
    sum_ref[0] = jnp.sum(top_ref[...].astype(F32) * keep_ref[...] * branch, axis=0, keepdims=True)


def result_call(g, w, bias, x1, mod, top, keep):
    tokens, width = x1.shape
    hidden = g.shape[1]
    tiles = tokens // ROW
    rows = pl.BlockSpec((ROW, width), lambda i: (i, 0))
    return call(
        result_body,
        "result",
        2 * tokens * width * hidden,
        2 * tokens * hidden + 2 * hidden * width + 8 * tokens * width,
        grid=(tiles,),
        in_specs=[
            pl.BlockSpec((ROW, hidden), lambda i: (i, 0)),
            pl.BlockSpec((hidden, width), lambda i: (0, 0)),
            pl.BlockSpec((1, width), lambda i: (0, 0)),
            rows,
            pl.BlockSpec(mod.shape, lambda i: (0, 0, 0)),
            rows,
            pl.BlockSpec((ROW, 1), lambda i: (i, 0)),
        ],
        out_specs=[rows, pl.BlockSpec((1, 1, width), lambda i: (i, 0, 0))],
        out_shape=[shaped((tokens, width), BF16), shaped((tiles, 1, width), F32)],
    )(g, w, bias, x1, mod, top, keep)


def middle_back_body(
    df_ref, w1_ref, x1_ref, mod_ref, top_ref, a_ref, wp_ref,
    dx_ref, da_ref, do_ref, sum_ref,
):
    tile = pl.program_id(0)
    grad = dot(df_ref[...], w1_ref[...], NT)
    normal, inverse = normed(x1_ref[...])
    back = normed_back(grad * (1.0 + mod_ref[tile, 4:5]), normal, inverse)
    dx = top_ref[...].astype(F32) + back
    dx_ref[...] = dx
    da = (dx * mod_ref[tile, 2:3]).astype(BF16)
    da_ref[...] = da
    do_ref[...] = dot(wp_ref[...], da, NT).astype(BF16)
    sum_ref[0, 0:1] = jnp.sum(dx * a_ref[...], axis=0, keepdims=True)
    sum_ref[0, 1:2] = jnp.sum(grad, axis=0, keepdims=True)
    sum_ref[0, 2:3] = jnp.sum(grad * normal, axis=0, keepdims=True)
    sum_ref[0, 3:4] = jnp.sum(da.astype(F32), axis=0, keepdims=True)


def middle_back_call(df, w1, x1, mod, top, a, wp):
    tokens, width = x1.shape
    hidden = df.shape[1]
    tiles = tokens // ROW
    rows = pl.BlockSpec((ROW, width), lambda i: (i, 0))
    return call(
        middle_back_body,
        "middle_back",
        2 * tokens * width * (hidden + width),
        2 * tokens * hidden + 2 * hidden * width + 18 * tokens * width,
        grid=(tiles,),
        in_specs=[
            pl.BlockSpec((ROW, hidden), lambda i: (i, 0)),
            pl.BlockSpec((width, hidden), lambda i: (0, 0)),
            rows,
            pl.BlockSpec(mod.shape, lambda i: (0, 0, 0)),
            rows,
            rows,
            pl.BlockSpec((width, width), lambda i: (0, 0)),
        ],
        out_specs=[
            rows,
            rows,
            pl.BlockSpec((width, ROW), lambda i: (0, i)),
            pl.BlockSpec((1, 4, width), lambda i: (i, 0, 0)),
        ],
        out_shape=[
            shaped((tokens, width), F32),
            shaped((tokens, width), BF16),
            shaped((width, tokens), BF16),
            shaped((tiles, 4, width), F32),
        ],
    )(df, w1, x1, mod, top, a, wp)


class Wide:
    def __init__(self, *parts):
        self.parts = parts
        self.count = sum(rows for _, _, rows in parts)
        self.steps = 3

    def arrays(self):
        return [array for array, _, _ in self.parts]

    def specs(self, at):
        return [
            pl.BlockSpec(
                (1, rows, array.shape[2]),
                functools.partial(lambda j, at, index: (jnp.clip(j - at, 0, 2), index, 0), at=at, index=first // rows),
            )
            for array, first, rows in self.parts
        ]

    def value(self, refs):
        got = [ref[0] for ref in refs]
        return jnp.concatenate(got, axis=0) if len(got) > 1 else got[0]

    def product(self, left, right):
        return dot(left, right, TT)

    def sums(self, right):
        return dot(jnp.ones((8, right.shape[1]), BF16), right, NT)[:1]


class Plain:
    def __init__(self, array, first, count, steps):
        self.array, self.first, self.count, self.steps = array, first, count, steps

    def arrays(self):
        return [self.array]

    def specs(self, at):
        base, steps = self.first // self.count, self.steps
        index = functools.partial(
            lambda j, at, base, steps: (0, base + jnp.clip(j - at, 0, steps - 1)), at=at, base=base, steps=steps
        )
        return [pl.BlockSpec((self.array.shape[0], self.count), index)]

    def value(self, refs):
        return refs[0][...]

    def product(self, left, right):
        return dot(left, right, TN)

    def sums(self, right):
        return jnp.sum(right.astype(F32), axis=0, keepdims=True)


def columns_body(*refs, right, both):
    count = len(right.arrays())
    left_ref, right_refs, rest = refs[0], refs[1 : 1 + count], refs[1 + count :]
    value = right.value(right_refs)
    made = right.product(left_ref[...], value)
    if both:
        got_ref, send_ref, keep_ref = rest
        made = made + got_ref[...]
        rows = keep_ref.shape[0]
        send_ref[...] = made[rows:]
        keep_ref[...] = made[:rows]
    else:
        send_ref, sum_ref = rest
        send_ref[...] = made
        sum_ref[...] = right.sums(value)


def columns_call(left, right, name, got=None):
    tokens, half = left.shape
    count = right.count * right.steps
    both = got is not None
    wide = pl.BlockSpec((half, right.count), lambda j: (0, j))
    narrow = pl.BlockSpec((half // 2, right.count), lambda j: (0, j))
    made = call(
        functools.partial(columns_body, right=right, both=both),
        name,
        2 * tokens * half * count,
        2 * tokens * (count + half) + 8 * half * count,
        grid=(right.steps,),
        in_specs=[pl.BlockSpec(left.shape, lambda j: (0, 0)), *right.specs(0)] + [wide] * both,
        out_specs=[narrow, narrow] if both else [wide, pl.BlockSpec((1, right.count), lambda j: (0, j))],
        out_shape=[shaped((half // 2, count), F32)] * 2
        if both
        else [shaped((half, count), F32), shaped((1, count), F32)],
    )(left, *right.arrays(), *([got] if both else []))
    return [tuple(made)] if both else made


def pair_body(*refs, rights, both):
    counts = [len(right.arrays()) for right in rights]
    step = pl.program_id(0)
    at = 0
    rest = refs[2 + sum(counts) :]
    for number, (right, count) in enumerate(zip(rights, counts)):
        mine = (refs[at], *refs[at + 1 : at + 1 + count], *rest)
        when = step < rights[0].steps if number == 0 else step >= rights[0].steps
        pl.when(when)(functools.partial(columns_body, *mine, right=right, both=both))
        at += 1 + count


def pair_call(lefts, rights, name, got=None):
    tokens, half = lefts[0].shape
    step = rights[0].count
    steps = sum(right.steps for right in rights)
    count = step * steps
    both = got is not None
    wide = pl.BlockSpec((half, step), lambda j: (0, j))
    narrow = pl.BlockSpec((half // 2, step), lambda j: (0, j))
    operands, specs, at = [], [], 0
    for left, right in zip(lefts, rights):
        operands += [left, *right.arrays()]
        specs += [pl.BlockSpec(left.shape, lambda j: (0, 0)), *right.specs(at)]
        at += right.steps
    made = call(
        functools.partial(pair_body, rights=rights, both=both),
        name,
        2 * tokens * half * count,
        2 * tokens * (count + half) + 8 * half * count,
        grid=(steps,),
        in_specs=specs + [wide] * both,
        out_specs=[narrow, narrow] if both else [wide, pl.BlockSpec((1, step), lambda j: (0, j))],
        out_shape=[shaped((half // 2, count), F32)] * 2
        if both
        else [shaped((half, count), F32), shaped((1, count), F32)],
    )(*operands, *([got] if both else []))
    return [tuple(made)] if both else made


def moved_body(left_ref, away_ref, own_ref, left_away_ref, left_own_ref, *, dims):
    left = left_ref[...]
    left_away_ref[...] = dot(left, away_ref[...], dims).astype(BF16)
    left_own_ref[...] = dot(left, own_ref[...], dims).astype(BF16)


def moved_call(left, away, own, turned):
    width, half = away.shape
    tokens = left.shape[1] if turned else left.shape[0]
    block = tokens // 2
    fixed = pl.BlockSpec((width, half), lambda i: (0, 0))
    out = pl.BlockSpec((block, half), lambda i: (i, 0))
    side = pl.BlockSpec((width, block), lambda i: (0, i)) if turned else pl.BlockSpec((block, width), lambda i: (i, 0))
    return call(
        functools.partial(moved_body, dims=TN if turned else NN),
        "moved",
        2 * tokens * width * width,
        4 * tokens * width + 2 * width * width,
        grid=(2,),
        in_specs=[side, fixed, fixed],
        out_specs=[out] * 2,
        out_shape=[shaped((tokens, half), BF16)] * 2,
    )(left, away, own)


def first_back_body(low_ref, high_ref, w_ref, x_ref, mod_ref, dx_ref, out_ref, sum_ref):
    tile = pl.program_id(0)
    width = x_ref.shape[1]
    grad = None
    for third in range(3):
        rows = jnp.concatenate([low_ref[third], high_ref[third]], axis=0)
        part = dot(rows, w_ref[:, third * width : (third + 1) * width], TT)
        grad = part if grad is None else grad + part
    normal, inverse = normed(x_ref[...].astype(F32))
    out_ref[...] = dx_ref[...] + normed_back(grad * (1.0 + mod_ref[tile, 1:2]), normal, inverse)
    sum_ref[0, 0:1] = jnp.sum(grad, axis=0, keepdims=True)
    sum_ref[0, 1:2] = jnp.sum(grad * normal, axis=0, keepdims=True)


def first_back_call(low, high, w, x, mod, dx):
    tokens, width = x.shape
    wide = w.shape[1]
    half = pl.BlockSpec((3, width // 2, ROW), lambda i: (0, 0, i))
    tiles = tokens // ROW
    rows = pl.BlockSpec((ROW, width), lambda i: (i, 0))
    return call(
        first_back_body,
        "first_back",
        2 * tokens * width * wide,
        2 * tokens * wide + 2 * width * wide + 10 * tokens * width,
        grid=(tiles,),
        in_specs=[
            half,
            half,
            pl.BlockSpec((width, wide), lambda i: (0, 0)),
            rows,
            pl.BlockSpec(mod.shape, lambda i: (0, 0, 0)),
            rows,
        ],
        out_specs=[rows, pl.BlockSpec((1, 2, width), lambda i: (i, 0, 0))],
        out_shape=[shaped((tokens, width), F32), shaped((tiles, 2, width), F32)],
    )(low, high, w, x, mod, dx)


def payload_body(item_ref, one_ref, two_ref, gate_ref, dm_ref, df_ref, first_ref, last_ref, cond_ref, out_ref):
    tiles, _, width = one_ref.shape
    items = out_ref.shape[0]
    parts = [(one_ref, 0), (one_ref, 1), (two_ref, 0), (two_ref, 1), (two_ref, 2), (gate_ref, 0)]
    for number, (ref, row) in enumerate(parts):
        for item in range(items):
            total = jnp.zeros((1, width), F32)
            for tile in range(tiles):
                total = total + jnp.where(item_ref[tile] == item, ref[tile, row : row + 1], 0.0)
            out_ref[item : item + 1, number * width : (number + 1) * width] = total.astype(BF16).astype(F32)
    at = 6 * width
    hidden = df_ref.shape[1]
    out_ref[0:1, at : at + hidden // 2] = df_ref[:, : hidden // 2]
    out_ref[1:2, at : at + hidden // 2] = df_ref[:, hidden // 2 :]
    out_ref[2:3, at : at + width] = jnp.sum(dm_ref[:, 0], axis=0, keepdims=True)
    out_ref[2:3, at + width : at + 2 * width] = jnp.sum(two_ref[:, 3], axis=0, keepdims=True)
    rest = width - COLUMNS
    for number, third in enumerate((0, 2)):
        spot = at + number * width
        out_ref[3:4, spot : spot + COLUMNS] = first_ref[:, width + third * COLUMNS : width + (third + 1) * COLUMNS]
        out_ref[3:4, spot + COLUMNS : spot + width] = last_ref[:, third * rest : (third + 1) * rest]
    out_ref[:, at + 2 * width :] = cond_ref[...]


def payload_call(tile_item, *sums):
    items, width = sums[-1].shape
    out = shaped((items, 9 * width), F32)
    return call(
        payload_body,
        "payload",
        0,
        0,
        grid=(1,),
        in_specs=[pl.BlockSpec(memory_space=pltpu.SMEM)]
        + [pl.BlockSpec(part.shape, functools.partial(lambda j, rank: (0,) * rank, rank=part.ndim)) for part in sums],
        out_specs=pl.BlockSpec(out.shape, lambda j: (0, 0)),
        out_shape=out,
    )(tile_item, *sums)


def chosen_sums(select, values, dims):
    high = values.astype(BF16)
    rest = values - high.astype(F32)
    middle = rest.astype(BF16)
    low = (rest - middle.astype(F32)).astype(BF16)
    return dot(select, high, dims) + (dot(select, middle, dims) + dot(select, low, dims))


def modulation_back_body(me_ref, *refs, count):
    part_refs, cond_refs, sum_refs = refs[:count], refs[count : 2 * count], refs[2 * count : 3 * count]
    label_ref, w_ref, grad_ref, bias_ref, table_ref, own_sums_ref, act_ref, own_ref, total_ref = refs[3 * count :]
    step = pl.program_id(0)
    width = act_ref.shape[1]
    shard = grad_ref.shape[0]
    items = own_sums_ref.shape[0]

    @pl.when(step == 0)
    def _():
        at = 0
        for cond_ref in cond_refs:
            cond = cond_ref[...]
            act_ref[at : at + cond.shape[0]] = (cond / (1.0 + jnp.exp(-cond))).astype(BF16)
            at += cond.shape[0]
        row = lax.broadcasted_iota(jnp.int32, (width, 128), 0)
        column = lax.broadcasted_iota(jnp.int32, (width, 128), 1)
        picked = jnp.where((column < shard) & (row == me_ref[0] * shard + column), 1.0, 0.0).astype(BF16)
        own_ref[...] = dot(act_ref[...], picked).astype(BF16)
        total_ref[...] = jnp.zeros_like(total_ref)
        sums = None
        for sum_ref in sum_refs:
            rows = sum_ref.shape[0]
            item = lax.broadcasted_iota(jnp.int32, (items, rows), 0)
            source = lax.broadcasted_iota(jnp.int32, (items, rows), 1)
            select = (lax.rem(source, jnp.full_like(source, items)) == item).astype(F32)
            part = chosen_sums(select.astype(BF16), sum_ref[...], NN)
            sums = part if sums is None else sums + part
        own_sums_ref[...] = sums

    mod = jnp.concatenate([part_ref[...] for part_ref in part_refs], axis=0)
    bias_ref[...] = jnp.sum(mod, axis=0, keepdims=True)
    mod = mod.astype(BF16)
    grad_ref[...] = dot(own_ref[...], mod, TN)[:shard]
    total_ref[...] += dot(w_ref[...], mod, NT)

    @pl.when(step == pl.num_programs(0) - 1)
    def _():
        cond = jnp.concatenate([cond_ref[...] for cond_ref in cond_refs], axis=0)
        gate = 1.0 / (1.0 + jnp.exp(-cond))
        grad = total_ref[...].T * (gate * (1.0 + cond * (1.0 - gate)))
        classes = table_ref.shape[0]
        select = (label_ref[...] == lax.broadcasted_iota(jnp.int32, (grad.shape[0], classes), 1)).astype(F32).astype(BF16)
        table_ref[...] = chosen_sums(select, grad, TN)


def modulation_back_call(me, parts, used, w, classes, shard, items):
    width, wide = w.shape
    block = 2 * width
    rows = sum(part.shape[0] for part in parts)
    extra = parts[0].shape[1] - wide - width
    at = (wide + extra) // width
    return call(
        functools.partial(modulation_back_body, count=len(parts)),
        "modulation_back",
        4 * rows * width * wide,
        2 * width * wide,
        grid=(wide // block,),
        in_specs=[
            pl.BlockSpec(memory_space=pltpu.SMEM),
            *[pl.BlockSpec((part.shape[0], block), lambda j: (0, j)) for part in parts],
            *[pl.BlockSpec((part.shape[0], width), lambda j: (0, at)) for part in parts],
            *[pl.BlockSpec((part.shape[0], extra), lambda j: (0, wide // extra)) for part in parts],
            pl.BlockSpec(used.shape, lambda j: (0, 0)),
            pl.BlockSpec((width, block), lambda j: (0, j)),
        ],
        out_specs=[
            pl.BlockSpec((shard, block), lambda j: (0, j)),
            pl.BlockSpec((1, block), lambda j: (0, j)),
            pl.BlockSpec((classes, width), lambda j: (0, 0)),
            pl.BlockSpec((items, extra), lambda j: (0, 0)),
        ],
        out_shape=[
            shaped((shard, wide), F32),
            shaped((1, wide), F32),
            shaped((classes, width), F32),
            shaped((items, extra), F32),
        ],
        scratch_shapes=[
            pltpu.VMEM((rows, width), BF16),
            pltpu.VMEM((rows, 128), BF16),
            pltpu.VMEM((width, rows), F32),
        ],
    )(me, *parts, *parts, *parts, used, w)


def add_body(*refs, plans):
    outs = refs[-len(plans) :]
    at = 0
    for out_ref, (count, first, rows) in zip(outs, plans):
        value = refs[at][first : first + rows]
        for term in range(1, count):
            value = value + refs[at + term][first : first + rows]
        out_ref[...] = value
        at += count


def add_call(jobs):
    steps = 1
    operands, specs, outs, shapes, plans = [], [], [], [], []
    moved = 0
    for terms, first, rows in jobs:
        wide = terms[0].shape[1]
        block = wide // steps
        for term in terms:
            size, index, at = rows, first // rows, 0
            while size % 8 and size < term.shape[0]:
                size, index, at = size * 2, 0, first
            operands.append(term)
            specs.append(pl.BlockSpec((size, block), functools.partial(lambda j, index: (index, j), index=index)))
        plans.append((len(terms), at, rows))
        outs.append(pl.BlockSpec((rows, block), lambda j: (0, j)))
        shapes.append(shaped((rows, wide), F32))
        moved += 4 * rows * wide * (len(terms) + 1)
    return call(
        functools.partial(add_body, plans=plans),
        "add",
        moved // 4,
        moved,
        grid=(steps,),
        in_specs=specs,
        out_specs=outs,
        out_shape=shapes,
    )(*operands)


def assemble_body(*refs, plans):
    outs = refs[-len(plans) :]
    for out_ref, (rows, blocks) in zip(outs, plans):
        for terms, source, target, count in blocks:
            value = refs[terms[0]][:rows, source : source + count]
            for term in terms[1:]:
                value = value + refs[term][:rows, source : source + count]
            out_ref[:, target : target + count] = value


def assemble_call(outputs):
    operands, specs, known, plans, shapes = [], [], {}, [], []
    for blocks in outputs:
        rows, target, made = blocks[0][0].rows, 0, []
        for chunk, source, count in blocks:
            if id(chunk) not in known:
                known[id(chunk)] = []
                for term in chunk.terms:
                    size = rows
                    while size % 8 and size < term.shape[0]:
                        size *= 2
                    known[id(chunk)].append(len(operands))
                    operands.append(term)
                    specs.append(pl.BlockSpec((size, term.shape[1]), lambda j: (0, 0)))
            made.append((known[id(chunk)], source, target, count))
            target += count
        plans.append((rows, made))
        shapes.append(shaped((rows, target), F32))
    return call(
        functools.partial(assemble_body, plans=plans),
        "assemble",
        0,
        sum(8 * 4 * shape.shape[0] * shape.shape[1] for shape in shapes),
        grid=(1,),
        in_specs=specs,
        out_specs=[pl.BlockSpec(shape.shape, lambda j: (0, 0)) for shape in shapes],
        out_shape=shapes,
    )(*operands)


def bit_order(bits, core, lead):
    order = list(range(bits))
    if bits >= 2 and core:
        order[:2] = [1, 0]
    if lead and lead < bits:
        order.remove(lead)
        order.insert(0, lead)
    return order


class Chunk:
    def __init__(self, send, kept, wait, lead):
        self.send, self.terms, self.wait, self.lead = send, [kept], wait, lead
        self.rows = kept.shape[0]
        self.stage = 0


class Spread:
    def __init__(self, rows):
        self.own, self.other = [rows], None
        self.stage = 0


class Flow:
    def __init__(self, bits):
        self.bits = bits
        self.fresh, self.crossing, self.chunks, self.last = [], [], [], []
        self.blocks = ([], [], [])
        self.spreads = []

    def emit(self, send, keep, store, waits=(0,), leads=(0,)):
        self.fresh.append((send, keep, store, waits, leads))

    def spread(self, rows):
        self.spreads.append(Spread(rows))
        return self.spreads[-1]

    def busy(self):
        moving = self.fresh or self.crossing or any(chunk.stage < self.bits for chunk in self.chunks)
        return moving or any(spread.stage <= self.bits for spread in self.spreads)

    def pairs(self, stage, lead):
        size = 1 << self.bits
        flips = [1 << bit_order(self.bits, core, lead)[stage] for core in range(2)]
        return [(core * size + i, core * size + (i ^ flips[core])) for core in range(2) for i in range(size)]

    def received(self, live):
        live, (cores, blocks, doubles) = lax.optimization_barrier((live, self.blocks))
        for spread, block in zip([spread for spread in self.spreads if spread.other is None and spread.stage], doubles):
            if spread.stage > self.bits:
                spread.other = block
            elif spread.stage == self.bits:
                spread.own += block
            else:
                spread.own = [jnp.concatenate(spread.own + block, axis=0)]
        jobs, waiting = [], []
        for chunk, block in zip(self.last, blocks):
            chunk.terms.append(block)
            if chunk.stage < self.bits:
                chunk.rows //= 2
                jobs.append((chunk.terms, chunk.rows, chunk.rows))
                waiting.append(chunk)
        for (_, keep, store, waits, leads), core in zip(self.crossing, cores):
            new = [Chunk(*pair, wait, lead) for pair, wait, lead in zip(keep(core), waits, leads)]
            store += new
            self.chunks += new
        for chunk, value in zip(waiting, add_call(jobs) if jobs else []):
            chunk.send = value
        return live

    def round(self, live):
        live = self.received(live)
        moving = [chunk for chunk in self.chunks if chunk.stage < self.bits and not chunk.wait]
        for chunk in self.chunks:
            chunk.wait = max(0, chunk.wait - 1)
        crossing, self.fresh = self.fresh, []
        doubling = [spread for spread in self.spreads if spread.stage <= self.bits]
        live, cores, sends, doubles = lax.optimization_barrier(
            (
                live,
                [entry[0] for entry in crossing],
                [chunk.send for chunk in moving],
                [spread.own for spread in doubling],
            )
        )
        blocks = []
        for chunk, send in zip(moving, sends):
            blocks.append(lax.ppermute(send, ("stream", "batch"), self.pairs(chunk.stage, chunk.lead)))
            chunk.stage += 1
        cores = [lax.ppermute(send, "stream", [(0, 1), (1, 0)]) for send in cores]
        for number, (spread, rows) in enumerate(zip(doubling, doubles)):
            spread.own = rows
            if spread.stage < self.bits:
                pairs = self.pairs(self.bits - 1 - spread.stage, 0)
                doubles[number] = [lax.ppermute(piece, ("stream", "batch"), pairs) for piece in rows]
            else:
                doubles[number] = [lax.ppermute(piece, "stream", [(0, 1), (1, 0)]) for piece in rows]
            spread.stage += 1
        self.crossing, self.last, self.blocks = crossing, moving, (cores, blocks, doubles)
        return live


def offsets_of(bits, side, lead):
    places = jnp.arange(1 << bits, dtype=jnp.int32)
    made = []
    for core in range(2):
        offset = jnp.zeros_like(places)
        for stage, bit in enumerate(bit_order(bits, core, lead)):
            offset = offset | (((places >> (bits - 1 - stage)) & 1) << bit)
        made.append(offset)
    return jnp.where(side == 0, made[0], made[1])


def places_of(bits, side, lead, offset):
    made = []
    for core in range(2):
        place = jnp.zeros_like(offset)
        for stage, bit in enumerate(bit_order(bits, core, lead)):
            place = place | (((offset >> bit) & 1) << (bits - 1 - stage))
        made.append(place)
    return jnp.where(side == 0, made[0], made[1])


def time_embed(steps_in, width):
    half_width = width // 2
    frequency = jnp.exp(-math.log(10000.0) * jnp.arange(half_width, dtype=F32) / half_width)
    angles = steps_in.astype(F32)[:, None] * frequency[None, :]
    return jnp.concatenate([jnp.cos(angles), jnp.sin(angles)], axis=1)


def per_device(
    tokens, segments, timesteps, labels, head_keep, token_keep, class_table, w_ada, b_ada,
    w_qkv, b_qv, w_proj, b_proj, w_fc1, b_fc1, w_fc2, b_fc2, out_grad, *, batch,
):
    x, top = tokens[0], out_grad[0]
    count, width = x.shape
    hidden = w_fc1.shape[1]
    heads = head_keep.shape[1]
    items = timesteps.shape[0]
    tiles = count // ROW
    groups = count // GROUP
    null_class = class_table.shape[0] - 1
    bits = batch.bit_length() - 1
    devices = 2 * batch
    stream = lax.axis_index("stream")
    index = lax.axis_index("batch")

    own_labels = lax.dynamic_slice_in_dim(labels, index * items, items)
    used = jnp.where(stream == 0, own_labels, null_class)
    cond = time_embed(timesteps, width) + jnp.take(class_table, used, axis=0).astype(F32)
    act = jax.nn.silu(cond).astype(BF16)
    modulation = dot(act, w_ada) + b_ada
    tile_item = segments[::ROW] - index * items
    chosen = tile_item[:, None] == jnp.arange(items, dtype=jnp.int32)[None, :]
    mod = jnp.sum(jnp.where(chosen[:, :, None], modulation[None], 0.0), axis=1)
    mod = mod.reshape(tiles, 6, width)
    tile_heads = jnp.sum(jnp.where(chosen[:, :, None], head_keep[None], 0), axis=1).astype(F32)
    head_columns = jnp.repeat(tile_heads.T, ROW, axis=1).reshape(heads, 1, count)
    keep = token_keep[0].astype(F32)[:, None]
    grouped = segments.reshape(groups, GROUP)
    flag = (grouped[:, 0] == grouped[:, -1]).astype(jnp.int32)

    shard = width // devices

    def picked(side):
        order = side * batch + (index ^ offsets_of(bits, side, 0))
        source = (order[:, None] * shard + jnp.arange(shard, dtype=jnp.int32)[None, :]).reshape(width // 2)
        return (jnp.arange(width, dtype=jnp.int32)[:, None] == source[None, :]).astype(BF16)

    def spots(side):
        return jnp.stack([index ^ offsets_of(bits, side, lead) for steps, lead in ROW_PARTS for _ in range(steps)])

    other = 1 - stream
    away, own = picked(other), picked(stream)

    bias_full = jnp.concatenate([b_qv[:width], jnp.zeros((width,), F32), b_qv[width:]])[None]
    h1, qkv = qkv_call(x, mod, w_qkv, bias_full)
    probs, mixed, om = attention_call(flag, qkv, head_columns, heads)
    a, x1, h2, h2_away, h2_own, dm, sum_dm = middle_call(om, w_proj, b_proj[None], x, mod, top, keep, away, own)

    flow = Flow(bits)
    fc1, fc2, wide = [], [], []

    filled, latest = (), {}
    for low, high in ((0, 2 * UNITS), (2 * UNITS, 5 * UNITS), (5 * UNITS, hidden)):
        *filled, send = hidden_call(h2, h2_away, dm, w_fc1, b_fc1[None], w_fc2, low, high - low, filled)
        latest["df"] = filled[1]

        def hidden_keep(got, low=low, count=high - low):
            return columns_call(h2_own, Plain(latest["df"], low, UNITS, count // UNITS), "hidden_keep", got)

        flow.emit(send, hidden_keep, fc1)
        h2, filled = flow.round((h2, filled))
        latest["df"] = filled[1]
    g, df, sum_df = filled

    rows_send = rows_send_call(other[None], spots(other), g, dm)
    flow.emit(
        rows_send.reshape(-1, width),
        lambda got: rows_keep_call(
            stream[None], spots(stream), g, dm, got.reshape(rows_send.shape), [steps for steps, _ in ROW_PARTS]
        ),
        fc2,
        [0] * len(ROW_PARTS),
        [lead for _, lead in ROW_PARTS],
    )
    om_away, om_own = moved_call(om, away, own, True)
    df, x1, om_away, om_own, h1 = flow.round((df, x1, om_away, om_own, h1))
    h1_away, h1_own = moved_call(h1, away, own, False)
    dx1, da, do, sums_two = middle_back_call(df, w_fc1, x1, mod, top, a, w_proj)

    me = stream * batch + index

    def used_labels(side):
        order = bit_order(bits, 0, 0)[::-1], bit_order(bits, 1, 0)[::-1]
        places = jnp.arange(batch, dtype=jnp.int32)
        offsets = [sum(((places >> n) & 1) << bit for n, bit in enumerate(bits_of)) for bits_of in order]
        from_device = index ^ jnp.where(side == 0, offsets[0], offsets[1])
        return jnp.where(side == 0, jnp.take(labels.reshape(batch, items), from_device, axis=0).reshape(-1), null_class)

    used_rows = jnp.concatenate([used_labels(stream), used_labels(other)])[:, None]
    dx1, da, do, sums_two, g, h1_away, h1_own = flow.round((dx1, da, do, sums_two, g, h1_away, h1_own))
    half = width // 2
    low = attention_back_call(flag, qkv, do, head_columns, probs, mixed, 0)
    rights = [Plain(da, 0, COLUMNS, width // COLUMNS), Wide((low, 0, COLUMNS))]
    send, first_sums = pair_call([om_away, h1_away], rights, "first_send")
    flow.emit(send, lambda got: pair_call([om_own, h1_own], rights, "first_keep", got), wide)
    result, sum_gate = result_call(g, w_fc2, b_fc2[None], x1, mod, top, keep)
    low, first_sums, result, sum_gate = flow.round((low, first_sums, result, sum_gate))
    high = attention_back_call(flag, qkv, do, head_columns, probs, mixed, 1)
    rest = Wide((low, COLUMNS, half - COLUMNS), (high, 0, half))
    send, high_sums = columns_call(h1_away, rest, "last_send")
    flow.emit(send, lambda got: columns_call(h1_own, rest, "last_keep", got), wide)
    low, high, dx1, high_sums = flow.round((low, high, dx1, high_sums))
    grad_tokens, sums_one = first_back_call(low, high, w_qkv, x, mod, dx1)

    spread = flow.spread(
        payload_call(tile_item, sums_one, sums_two, sum_gate, sum_dm, sum_df, first_sums, high_sums, cond)
    )
    while any(chunk.stage < bits for chunk in fc1 + fc2):
        result = flow.round(result)
    result = flow.round(result)
    grad_w_fc1, grad_w_fc2 = assemble_call(
        [[(chunk, 0, chunk.terms[0].shape[1]) for chunk in store] for store in (fc1, fc2)]
    )
    result, grad_w_fc1, grad_w_fc2, used_rows = flow.round((result, grad_w_fc1, grad_w_fc2, used_rows))
    while any(chunk.stage < bits for chunk in wide):
        result = flow.round(result)
    result = flow.round(result)
    first, last = wide
    each = COLUMNS, width - COLUMNS
    blocks = [
        block
        for third in range(3)
        for block in ((first, width + third * each[0], each[0]), (last, third * each[1], each[1]))
    ]
    grad_w_proj, grad_w_qkv = assemble_call([[(first, 0, width)], blocks])
    while flow.busy():
        result = flow.round(result)
    result, grad_w_proj = flow.received((result, grad_w_proj))
    grad_w_ada, mod_sums, grad_table, own_sums = modulation_back_call(
        me[None], spread.own + spread.other, used_rows, w_ada, null_class + 1, shard, items
    )
    share = 6 * width // devices
    grad_b_ada = lax.dynamic_slice_in_dim(mod_sums[0], me * share, share)
    def own_sums_of(row, first, count):
        return lax.dynamic_slice(own_sums, (row, first), (1, count))[0]

    each = hidden // devices
    grad_b_fc1 = own_sums_of(me // (devices // 2), me % (devices // 2) * each, each)
    grad_b_fc2 = own_sums_of(2, me * shard, shard)
    grad_b_proj = own_sums_of(2, width + me * shard, shard)
    grad_b_qv = own_sums_of(3, me * 2 * shard, 2 * shard)

    return (
        result[None],
        grad_tokens[None],
        grad_table,
        grad_w_ada,
        grad_b_ada,
        grad_w_qkv,
        grad_b_qv,
        grad_w_proj,
        grad_b_proj,
        grad_w_fc1,
        grad_b_fc1,
        grad_w_fc2,
        grad_b_fc2,
    )


def solution(mesh):
    both = ("stream", "batch")
    return jax.shard_map(
        functools.partial(per_device, batch=mesh.shape["batch"]),
        mesh=mesh,
        in_specs=(
            P("stream", "batch", None),
            P("batch"),
            P("batch"),
            P(),
            P("batch", None),
            P("stream", "batch"),
            P(), P(), P(), P(), P(), P(), P(), P(), P(), P(), P(),
            P("stream", "batch", None),
        ),
        out_specs=(
            P("stream", "batch", None),
            P("stream", "batch", None),
            P(),
            P(both, None),
            P(both),
            P(both, None),
            P(both),
            P(both, None),
            P(both),
            P(both, None),
            P(both),
            P(both, None),
            P(both),
        ),
        check_vma=False,
    )
```
